32 devices in a mesh: section: 16 (over z, x, core), dp: 2 (over y).
Axes of the slice: x: 2, y: 2, z: 4, core: 2. Of those that a mesh axis runs over, the one named last changes fastest.
Arguments:
- token_ids: int32 [2, 16, 2, 128], P('dp', 'section'), may hold values from 0 to 32127
- targets: int32 [2, 16, 128], P('dp', 'section'), may hold values from 0 to 32127
- objective: int32 [2, 16], P('dp', 'section'), may hold values from 0 to 1
- buckets: int32 [2, 255], replicated, may hold values from 0 to 31, as said below
- table: float32 [32128, 768], P('section')
- table_first: float32 [32128, 768], P('section'), may hold values from -0.00024414062 to 0.00024414062
- table_second: float32 [32128, 768], P('section'), may hold values from 1.2867396e-09 to 5.098402e-09
- inner_weight: float32 [2, 768, 3072], P(None, None, 'section'), may hold values from -0.21875 to 0.21875
- inner_first: float32 [2, 768, 3072], P(None, None, 'section'), may hold values from -0.00024414062 to 0.00024414062
- inner_second: float32 [2, 768, 3072], P(None, None, 'section'), may hold values from 1.2867396e-09 to 5.098402e-09
- outer_weight: float32 [2, 3072, 768], P(None, 'section'), may hold values from -0.109375 to 0.109375
- outer_first: float32 [2, 3072, 768], P(None, 'section'), may hold values from -0.00024414062 to 0.00024414062
- outer_second: float32 [2, 3072, 768], P(None, 'section'), may hold values from 1.2867396e-09 to 5.098402e-09
- gain_rows: float32 [7, 768], replicated, may hold values from 0.5 to 1.5
- gain_first: float32 [7, 768], replicated, may hold values from -0.0024414062 to 0.0024414062
- gain_second: float32 [7, 768], replicated, may hold values from 1.2867396e-07 to 5.098402e-07
- position_bias: float32 [2, 32, 12], replicated, may hold values from -4 to 4
- bias_first: float32 [2, 32, 12], replicated, may hold values from -0.0024414062 to 0.0024414062
- bias_second: float32 [2, 32, 12], replicated, may hold values from 1.2867396e-07 to 5.098402e-07
- attention: float32 [12, 768, 768], P(None, 'section'), may hold values from -0.21875 to 0.21875
- left_stats: float32 [12, 768, 768], P(None, 'section'), as said below
- right_stats: float32 [12, 768, 768], P(None, 'section'), as said below
- left_roots: bfloat16 [12, 768, 768], P(None, 'section'), as said below
- right_inverse_roots: bfloat16 [12, 768, 768], P(None, 'section'), as said below
Outputs:
- loss_sum: float32 [], replicated
- loss_count: float32 [], replicated
- grad_norm: float32 [], replicated
- table_moment: float32 [32128, 768], P('section')
- table_square: float32 [32128, 768], P('section')
- table_new: float32 [32128, 768], P('section')
- inner_moment: float32 [2, 768, 3072], P(None, None, 'section')
- inner_second_moment: float32 [2, 768, 3072], P(None, None, 'section')
- inner_new: float32 [2, 768, 3072], P(None, None, 'section')
- outer_moment: float32 [2, 3072, 768], P(None, 'section')
- outer_second_moment: float32 [2, 3072, 768], P(None, 'section')
- outer_new: float32 [2, 3072, 768], P(None, 'section')
- gain_moment: float32 [7, 768], replicated
- gain_square: float32 [7, 768], replicated
- gain_new: float32 [7, 768], replicated
- bias_moment: float32 [2, 32, 12], replicated
- bias_square: float32 [2, 32, 12], replicated
- updated_position_bias: float32 [2, 32, 12], replicated
- attention_grad: float32 [12, 768, 768], P(None, 'section')
- left_new: float32 [12, 768, 768], P(None, 'section')
- right_new: float32 [12, 768, 768], P(None, 'section')
- attention_new: float32 [12, 768, 768], P(None, 'section')
The draws below stay inside these ranges and needn't reach their ends.
Inputs may be any that keep to these rules, and one draw needn't show every extreme that they name: `buckets`: on each side of offset 0 the bucket does not fall as the offset's magnitude grows; offsets before the query use 0 to 15, offsets after it the upper half. `left_stats`: Symmetric, dominated by a positive diagonal. `right_stats`: Symmetric, dominated by a positive diagonal. `left_roots`: Symmetric. `right_inverse_roots`: Symmetric.
All inputs are finite; a program needn't handle non-finite values.
Results may differ from the reference program's by a relative error of at most 0.0078.
Values may be sent and summed in bfloat16 or wider, within the bound.
No kernel may reach another device: no remote copies, remote signals or barrier semaphores. Data moves between devices by JAX's collectives and lax.ppermute only.
A program may use at most 640 MiB of HBM per device.

```python
import math
import jax
import jax.numpy as jnp
import numpy as np
from jax import lax

D = 768
FF = 3072
HEADS = 12
DK = 64
BUCKETS = 32
VOCAB = 32128
LEN = 128
MICRO = 2
STEP = 5
SPAN = 28
SECTIONS = 16
REPLICAS = 2


def draw_buckets(key, part):
    key = jax.random.fold_in(key, 11)
    half_range = BUCKETS // 2
    exact_range = max(1, BUCKETS // 4)
    magnitude = jnp.arange(LEN)
    steps_drawn = jax.random.randint(key, (2, LEN), 0, 2)
    steps_drawn = jnp.where(magnitude[None, :] <= exact_range, 1, steps_drawn)
    steps_drawn = jnp.where(magnitude[None, :] == 0, 0, steps_drawn)
    level = jnp.minimum(jnp.cumsum(steps_drawn, 1), half_range - 1)
    level = jnp.where(magnitude[None, :] == LEN - 1, half_range - 1, level)
    offsets = jnp.arange(2 * LEN - 1) - (LEN - 1)
    distance = jnp.broadcast_to(jnp.abs(offsets)[None, :], (2, 2 * LEN - 1))
    picked = jnp.take_along_axis(level, distance, 1)
    return (picked + jnp.where(offsets > 0, half_range, 0)[None, :]).astype(jnp.int32)


def draw_table(key, part):
    key = jax.random.fold_in(key, 12)
    rising = jnp.arange(VOCAB, dtype=jnp.float32)[:, None] / VOCAB
    values = jax.random.normal(key, (VOCAB, D), jnp.float32)
    return values * (1.0 + 2.0 * rising)


def symmetric_matrix(key, noise_level):
    first_key, second_key = jax.random.split(key)
    diagonal = jnp.exp(jax.random.uniform(first_key, (12, D), jnp.float32, 0.0, math.log(4.0)))
    noise = jax.random.normal(second_key, (12, D, D), jnp.float32)
    noise = (noise + jnp.swapaxes(noise, 1, 2)) * (noise_level / math.sqrt(D))
    return noise + diagonal[:, :, None] * jnp.eye(D, dtype=jnp.float32)[None]


def draw_left_stats(key, part):
    key = jax.random.fold_in(key, 13)
    return symmetric_matrix(key, 0.1) * (0.053 * D / (VOCAB * D + 4 * D * FF + 12 * D * D))


def draw_right_stats(key, part):
    key = jax.random.fold_in(key, 14)
    return symmetric_matrix(key, 0.1) * (0.053 * D / (VOCAB * D + 4 * D * FF + 12 * D * D))


def draw_left_roots(key, part):
    key = jax.random.fold_in(key, 15)
    ramp = jnp.arange(D, dtype=jnp.float32) / D
    scaling = jnp.sqrt(1.0 + 2.0 * ramp)
    matrix = symmetric_matrix(key, 0.7) * scaling[None, :, None] * scaling[None, None, :]
    return matrix.astype(jnp.bfloat16)


def draw_right_inverse_roots(key, part):
    key = jax.random.fold_in(key, 16)
    return symmetric_matrix(key, 0.7).astype(jnp.bfloat16)


def set_ends(array, own_key, low, high):
    longest = array.shape.index(max(array.shape))
    spots = []
    for shift in (0, 1):
        where = [jax.random.randint(jax.random.fold_in(own_key, axis), (), 0, length) for axis, length in enumerate(array.shape)]
        where[longest] = (where[longest] + shift) % array.shape[longest]
        spots.append(tuple(where))
    return array.at[spots[0]].set(low).at[spots[1]].set(high)


def shard_levels(stream_key, extent, pieces, low, high):
    level, own = 1.0, jax.random.fold_in(stream_key, 6)
    for position, parts in pieces:
        heights = jnp.exp(jax.random.uniform(jax.random.fold_in(own, position), (parts,), jnp.float32, low / len(pieces), high / len(pieces)))
        level = level * jnp.repeat(heights, extent[position] // parts).reshape([-1 if axis == position else 1 for axis in range(len(extent))])
    return level


def cumulative_ranks(amount, lean):
    portions = [(1 << 20) // math.isqrt(rank ** lean) + 1 for rank in range(1, amount + 1)]
    width = 1 + sum(portions) // (1 << 30)
    return np.cumsum(np.array([max(1, weight // width) for weight in portions]))


def skewed_ids(own_key, shape, count, lean):
    table = cumulative_ranks(count, lean)
    pick = jax.random.randint(jax.random.fold_in(own_key, 1), shape, 0, int(table[count - 1]))
    grade = jnp.searchsorted(jnp.asarray(table, jnp.int32), pick, side="right")
    return jax.random.permutation(jax.random.fold_in(own_key, 2), count)[grade].astype(jnp.int32)


def scatter_about(own_key, dims, width, most, cuts=(), held_as=jnp.bfloat16):
    array = jax.random.normal(own_key, dims, jnp.float32) * width
    if len(cuts) > 0:
        array = shard_levels(own_key, dims, cuts, -0.22, 0.18) * array
    return jnp.clip(array, min=-most, max=most).astype(held_as)


def setup_inputs(seed: int = 0) -> dict:
    keys = jax.random.split(jax.random.key(seed), 25)
    token_ids = set_ends(skewed_ids(keys[0], (REPLICAS, SECTIONS, MICRO, LEN), VOCAB, 2), jax.random.fold_in(keys[0], 3), 0, VOCAB - 1).astype(jnp.int32)
    targets = set_ends(skewed_ids(keys[1], (REPLICAS, SECTIONS, LEN), VOCAB, 2), jax.random.fold_in(keys[1], 3), 0, VOCAB - 1).astype(jnp.int32)
    objective = set_ends(jax.random.randint(keys[2], (REPLICAS, SECTIONS), 0, 2), jax.random.fold_in(keys[2], 1), 0, 1).astype(jnp.int32)
    buckets = draw_buckets(jax.random.fold_in(keys[24], 71), 0)
    table = draw_table(jax.random.fold_in(keys[24], 71), 0)
    table_first = scatter_about(keys[5], (VOCAB, D), (0.11 * (VOCAB * D + 4 * D * FF + 12 * D * D) ** -0.5), 0.00024414062, ((0, 16),), jnp.float32)
    table_second = jnp.clip(jnp.exp(math.log(5.098402144909642e-09) - 1.3768156 * jax.random.uniform(keys[6], (VOCAB, D), jnp.float32) ** shard_levels(keys[6], (VOCAB, D), ((0, 16),), -0.2, 0.2)), 1.2867396037563594e-09, 5.098402144909642e-09)
    inner_weight = scatter_about(keys[7], (2, D, FF), D ** -0.5, 0.21875, ((2, 16),), jnp.float32)
    inner_first = scatter_about(keys[8], (2, D, FF), (0.11 * (VOCAB * D + 4 * D * FF + 12 * D * D) ** -0.5), 0.00024414062, ((2, 16),), jnp.float32)
    inner_second = jnp.clip(jnp.exp(math.log(5.098402144909642e-09) - 1.3768156 * jax.random.uniform(keys[9], (2, D, FF), jnp.float32) ** shard_levels(keys[9], (2, D, FF), ((2, 16),), -0.2, 0.2)), 1.2867396037563594e-09, 5.098402144909642e-09)
    outer_weight = scatter_about(keys[10], (2, FF, D), FF ** -0.5, 0.109375, ((1, 16),), jnp.float32)
    outer_first = scatter_about(keys[11], (2, FF, D), (0.11 * (VOCAB * D + 4 * D * FF + 12 * D * D) ** -0.5), 0.00024414062, ((1, 16),), jnp.float32)
    outer_second = jnp.clip(jnp.exp(math.log(5.098402144909642e-09) - 1.3768156 * jax.random.uniform(keys[12], (2, FF, D), jnp.float32) ** shard_levels(keys[12], (2, FF, D), ((1, 16),), -0.2, 0.2)), 1.2867396037563594e-09, 5.098402144909642e-09)
    gain_rows = jnp.clip(1.0 + 0.1 * jax.random.normal(keys[13], (7, D), jnp.float32), 0.5, 1.5)
    gain_first = scatter_about(keys[14], (7, D), (1.1 * (VOCAB * D + 4 * D * FF + 12 * D * D) ** -0.5), 0.0024414062, (), jnp.float32)
    gain_second = jnp.clip(jnp.exp(jax.random.uniform(keys[15], (7, D), jnp.float32, math.log(1.2867396037563594e-07), math.log(5.098402198200347e-07))), 1.2867396037563594e-07, 5.098402198200347e-07)
    position_bias = scatter_about(keys[16], (2, BUCKETS, HEADS), 1.0, 4.0, (), jnp.float32)
    bias_first = scatter_about(keys[17], (2, BUCKETS, HEADS), (1.1 * (VOCAB * D + 4 * D * FF + 12 * D * D) ** -0.5), 0.0024414062, (), jnp.float32)
    bias_second = jnp.clip(jnp.exp(jax.random.uniform(keys[18], (2, BUCKETS, HEADS), jnp.float32, math.log(1.2867396037563594e-07), math.log(5.098402198200347e-07))), 1.2867396037563594e-07, 5.098402198200347e-07)
    attention = scatter_about(keys[19], (12, D, D), D ** -0.5, 0.21875, ((1, 16),), jnp.float32)
    left_stats = draw_left_stats(jax.random.fold_in(keys[24], 71), 0)
    right_stats = draw_right_stats(jax.random.fold_in(keys[24], 71), 0)
    left_roots = draw_left_roots(jax.random.fold_in(keys[24], 71), 0)
    right_inverse_roots = draw_right_inverse_roots(jax.random.fold_in(keys[24], 71), 0)
    return dict(token_ids=token_ids, targets=targets, objective=objective, buckets=buckets, table=table, table_first=table_first, table_second=table_second, inner_weight=inner_weight, inner_first=inner_first, inner_second=inner_second, outer_weight=outer_weight, outer_first=outer_first, outer_second=outer_second, gain_rows=gain_rows, gain_first=gain_first, gain_second=gain_second, position_bias=position_bias, bias_first=bias_first, bias_second=bias_second, attention=attention, left_stats=left_stats, right_stats=right_stats, left_roots=left_roots, right_inverse_roots=right_inverse_roots)


EPS = 1e-06
CLIP = 1.0
BETA_ONE = 0.9
BETA_TWO = 0.95
BETA_STATS = 0.95
ADAM_EPS = 1e-08
DECAY = 0.01
RATE_TABLE = 0.5
RATE_INNER = 0.01
RATE_GAIN = 0.2
RATE_BIAS = 0.3
RATE_ATTENTION = 0.01
NEGATIVE = -1000000000.0
HIGH = lax.Precision.HIGHEST

@jax.custom_vjp
def low(v):
    return lax.optimization_barrier(v.astype(jnp.bfloat16)).astype(jnp.float32)

@jax.custom_vjp
def low_back(v):
    return v

def low_keep(v):
    return (low(v), None)

def low_pass(kept, grad):
    return (grad,)

def back_keep(v):
    return (v, None)

def back_low(kept, grad):
    return (low(grad),)
low.defvjp(low_keep, low_pass)
low_back.defvjp(back_keep, back_low)

def rms_rows(values, gain_row):
    return values * lax.rsqrt(lax.optimization_barrier(jnp.mean(values * values, -1, keepdims=True)) + EPS) * gain_row

def matmul(left, right):
    return jnp.dot(left, right, precision=HIGH)

def position_table(bucket_row, bias_layer):
    length = (bucket_row.shape[0] + 1) // 2
    offsets = jnp.arange(length)[None, :] - jnp.arange(length)[:, None] + length - 1
    return jnp.transpose(bias_layer[bucket_row[offsets]], (2, 0, 1))

def split_heads(values):
    return values.reshape(MICRO, -1, HEADS, DK)

def attend(queries, keys_in, values_in, bias_term, causal):
    scores = jnp.einsum('sqhd,skhd->shqk', split_heads(queries), split_heads(keys_in), precision=HIGH) * DK ** (-0.5)
    if bias_term is not None:
        scores = scores + bias_term[None]
    scores = low_back(scores)
    if causal:
        length = scores.shape[-1]
        lower_mask = jnp.arange(length)[:, None] >= jnp.arange(length)[None, :]
        scores = jnp.where(lower_mask, scores, NEGATIVE)
    row_peak = lax.optimization_barrier(jnp.max(scores, -1, keepdims=True))
    raised = jnp.exp(scores - row_peak)
    probs = raised / lax.optimization_barrier(jnp.sum(raised, -1, keepdims=True))
    mixed = jnp.einsum('shqk,skhd->sqhd', low(probs), split_heads(values_in), precision=HIGH)
    return low(low_back(mixed.reshape(queries.shape)))

def attention_layer(resid, gain_row, weight_set, source, bias_term, causal):
    normed = low(rms_rows(resid, gain_row))
    kv_input = normed if source is None else source
    queries = low(low_back(matmul(normed, weight_set[0])))
    keys_in = low(low_back(matmul(kv_input, weight_set[1])))
    values_in = low(low_back(matmul(kv_input, weight_set[2])))
    mixed = attend(queries, keys_in, values_in, bias_term, causal)
    return resid + low_back(matmul(mixed, weight_set[3]))

def feed_layer(resid, gain_row, inner, outer):
    normed = low(rms_rows(resid, gain_row))
    active = low(jax.nn.gelu(low_back(matmul(normed, inner))))
    return resid + low_back(matmul(active, outer))

def pair_loss(lowered, buckets, enc_rows, dec_rows, goal_rows, live_rows):
    table_low, inner_low, outer_low, gain_rows, bias_rows, attention_low = lowered
    resid = low_back(table_low[enc_rows.reshape(-1)])
    resid = attention_layer(resid, gain_rows[0], attention_low[0:4], None, position_table(buckets[0], bias_rows[0]), False)
    resid = feed_layer(resid, gain_rows[1], inner_low[0], outer_low[0])
    encoded = low(low_back(rms_rows(resid, gain_rows[2])))
    resid = low_back(table_low[dec_rows.reshape(-1)])
    resid = attention_layer(resid, gain_rows[3], attention_low[4:8], None, position_table(buckets[1], bias_rows[1]), True)
    resid = attention_layer(resid, gain_rows[4], attention_low[8:12], encoded, None, False)
    resid = feed_layer(resid, gain_rows[5], inner_low[1], outer_low[1])
    final = low(low_back(rms_rows(resid, gain_rows[6]) * D ** (-0.5)))
    live_flat = live_rows.reshape(-1)
    head = final * live_flat[:, None]
    logits = low_back(matmul(head, table_low.T))
    row_peak = lax.optimization_barrier(jnp.max(logits, -1, keepdims=True))
    log_total = row_peak[:, 0] + jnp.log(lax.optimization_barrier(jnp.sum(jnp.exp(logits - row_peak), -1)))
    target_logit = lax.optimization_barrier(jnp.sum(head * table_low[goal_rows.reshape(-1)], -1))
    return jnp.sum(live_flat * (log_total - target_logit))

def adamw(weight, first, second, gradient, rate):
    first = BETA_ONE * first + (1 - BETA_ONE) * gradient
    second = BETA_TWO * second + (1 - BETA_TWO) * gradient * gradient
    stepped = first / (1 - BETA_ONE ** STEP) / (jnp.sqrt(second / (1 - BETA_TWO ** STEP)) + ADAM_EPS)
    return (first, second, weight - rate * (stepped + DECAY * weight))

def reference(token_ids, targets, objective, buckets, table, table_first, table_second, inner_weight, inner_first, inner_second, outer_weight, outer_first, outer_second, gain_rows, gain_first, gain_second, position_bias, bias_first, bias_second, attention, left_stats, right_stats, left_roots, right_inverse_roots):
    half_sections = SECTIONS // 2
    enc_rows = token_ids[:, :half_sections].reshape(-1, MICRO, LEN)
    dec_rows = token_ids[:, half_sections:].reshape(-1, MICRO, LEN)
    goal_rows = jnp.stack([targets[:, half_sections:], targets[:, :half_sections]], 2).reshape(-1, MICRO, LEN)
    objective_pairs = jnp.stack([objective[:, half_sections:], objective[:, :half_sections]], 2).reshape(-1, MICRO)
    live_length = jnp.where(objective_pairs == 1, LEN, SPAN)
    live_rows = (jnp.arange(LEN)[None, None, :] < live_length[:, :, None]).astype(jnp.float32)

    def total_loss(params):
        lowered = (low(params[0]), low(params[1]), low(params[2]), params[3], params[4], low(params[5]))

        def visit(running, pair_data):
            return (running + jax.checkpoint(pair_loss)(lowered, buckets, *pair_data), None)
        result, unused = lax.scan(visit, jnp.zeros((), jnp.float32), (enc_rows, dec_rows, goal_rows, live_rows))
        return result
    params = (table, inner_weight, outer_weight, gain_rows, position_bias, attention)
    loss_sum, pull = jax.vjp(total_loss, params)
    grads = pull(jnp.ones_like(loss_sum))[0]
    loss_count = jnp.sum(live_rows)
    square_sum = sum((jnp.sum(member * member) for member in grads))
    grad_norm = jnp.sqrt(square_sum)
    clip_factor = CLIP / jnp.maximum(grad_norm, CLIP)
    table_out = adamw(table, table_first, table_second, grads[0] * clip_factor, RATE_TABLE)
    inner_out = adamw(inner_weight, inner_first, inner_second, grads[1] * clip_factor, RATE_INNER)
    outer_out = adamw(outer_weight, outer_first, outer_second, grads[2] * clip_factor, RATE_INNER)
    gain_out = adamw(gain_rows, gain_first, gain_second, grads[3] * clip_factor, RATE_GAIN)
    bias_out = adamw(position_bias, bias_first, bias_second, grads[4] * clip_factor, RATE_BIAS)
    graded = grads[5]
    blended_left_factor = low(jnp.einsum('mij,mjk->mik', left_roots.astype(jnp.float32), graded, precision=HIGH))
    direction = jnp.einsum('mij,mjk->mik', blended_left_factor, right_inverse_roots.astype(jnp.float32), precision=HIGH)
    spread = jnp.sqrt(lax.optimization_barrier(jnp.mean(direction * direction, (1, 2), keepdims=True)) + EPS)
    clipped = graded * clip_factor
    left_new = BETA_STATS * left_stats + (1 - BETA_STATS) * jnp.einsum('mij,mkj->mik', clipped, clipped, precision=HIGH)
    right_new = BETA_STATS * right_stats + (1 - BETA_STATS) * jnp.einsum('mji,mjk->mik', clipped, clipped, precision=HIGH)
    attention_new = attention - RATE_ATTENTION * (direction / spread + DECAY * attention)
    return (loss_sum, loss_count, grad_norm, table_out[0], table_out[1], table_out[2], inner_out[0], inner_out[1], inner_out[2], outer_out[0], outer_out[1], outer_out[2], gain_out[0], gain_out[1], gain_out[2], bias_out[0], bias_out[1], bias_out[2], clipped, left_new, right_new, attention_new)
```

```python
import jax
import jax.numpy as jnp
from jax import lax
from jax.sharding import PartitionSpec as P

D = 768
HEADS = 12
DK = 64
MICRO = 2
STEP = 5
SPAN = 28
MATRICES = 4


EPS = 1e-06
CLIP = 1.0
BETA_ONE = 0.9
BETA_TWO = 0.95
BETA_STATS = 0.95
ADAM_EPS = 1e-08
DECAY = 0.01
RATE_TABLE = 0.5
RATE_INNER = 0.01
RATE_GAIN = 0.2
RATE_BIAS = 0.3
RATE_ATTENTION = 0.01
NEGATIVE = -1000000000.0
HIGH = lax.Precision.HIGHEST


def to_low(values):
    return values.astype(jnp.bfloat16)


def to_full(values):
    return values.astype(jnp.float32)


def pick(values, index, axis):
    return lax.dynamic_index_in_dim(values, index, axis, False)


def swap_bit(value, bit):
    pairs = [(source, source ^ (1 << bit)) for source in range(lax.axis_size("section"))]
    return lax.ppermute(value, "section", pairs)


def section_bit(bit):
    return (lax.axis_index("section") >> bit) & 1


def swap_half(value):
    return lax.ppermute(value, "dp", [(0, 1), (1, 0)])


def to_decoder(value):
    return lax.ppermute(value, "dp", [(0, 1)])


def to_encoder(value):
    return lax.ppermute(value, "dp", [(1, 0)])


def sum_to_owner(values, axes):
    axes = list(axes)
    while axes:
        bit, axis = axes.pop(0)
        mine = section_bit(bit)
        arrived = swap_bit(to_low(pick(values, 1 - mine, axis)), bit)
        values = to_full(pick(values, mine, axis)) + to_full(arrived)
        axes = [(b, a - 1 if a > axis else a) for b, a in axes]
    return values


def forward_mul(left, right):
    return jnp.dot(left, right, preferred_element_type=jnp.float32)


def weight_grad(inputs, upstream):
    return jnp.einsum("nd,ne->de", inputs, upstream, preferred_element_type=jnp.float32)


def input_grad(upstream, weight):
    return jnp.einsum("ne,de->nd", upstream, weight, preferred_element_type=jnp.float32)


def rms_rows(values, gain_row):
    return values * lax.rsqrt(jnp.mean(values * values, -1, keepdims=True) + EPS) * gain_row


def final_rows(values, gain_row):
    return rms_rows(values, gain_row) * D ** (-0.5)


def norm_back(norm_rule, values, gain_row, upstream):
    result, pull = jax.vjp(norm_rule, values, gain_row)
    return pull(upstream)


def split_heads(values):
    return values.reshape(MICRO, -1, HEADS, DK)


def offset_square(row, length):
    width = 2 * length
    padded = jnp.pad(row, (0, width - row.shape[0]))
    flat = jnp.tile(padded, length)[length - 1 : length - 1 + length * (width - 1)]
    return flat.reshape(length, width - 1)[:, :length]


def position_table(onehot, bias_layer):
    return jnp.einsum("qkb,bh->hqk", onehot.astype(jnp.float32), bias_layer, precision=HIGH)


def score_block(query_heads, key_heads, bias_term, allowed):
    scores = jnp.einsum(
        "sqhd,skhd->shqk", query_heads, key_heads, preferred_element_type=jnp.float32
    ) * DK ** (-0.5)
    if bias_term is not None:
        scores = jnp.where(allowed, scores + bias_term[None], NEGATIVE)
    return scores


def attend_forward(query_heads, key_heads, value_heads, bias_term, allowed):
    scores = score_block(query_heads, key_heads, bias_term, allowed)
    row_peak = jnp.max(scores, -1, keepdims=True)
    log_total = row_peak + jnp.log(jnp.sum(jnp.exp(scores - row_peak), -1, keepdims=True))
    probs_low = to_low(jnp.exp(scores - log_total))
    mixed = jnp.einsum(
        "shqk,skhd->sqhd", probs_low, value_heads, preferred_element_type=jnp.float32
    )
    return (mixed, log_total)


def attend_backward(query_heads, key_heads, value_heads, bias_term, allowed, log_total, grad_mixed):
    scores = score_block(query_heads, key_heads, bias_term, allowed)
    probs = jnp.exp(scores - log_total)
    grad_probs = jnp.einsum(
        "sqhd,skhd->shqk", grad_mixed, value_heads, preferred_element_type=jnp.float32
    )
    grad_scores = to_low(probs * (grad_probs - jnp.sum(probs * grad_probs, -1, keepdims=True)))
    grad_value = jnp.einsum(
        "shqk,sqhd->skhd", to_low(probs), grad_mixed, preferred_element_type=jnp.float32
    )
    grad_query = jnp.einsum(
        "shqk,skhd->sqhd", grad_scores, key_heads, preferred_element_type=jnp.float32
    ) * DK ** (-0.5)
    grad_key = jnp.einsum(
        "shqk,sqhd->skhd", grad_scores, query_heads, preferred_element_type=jnp.float32
    ) * DK ** (-0.5)
    return (grad_query, grad_key, grad_value, grad_scores)


def attention_forward(resid, gain_row, weight_set, source, bias_term, allowed):
    normed = to_low(rms_rows(resid, gain_row))
    kv_input = normed if source is None else source
    query_rows = to_low(forward_mul(normed, weight_set[0]))
    key_rows = to_low(forward_mul(kv_input, weight_set[1]))
    value_rows = to_low(forward_mul(kv_input, weight_set[2]))
    mixed, log_total = attend_forward(
        split_heads(query_rows), split_heads(key_rows), split_heads(value_rows), bias_term, allowed
    )
    mixed_low = to_low(mixed.reshape(resid.shape))
    kept = (resid, normed, query_rows, key_rows, value_rows, mixed_low, log_total)
    return (resid + forward_mul(mixed_low, weight_set[3]), kept)


def attention_backward(grad_resid, kept, gain_row, weight_set, source, bias_term, allowed, onehot):
    resid, normed, query_rows, key_rows, value_rows, mixed_low, log_total = kept
    kv_input = normed if source is None else source
    grad_out = to_low(grad_resid)
    grad_mixed = to_low(input_grad(grad_out, weight_set[3]))
    grad_query, grad_key, grad_value, grad_scores = attend_backward(
        split_heads(query_rows),
        split_heads(key_rows),
        split_heads(value_rows),
        bias_term,
        allowed,
        log_total,
        split_heads(grad_mixed),
    )
    grad_query = to_low(grad_query.reshape(resid.shape))
    grad_key = to_low(grad_key.reshape(key_rows.shape))
    grad_value = to_low(grad_value.reshape(value_rows.shape))
    weight_grads = jnp.stack(
        [
            weight_grad(normed, grad_query),
            weight_grad(kv_input, grad_key),
            weight_grad(kv_input, grad_value),
            weight_grad(mixed_low, grad_out),
        ]
    )
    grad_normed = input_grad(grad_query, weight_set[0])
    source_grad = input_grad(grad_key, weight_set[1]) + input_grad(grad_value, weight_set[2])
    if source is None:
        grad_normed = grad_normed + source_grad
    grad_in, grad_gain = norm_back(rms_rows, resid, gain_row, grad_normed)
    bias_grad = None
    if bias_term is not None:
        bias_grad = jnp.einsum(
            "shqk,qkb->bh", grad_scores, onehot, preferred_element_type=jnp.float32
        )
    return (grad_resid + grad_in, grad_gain, weight_grads, source_grad, bias_grad)


def feed_forward(resid, gain_row, feed):
    normed = to_low(rms_rows(resid, gain_row))
    before = input_grad(normed, feed[0])
    active = to_low(jax.nn.gelu(before))
    return (resid + forward_mul(active, feed[1]), (resid, normed, before, active))


def feed_backward(grad_resid, kept, gain_row, feed):
    resid, normed, before, active = kept
    grad_out = to_low(grad_resid)
    grad_active = input_grad(grad_out, feed[1])
    result, pull = jax.vjp(jax.nn.gelu, before)
    grad_before = to_low(pull(grad_active)[0])
    grad_normed = forward_mul(grad_before, feed[0])
    grad_in, grad_gain = norm_back(rms_rows, resid, gain_row, grad_normed)
    feed_grads = jnp.stack([weight_grad(grad_before, normed), weight_grad(active, grad_out)])
    return (grad_resid + grad_in, grad_gain, feed_grads)


def adamw(weight, first, second, gradient, rate):
    first = BETA_ONE * first + (1 - BETA_ONE) * gradient
    second = BETA_TWO * second + (1 - BETA_TWO) * gradient * gradient
    stepped = first / (1 - BETA_ONE**STEP) / (jnp.sqrt(second / (1 - BETA_TWO**STEP)) + ADAM_EPS)
    return (first, second, weight - rate * (stepped + DECAY * weight))


def ordered(own, other, mine, axis):
    return jnp.where(
        mine == 0, jnp.stack([own, other], axis), jnp.stack([other, own], axis)
    )


def rows_to_matrix(rows):
    first, second = section_bit(0), section_bit(1)
    split = rows.reshape(2, 2, -1, D)
    arrived = swap_bit(pick(split, 1 - second, 1), 1)
    split = ordered(pick(split, second, 1), arrived, second, 1)
    arrived = swap_bit(pick(split, 1 - first, 0), 0)
    return ordered(pick(split, first, 0), arrived, first, 1).reshape(-1, D)


def matrix_to_rows(block):
    first, second = section_bit(0), section_bit(1)
    kinds, rows = block.shape[0], block.shape[1] // 4
    split = block.reshape(kinds, 2, 2, rows, D)
    arrived = swap_bit(pick(split, 1 - first, 2), 0)
    split = ordered(pick(split, first, 2), arrived, first, 1)
    arrived = swap_bit(pick(split, 1 - second, 2), 1)
    split = ordered(pick(split, second, 2), arrived, second, 2)
    return split.reshape(kinds, MATRICES, rows, D)


def gather_group(block):
    sections = lax.axis_size("section")
    groups = [list(range(low, sections, MATRICES)) for low in range(MATRICES)]
    return lax.all_gather(block, "section", axis=0, tiled=True, axis_index_groups=groups)


def sum_matrices(grads):
    bits = lax.axis_size("section").bit_length() - 1
    split = grads.reshape((2,) * bits + (-1, D))
    axes = [(0, 0), (1, 1)] + [(bit, 1 + bits - bit) for bit in range(2, bits)]
    return sum_to_owner(split, axes)


def sum_feed(grads):
    bits = lax.axis_size("section").bit_length() - 1
    split = grads.reshape((2,) + (2,) * bits + (-1, D))
    return sum_to_owner(split, [(bit, bits - bit) for bit in range(bits)])


def shampoo_terms(block, left_block, right_full):
    low = to_low(block)
    full = gather_group(low)
    rows = block.shape[0]
    start = (lax.axis_index("section") // MATRICES) * rows
    columns = lax.dynamic_slice_in_dim(full, start, rows, 1)
    blended = to_low(forward_mul(left_block, full))
    direction = forward_mul(blended, right_full)
    left_term = jnp.einsum("rd,ed->re", low, full, preferred_element_type=jnp.float32)
    right_term = jnp.einsum("dr,de->re", columns, full, preferred_element_type=jnp.float32)
    return matrix_to_rows(
        jnp.stack([low, to_low(direction), to_low(left_term), to_low(right_term)])
    )


def lookup_rows(ids, shard_low):
    sections = lax.axis_size("section")
    bits = sections.bit_length() - 1
    count = ids.shape[1]
    start = lax.axis_index("section") * shard_low.shape[0]
    split = (ids - start).reshape((2,) * bits + (count,))

    def owned(some_ids):
        hit = some_ids.reshape(-1, 1) == jnp.arange(shard_low.shape[0])[None, :]
        return to_low(forward_mul(hit.astype(jnp.bfloat16), shard_low))

    mine = section_bit(0)
    arrived = swap_bit(owned(pick(split, 1 - mine, bits - 1)), 0)
    rows = owned(pick(split, mine, bits - 1)) + arrived
    rows = rows.reshape((2,) * (bits - 1) + (count, D))
    for bit in range(1, bits):
        axis = bits - 1 - bit
        mine = section_bit(bit)
        arrived = swap_bit(pick(rows, 1 - mine, axis), bit)
        rows = pick(rows, mine, axis) + arrived
    return rows


def local(
    token_ids,
    targets,
    objective,
    buckets,
    table,
    table_first,
    table_second,
    inner_weight,
    inner_first,
    inner_second,
    outer_weight,
    outer_first,
    outer_second,
    gain_rows,
    gain_first,
    gain_second,
    position_bias,
    bias_first,
    bias_second,
    attention,
    left_stats,
    right_stats,
    left_roots,
    right_inverse_roots,
):
    sections = lax.axis_size("section")
    section_index = lax.axis_index("section")
    half = lax.axis_index("dp")
    is_encoder = half == 0
    is_decoder = half == 1
    length = token_ids.shape[-1]
    vocab_rows = table.shape[0]
    bits = sections.bit_length() - 1

    packed = jnp.concatenate(
        [token_ids.reshape(-1), targets.reshape(-1), objective.reshape(-1)]
    )
    every = lax.all_gather(packed, ("section", "dp")).reshape(sections, 2, -1).swapaxes(0, 1)
    every_tokens = every[:, :, : MICRO * length]
    every_targets = every[:, :, MICRO * length : (MICRO + 1) * length]
    every_objective = every[:, :, (MICRO + 1) * length]
    halves = sections // 2
    encoder_ids = every_tokens[:, :halves].reshape(sections, MICRO * length)
    decoder_ids = every_tokens[:, halves:].reshape(sections, MICRO * length)
    own_ids = jnp.where(is_encoder, encoder_ids, decoder_ids)

    def of_micro(values):
        return jnp.where(is_encoder, values[:, halves:], values[:, :halves])

    goal_ids = of_micro(every_targets).reshape(-1)
    goal_objective = of_micro(every_objective).reshape(sections)
    live_all = (
        jnp.arange(length)[None, :] < jnp.where(goal_objective == 1, length, SPAN)[:, None]
    ).astype(jnp.float32)
    live_rows = pick(live_all, section_index, 0)

    shard_low = to_low(table)
    attention_low = to_low(attention)
    self_shard = lax.dynamic_slice_in_dim(attention_low, half * MATRICES, MATRICES, 0)
    feed_shard = jnp.stack(
        [to_low(pick(inner_weight, half, 0).T), to_low(pick(outer_weight, half, 0))]
    )
    self_weights = lax.all_gather(self_shard, "section", axis=1, tiled=True)
    feed_weights = lax.all_gather(feed_shard, "section", axis=1, tiled=True)
    cross_weights = lax.all_gather(attention_low[8:12], "section", axis=1, tiled=True)

    bucket_square = offset_square(pick(buckets, half, 0), length)
    bucket_range = jnp.arange(position_bias.shape[1])
    onehot = (bucket_square[:, :, None] == bucket_range).astype(jnp.bfloat16)
    bias_term = position_table(onehot, pick(position_bias, half, 0))
    allowed = is_encoder | (jnp.arange(length)[:, None] >= jnp.arange(length)[None, :])

    resid = to_full(lookup_rows(own_ids, shard_low))
    gain_self = gain_rows[jnp.where(is_encoder, 0, 3)]
    gain_feed = gain_rows[jnp.where(is_encoder, 1, 5)]
    resid, kept_self = attention_forward(
        resid, gain_self, self_weights, None, bias_term, allowed
    )

    def encoder_rest():
        after, kept_feed = feed_forward(resid, gain_feed, feed_weights)
        return (to_low(rms_rows(after, gain_rows[2])), after, kept_feed)

    encoded, resid_enc, kept_feed = lax.cond(
        is_encoder, encoder_rest, lambda: jax.tree.map(jnp.zeros_like, encoder_rest())
    )
    arrived = to_decoder(encoded)

    def decoder_rest(kept_feed, resid_enc):
        after, kept_cross = attention_forward(
            resid, gain_rows[4], cross_weights, arrived, None, None
        )
        after, kept_feed = feed_forward(after, gain_feed, feed_weights)
        return (to_low(final_rows(after, gain_rows[6])), after, kept_feed, kept_cross)

    def decoder_skip(kept_feed, resid_enc):
        shapes = jax.eval_shape(decoder_rest, kept_feed, resid_enc)
        empty = jax.tree.map(lambda a: jnp.zeros(a.shape, a.dtype), shapes)
        return (empty[0], resid_enc, kept_feed, empty[3])

    final_low, resid_last, kept_feed, kept_cross = lax.cond(
        is_decoder, decoder_rest, decoder_skip, kept_feed, resid_enc
    )

    final_split = final_low.reshape(MICRO, length, D)
    handed = to_encoder(final_split[0])
    own_rows = jnp.where(is_encoder, handed, final_split[1])
    head_low = own_rows * live_rows[:, None].astype(jnp.bfloat16)
    all_rows = lax.all_gather(head_low, "section", axis=0, tiled=True)
    logits = jnp.einsum("nd,vd->nv", all_rows, shard_low, preferred_element_type=jnp.float32)
    goal_hit = (goal_ids - section_index * vocab_rows)[:, None] == jnp.arange(vocab_rows)[None, :]
    row_peak = jnp.max(logits, -1)
    row_total = jnp.sum(jnp.exp(logits - row_peak[:, None]), -1)
    goal_logit = jnp.sum(jnp.where(goal_hit, logits, 0.0), -1)
    every_stat = lax.all_gather(jnp.stack([row_peak, row_total]), "section")
    top_peak = jnp.max(every_stat[:, 0], 0)
    log_total = top_peak + jnp.log(
        jnp.sum(every_stat[:, 1] * jnp.exp(every_stat[:, 0] - top_peak), 0)
    )
    grad_logits = to_low(jnp.exp(logits - log_total[:, None]) - goal_hit.astype(jnp.float32))
    grad_all = forward_mul(grad_logits, shard_low)
    split_grad = grad_all.reshape((2,) * bits + (length, D))
    grad_head = sum_to_owner(split_grad, [(bit, bits - 1 - bit) for bit in range(bits)])
    grad_head = to_low(grad_head * live_rows[:, None])
    own_live = lax.dynamic_slice_in_dim(log_total, section_index * length, length, 0)
    loss_part = jnp.sum(live_rows * own_live) - jnp.sum(live_all.reshape(-1) * goal_logit)
    count_part = jnp.sum(live_rows)
    head_table = to_low(
        jnp.einsum("nv,nd->vd", grad_logits, all_rows, preferred_element_type=jnp.float32)
    )
    grad_final = jnp.stack([to_decoder(grad_head), grad_head]).reshape(MICRO * length, D)

    def decoder_back():
        grad_resid, gain_last = norm_back(
            final_rows, resid_last, gain_rows[6], to_full(grad_final)
        )
        grad_resid, gain_fed, feed_grads = feed_backward(
            grad_resid, kept_feed, gain_feed, feed_weights
        )
        grad_resid, gain_crossed, cross_grads, grad_source, unused = attention_backward(
            grad_resid, kept_cross, gain_rows[4], cross_weights, arrived, None, None, None
        )
        return (
            grad_resid,
            feed_grads,
            cross_grads,
            to_low(grad_source),
            gain_fed,
            gain_last,
            gain_crossed,
        )

    grad_resid, feed_grads, cross_grads, grad_source, gain_fed, gain_last, gain_crossed = lax.cond(
        is_decoder, decoder_back, lambda: jax.tree.map(jnp.zeros_like, decoder_back())
    )
    back_source = to_encoder(grad_source)

    def encoder_back(grad_resid, feed_grads, gain_fed, gain_last):
        grad_resid, gain_last = norm_back(
            rms_rows, resid_last, gain_rows[2], to_full(back_source)
        )
        grad_resid, gain_fed, feed_grads = feed_backward(
            grad_resid, kept_feed, gain_feed, feed_weights
        )
        return (grad_resid, feed_grads, gain_fed, gain_last)

    grad_resid, feed_grads, gain_fed, gain_last = lax.cond(
        is_encoder,
        encoder_back,
        lambda *same: same,
        grad_resid,
        feed_grads,
        gain_fed,
        gain_last,
    )
    grad_resid, gain_selfed, self_grads, unused, bias_grad = attention_backward(
        grad_resid, kept_self, gain_self, self_weights, None, bias_term, allowed, onehot
    )

    embed_low = to_low(grad_resid)
    both_rows = ordered(embed_low, swap_half(embed_low), half, 0)
    every_rows = lax.all_gather(both_rows, "section").reshape(-1, D)
    every_ids = jnp.stack([encoder_ids, decoder_ids], 1).reshape(-1)
    table_hit = (every_ids - section_index * vocab_rows)[None, :] == jnp.arange(vocab_rows)[:, None]
    head_both = to_full(head_table) + to_full(swap_half(head_table))
    table_grad = forward_mul(table_hit.astype(jnp.bfloat16), every_rows) + head_both

    feed_own = to_low(sum_feed(feed_grads))
    feed_both = to_full(ordered(feed_own, swap_half(feed_own), half, 1))
    inner_part = jnp.swapaxes(feed_both[0], 1, 2)
    outer_part = feed_both[1]

    left_self = lax.dynamic_slice_in_dim(left_roots, half * MATRICES, MATRICES, 0)
    right_self = lax.dynamic_slice_in_dim(right_inverse_roots, half * MATRICES, MATRICES, 0)
    cross_terms = shampoo_terms(
        sum_matrices(cross_grads),
        rows_to_matrix(left_roots[8:12]),
        gather_group(rows_to_matrix(right_inverse_roots[8:12])),
    )
    self_terms = shampoo_terms(
        sum_matrices(self_grads),
        rows_to_matrix(left_self),
        gather_group(rows_to_matrix(right_self)),
    )
    other_terms = swap_half(self_terms)
    cross_terms = jnp.where(is_encoder, to_encoder(cross_terms), cross_terms)
    terms = jnp.concatenate(
        [ordered(self_terms, other_terms, half, 1).reshape(4, 2 * MATRICES, -1, D), cross_terms], 1
    )
    attention_grad, direction, left_term, right_term = to_full(terms)

    gain_none = jnp.zeros_like(gain_selfed)
    gain_part = jnp.where(
        is_encoder,
        jnp.stack([gain_selfed, gain_fed, gain_last] + [gain_none] * 4),
        jnp.stack([gain_none] * 3 + [gain_selfed, gain_crossed, gain_fed, gain_last]),
    )
    bias_part = jnp.stack([jnp.where(half == layer, bias_grad, 0.0) for layer in range(2)])
    gain_full, bias_full = lax.psum((gain_part, bias_part), ("section", "dp"))

    square_sum = (
        jnp.sum(table_grad * table_grad)
        + jnp.sum(inner_part * inner_part)
        + jnp.sum(outer_part * outer_part)
        + jnp.sum(attention_grad * attention_grad)
    )
    small_square = jnp.sum(gain_full * gain_full) + jnp.sum(bias_full * bias_full)
    sums = jnp.concatenate(
        [
            jnp.stack([loss_part, count_part, 0.5 * square_sum]),
            0.5 * jnp.sum(direction * direction, (1, 2)),
        ]
    )
    sums = lax.psum(sums, ("section", "dp"))
    grad_norm = jnp.sqrt(sums[2] + small_square)
    clip_factor = CLIP / jnp.maximum(grad_norm, CLIP)
    table_out = adamw(table, table_first, table_second, table_grad * clip_factor, RATE_TABLE)
    inner_out = adamw(inner_weight, inner_first, inner_second, inner_part * clip_factor, RATE_INNER)
    outer_out = adamw(outer_weight, outer_first, outer_second, outer_part * clip_factor, RATE_INNER)
    gain_out = adamw(gain_rows, gain_first, gain_second, gain_full * clip_factor, RATE_GAIN)
    bias_out = adamw(position_bias, bias_first, bias_second, bias_full * clip_factor, RATE_BIAS)
    clip_square = clip_factor * clip_factor
    left_new = BETA_STATS * left_stats + (1 - BETA_STATS) * clip_square * left_term
    right_new = BETA_STATS * right_stats + (1 - BETA_STATS) * clip_square * right_term
    spread = jnp.sqrt(sums[3:] / (D * D) + EPS)[:, None, None]
    attention_new = attention - RATE_ATTENTION * (direction / spread + DECAY * attention)
    return (
        sums[0],
        sums[1],
        grad_norm,
        *table_out,
        *inner_out,
        *outer_out,
        *gain_out,
        *bias_out,
        attention_grad * clip_factor,
        left_new,
        right_new,
        attention_new,
    )


def solution(mesh):
    in_specs = (
        P("dp", "section", None, None),
        P("dp", "section", None),
        P("dp", "section"),
        P(),
        P("section", None),
        P("section", None),
        P("section", None),
        P(None, None, "section"),
        P(None, None, "section"),
        P(None, None, "section"),
        P(None, "section", None),
        P(None, "section", None),
        P(None, "section", None),
        P(),
        P(),
        P(),
        P(),
        P(),
        P(),
        P(None, "section", None),
        P(None, "section", None),
        P(None, "section", None),
        P(None, "section", None),
        P(None, "section", None),
    )
    out_specs = (
        P(),
        P(),
        P(),
        P("section", None),
        P("section", None),
        P("section", None),
        P(None, None, "section"),
        P(None, None, "section"),
        P(None, None, "section"),
        P(None, "section", None),
        P(None, "section", None),
        P(None, "section", None),
        P(),
        P(),
        P(),
        P(),
        P(),
        P(),
        P(None, "section", None),
        P(None, "section", None),
        P(None, "section", None),
        P(None, "section", None),
    )
    return jax.shard_map(local, mesh=mesh, in_specs=in_specs, out_specs=out_specs, check_vma=False)
```

```python
import functools
import heapq
import math

import jax
import jax.numpy as jnp
from jax import lax
from jax.experimental import pallas as pl
from jax.experimental.pallas import tpu as pltpu
from jax.sharding import PartitionSpec as P

D = 768
HEADS = 12
DK = 64
MICRO = 2
STEP = 5
SPAN = 28
MATRICES = 4


EPS = 1e-06
CLIP = 1.0
BETA_ONE = 0.9
BETA_TWO = 0.95
BETA_STATS = 0.95
ADAM_EPS = 1e-08
DECAY = 0.01
RATE_TABLE = 0.5
RATE_INNER = 0.01
RATE_GAIN = 0.2
RATE_BIAS = 0.3
RATE_ATTENTION = 0.01
NEGATIVE = -1000000000.0
HIGH = lax.Precision.HIGHEST
VMEM_BYTES = 52 * 1024 * 1024
LOW = jnp.bfloat16
FULL = jnp.float32


def to_low(values):
    return values.astype(jnp.bfloat16)


def to_full(values):
    return values.astype(jnp.float32)


def pick(values, index, axis):
    return lax.dynamic_index_in_dim(values, index, axis, False)


def bit_count():
    return lax.axis_size("section").bit_length() - 1


def section_bit(bit):
    return (lax.axis_index("section") >> bit) & 1


def swap_bit(value, bit, planes=(0, 1)):
    pairs = [
        (2 * source + plane, 2 * (source ^ (1 << bit)) + plane)
        for source in range(lax.axis_size("section"))
        for plane in planes
    ]
    return lax.ppermute(value, ("section", "dp"), pairs)


def swap_half(value):
    return lax.ppermute(value, "dp", [(0, 1), (1, 0)])


def to_decoder(value):
    return lax.ppermute(value, "dp", [(0, 1)])


def to_encoder(value):
    return lax.ppermute(value, "dp", [(1, 0)])


def over(bit, planes=(0, 1)):
    return lambda value: swap_bit(value, bit, planes)


def link_cost(bit, value):
    return 4 + value.size * (6e-6 if bit == 0 else 5.5e-5 if bit < 3 else 1.1e-4)


def interleave(tasks, after):
    results, free, pending, now, count = [None] * len(tasks), {}, [], 0.0, 0
    last = after

    def advance(index, arrived):
        nonlocal last, now, count
        try:
            link, cost, move, value = tasks[index].send(arrived)
        except StopIteration as stop:
            results[index] = stop.value
            return
        count += 1
        if move is None:
            heapq.heappush(pending, (now + cost, count, index, None))
            return
        value, last = lax.optimization_barrier((value, last))
        if link == "core":
            now += cost
            free[link] = now
        else:
            now += 1.0
            free[link] = max(now, free.get(link, 0.0)) + cost
        heapq.heappush(pending, (free[link], count, index, move(value)))

    for index in range(len(tasks)):
        advance(index, None)
    while pending:
        ended, unused, index, arrived = heapq.heappop(pending)
        now = max(now, ended)
        if arrived is not None:
            now += 1.0 + 4e-6 * arrived.size
            arrived, last = lax.optimization_barrier((arrived, last))
            last = arrived
        advance(index, arrived)
    return results


def halved(rows, layout, order, planes=(0, 1)):
    layout = list(layout)
    if isinstance(rows, tuple):
        part, kept = rows
        arrived = yield (0, link_cost(0, part), over(0, planes), part)
        rows = to_low(to_full(kept) + to_full(arrived))
    for bit in order:
        place = layout.index(bit)
        layout.remove(bit)
        split = rows.reshape(2**place, 2, -1, D)
        mine = section_bit(bit)
        part = to_low(pick(split, 1 - mine, 1)).reshape(-1, D)
        arrived = yield (bit, link_cost(bit, part), over(bit, planes), part)
        rows = to_low(to_full(pick(split, mine, 1).reshape(-1, D)) + to_full(arrived))
    return rows


def doubled(block, planes=(0, 1)):
    for stage, bit in enumerate(range(bit_count() - 1, 1, -1)):
        arrived = yield (bit, link_cost(bit, block), over(bit, planes), block)
        block = ordered(block, arrived, section_bit(bit), stage)
    return block.reshape(-1, D)


def to_rows(terms, planes=(0, 1)):
    first, second = section_bit(0), section_bit(1)
    part = pick(terms, 1 - first, 2)
    arrived = yield (0, link_cost(0, part), over(0, planes), part)
    terms = ordered(pick(terms, first, 2), arrived, first, 1)
    part = pick(terms, 1 - second, 2)
    arrived = yield (1, link_cost(1, part), over(1, planes), part)
    terms = ordered(pick(terms, second, 2), arrived, second, 2)
    return terms.reshape(terms.shape[0], MATRICES, -1, D)


def summed(values):
    arrived = yield ("dp", 5, swap_half, values)
    values = values + arrived
    for bit in range(bit_count()):
        arrived = yield (bit, 5, over(bit), values)
        values = values + arrived
    return values


def until(found, names):
    while not all(name in found for name in names):
        yield (None, 2, None, None)


def forward_mul(left, right):
    return jnp.dot(left, right, preferred_element_type=jnp.float32)


def offset_square(row, length):
    width = 2 * length
    padded = jnp.pad(row, (0, width - row.shape[0]))
    flat = jnp.tile(padded, length)[length - 1 : length - 1 + length * (width - 1)]
    return flat.reshape(length, width - 1)[:, :length]


def position_table(onehot, bias_layer):
    return jnp.einsum("qkb,bh->hqk", onehot.astype(jnp.float32), bias_layer, precision=HIGH)


def mul(left, right):
    return lax.dot_general(left, right, (((1,), (0,)), ((), ())), preferred_element_type=FULL)


def mul_right(left, right):
    return lax.dot_general(left, right, (((1,), (1,)), ((), ())), preferred_element_type=FULL)


def mul_left(left, right):
    return lax.dot_general(left, right, (((0,), (0,)), ((), ())), preferred_element_type=FULL)


def rms_scale(values):
    return lax.rsqrt(jnp.mean(values * values, -1, keepdims=True) + EPS)


def rms_back(values, gain_row, upstream):
    scale = rms_scale(values)
    normal = values * scale
    grad_gain = jnp.sum(upstream * normal, 0, keepdims=True)
    weighted = upstream * gain_row
    inner = jnp.mean(weighted * normal, -1, keepdims=True)
    return scale * (weighted - normal * inner), grad_gain


def gelu_parts(values):
    inner = math.sqrt(2.0 / math.pi) * (values + 0.044715 * values * values * values)
    bent = jnp.tanh(inner)
    slope = math.sqrt(2.0 / math.pi) * (1.0 + 3 * 0.044715 * values * values)
    value = 0.5 * values * (1.0 + bent)
    grad = 0.5 * (1.0 + bent) + 0.5 * values * (1.0 - bent * bent) * slope
    return value, grad


def params():
    return pltpu.CompilerParams(vmem_limit_bytes=VMEM_BYTES)


def whole():
    return pl.BlockSpec(memory_space=pltpu.VMEM)


def feed_forward_kernel(
    last_scale, rows_ref, gain_ref, last_ref, in_ref, out_ref, after_ref, head_ref, before_ref, norm_ref, total_ref
):
    step = pl.program_id(0)

    @pl.when(step == 0)
    def start():
        rows = rows_ref[...]
        norm_ref[...] = (rows * rms_scale(rows) * gain_ref[...]).astype(LOW)
        total_ref[...] = rows

    before = mul_right(norm_ref[...], in_ref[0])
    before_ref[...] = before
    active, unused = gelu_parts(before)
    total_ref[...] += mul(active.astype(LOW), out_ref[0])

    @pl.when(step == pl.num_programs(0) - 1)
    def finish():
        after = total_ref[...]
        after_ref[...] = after
        head_ref[...] = (after * rms_scale(after) * last_ref[...] * last_scale).astype(LOW)


def feed_forward(rows, gain_row, last_gain, weights, last_scale):
    count, hidden = rows.shape[0], weights.shape[1]
    chunk = D
    fixed = pl.BlockSpec((count, D), lambda j: (0, 0))
    row = pl.BlockSpec((1, D), lambda j: (0, 0))
    return pl.pallas_call(
        functools.partial(feed_forward_kernel, last_scale),
        grid=(hidden // chunk,),
        in_specs=[
            fixed,
            row,
            row,
            pl.BlockSpec((1, chunk, D), lambda j: (1, j, 0)),
            pl.BlockSpec((1, chunk, D), lambda j: (2, j, 0)),
        ],
        out_specs=[fixed, fixed, pl.BlockSpec((count, chunk), lambda j: (0, j))],
        out_shape=[
            jax.ShapeDtypeStruct((count, D), FULL),
            jax.ShapeDtypeStruct((count, D), LOW),
            jax.ShapeDtypeStruct((count, hidden), FULL),
        ],
        scratch_shapes=[pltpu.VMEM((count, D), LOW), pltpu.VMEM((count, D), FULL)],
        compiler_params=params(),
        name="feed_forward",
    )(rows, gain_row[None], last_gain[None], weights, weights)


def feed_backward_kernel(
    last_scale,
    mine_ref,
    upstream_ref,
    after_ref,
    last_ref,
    rows_ref,
    gain_ref,
    before_ref,
    in_ref,
    out_ref,
    grad_ref,
    in_sent_ref,
    in_kept_ref,
    out_sent_ref,
    out_kept_ref,
    gains_ref,
    resid_ref,
    low_ref,
    norm_ref,
    total_ref,
):
    step = pl.program_id(0)

    @pl.when(step == 0)
    def start():
        upstream = upstream_ref[...].astype(FULL) * last_scale
        resid, grad_last = rms_back(after_ref[...], last_ref[...], upstream)
        resid_ref[...] = resid
        low_ref[...] = resid.astype(LOW)
        rows = rows_ref[...]
        norm_ref[...] = (rows * rms_scale(rows) * gain_ref[...]).astype(LOW)
        total_ref[...] = jnp.zeros_like(total_ref)
        gains_ref[1:2] = grad_last

    grad_out = low_ref[...]
    active, slope = gelu_parts(before_ref[...])
    grad_before = (mul_right(grad_out, out_ref[0]) * slope).astype(LOW)
    total_ref[...] += mul(grad_before, in_ref[0])
    in_grad = mul_left(grad_before, norm_ref[...]).astype(LOW)
    out_grad = mul_left(active.astype(LOW), grad_out).astype(LOW)

    @pl.when(step < 2)
    def send():
        in_sent_ref[...] = in_grad
        out_sent_ref[...] = out_grad

    @pl.when(step >= 2)
    def keep():
        in_kept_ref[...] = in_grad
        out_kept_ref[...] = out_grad

    @pl.when(step == pl.num_programs(0) - 1)
    def finish():
        grad_rows, grad_gain = rms_back(rows_ref[...], gain_ref[...], total_ref[...])
        grad_ref[...] = resid_ref[...] + grad_rows
        gains_ref[0:1] = grad_gain


def feed_backward(upstream, after, last_gain, rows, gain_row, before, weights, last_scale):
    count, hidden = before.shape
    chunk = hidden // 4

    def place(step, mine):
        return 2 * ((step >= 2) == (mine[0] == 1)) + step % 2

    fixed = pl.BlockSpec((count, D), lambda j, mine: (0, 0))
    row = pl.BlockSpec((1, D), lambda j, mine: (0, 0))
    sent = pl.BlockSpec((chunk, D), lambda j, mine: (jnp.minimum(j, 1), 0))
    kept = pl.BlockSpec((chunk, D), lambda j, mine: (jnp.maximum(j - 2, 0), 0))
    half = jax.ShapeDtypeStruct((hidden // 2, D), LOW)
    return pl.pallas_call(
        functools.partial(feed_backward_kernel, last_scale),
        grid_spec=pltpu.PrefetchScalarGridSpec(
            num_scalar_prefetch=1,
            grid=(4,),
            in_specs=[
                fixed,
                fixed,
                row,
                fixed,
                row,
                pl.BlockSpec((count, chunk), lambda j, mine: (0, place(j, mine))),
                pl.BlockSpec((1, chunk, D), lambda j, mine: (1, place(j, mine), 0)),
                pl.BlockSpec((1, chunk, D), lambda j, mine: (2, place(j, mine), 0)),
            ],
            out_specs=[fixed, sent, kept, sent, kept, pl.BlockSpec((2, D), lambda j, mine: (0, 0))],
            scratch_shapes=[
                pltpu.VMEM((count, D), FULL),
                pltpu.VMEM((count, D), LOW),
                pltpu.VMEM((count, D), LOW),
                pltpu.VMEM((count, D), FULL),
            ],
        ),
        out_shape=[jax.ShapeDtypeStruct((count, D), FULL)]
        + [half] * 4
        + [jax.ShapeDtypeStruct((2, D), FULL)],
        compiler_params=params(),
        name="feed_backward",
    )(section_bit(0)[None], upstream, after, last_gain[None], rows, gain_row[None], before, weights, weights)


def weight_spec(weights):
    slot, values = weights
    if slot is None:
        return pl.BlockSpec(memory_space=pltpu.VMEM)
    return pl.BlockSpec((1,) + values.shape[1:], lambda i: (slot, 0, 0))


def matrix_reader(ref, places):
    if places is None:
        return lambda m: ref[m]
    rows = D // len(places)
    return lambda m: jnp.concatenate(
        [ref[0, pl.ds((place * MATRICES + m) * rows, rows)] for place in places]
    )


def head_pairs(length):
    for sequence in range(MICRO):
        for pair in range(HEADS // 2):
            yield slice(sequence * length, (sequence + 1) * length), slice(
                pair * 2 * DK, (pair + 1) * 2 * DK
            ), pair


def probabilities(queries, keys_in, bias):
    scores = mul_right(queries, keys_in) * DK ** (-0.5)
    if bias is not None:
        scores = scores + bias
    raised = jnp.exp(scores - jnp.max(scores, -1, keepdims=True))
    return raised * (1.0 / jnp.sum(raised, -1, keepdims=True))


def attention_forward_kernel(biased, crossed, places, *refs):
    refs = list(refs)
    rows_ref, gain_ref, weight_ref = refs[:3]
    matrix = matrix_reader(weight_ref, places)
    source_ref = refs[3] if crossed else None
    bias_ref = refs[3 + crossed] if biased else None
    after_ref, norm_ref, query_ref, key_ref, value_ref, mixed_ref = refs[3 + crossed + biased :]
    rows = rows_ref[...]
    normed = (rows * rms_scale(rows) * gain_ref[...]).astype(LOW)
    norm_ref[...] = normed
    source = source_ref[...] if crossed else normed
    query_ref[...] = mul(normed, matrix(0)).astype(LOW)
    key_ref[...] = mul(source, matrix(1)).astype(LOW)
    value_ref[...] = mul(source, matrix(2)).astype(LOW)
    length = rows.shape[0] // MICRO
    left = lax.broadcasted_iota(jnp.int32, (length, 2 * DK), 1) < DK
    for rows_at, columns, pair in head_pairs(length):
        queries = query_ref[rows_at, columns]
        keys_in, values_in = key_ref[rows_at, columns], value_ref[rows_at, columns]
        mixed = []
        for side in range(2):
            picked = jnp.where(left == (side == 0), queries, jnp.zeros_like(queries))
            bias = bias_ref[2 * pair + side] if biased else None
            probs = probabilities(picked, keys_in, bias)
            mixed.append(mul(probs.astype(LOW), values_in))
        mixed_ref[rows_at, columns] = jnp.where(left, mixed[0], mixed[1]).astype(LOW)
    after_ref[...] = rows + mul(mixed_ref[...], matrix(3))


def attention_forward(rows, gain_row, weights, source, bias):
    crossed, biased = source is not None, bias is not None
    operands = [rows, gain_row[None], weights[1]]
    operands += [source] * crossed + [bias] * biased
    places = None if weights[0] is None else slot_places()
    low = jax.ShapeDtypeStruct(rows.shape, LOW)
    after, *kept = pl.pallas_call(
        functools.partial(attention_forward_kernel, biased, crossed, places),
        grid=(1,),
        in_specs=[whole()] * 2 + [weight_spec(weights)] + [whole()] * (len(operands) - 3),
        out_specs=[whole()] * 6,
        out_shape=[jax.ShapeDtypeStruct(rows.shape, FULL)] + [low] * 5,
        compiler_params=params(),
        name="attention_forward",
    )(*operands)
    return after, kept


def attention_backward_kernel(biased, crossed, places, mine_ref, *refs):
    refs = list(refs)
    grad_ref, rows_ref, gain_ref, weight_ref = refs[:4]
    matrix = matrix_reader(weight_ref, places)
    norm_ref, query_ref, key_ref, value_ref, mixed_ref = refs[4:9]
    source_ref = refs[9] if crossed else None
    bias_ref = refs[9 + crossed] if biased else None
    refs = refs[9 + crossed + biased :]
    result_ref, sent_ref, kept_ref, gain_grad_ref, extra_ref = refs[:5]
    grad_query_ref, grad_key_ref, grad_value_ref, grad_mixed_ref = refs[5:]
    mine = mine_ref[0]

    def put(m, value):
        @pl.when(mine == m // 2)
        def keep():
            kept_ref[pl.ds(m % 2 * D, D)] = value

        @pl.when(mine != m // 2)
        def send():
            sent_ref[pl.ds(m % 2 * D, D)] = value

    grad = grad_ref[...]
    grad_out = grad.astype(LOW)
    grad_mixed_ref[...] = mul_right(grad_out, matrix(3)).astype(LOW)
    put(3, mul_left(mixed_ref[...], grad_out).astype(LOW))
    length = grad.shape[0] // MICRO
    left = lax.broadcasted_iota(jnp.int32, (length, 2 * DK), 1) < DK
    for rows_at, columns, pair in head_pairs(length):
        queries, keys_in = query_ref[rows_at, columns], key_ref[rows_at, columns]
        values_in, grad_mixed = value_ref[rows_at, columns], grad_mixed_ref[rows_at, columns]
        parts = []
        for side in range(2):
            half = left == (side == 0)
            bias = bias_ref[2 * pair + side] if biased else None
            probs = probabilities(jnp.where(half, queries, jnp.zeros_like(queries)), keys_in, bias)
            picked = jnp.where(half, grad_mixed, jnp.zeros_like(grad_mixed))
            grad_probs = mul_right(picked, values_in)
            grad_scores = probs * (grad_probs - jnp.sum(probs * grad_probs, -1, keepdims=True))
            grad_scores = grad_scores.astype(LOW)
            if biased:
                if rows_at.start == 0:
                    extra_ref[2 * pair + side] = grad_scores.astype(FULL)
                else:
                    extra_ref[2 * pair + side] += grad_scores.astype(FULL)
            parts.append(
                (
                    mul(grad_scores, keys_in),
                    mul_left(grad_scores, queries),
                    mul_left(probs.astype(LOW), grad_mixed),
                )
            )
        scale = DK ** (-0.5)
        grad_query_ref[rows_at, columns] = (
            jnp.where(left, parts[0][0], parts[1][0]) * scale
        ).astype(LOW)
        grad_key_ref[rows_at, columns] = (
            jnp.where(left, parts[0][1], parts[1][1]) * scale
        ).astype(LOW)
        grad_value_ref[rows_at, columns] = jnp.where(left, parts[0][2], parts[1][2]).astype(LOW)
    normed = norm_ref[...]
    source = source_ref[...] if crossed else normed
    put(0, mul_left(normed, grad_query_ref[...]).astype(LOW))
    put(1, mul_left(source, grad_key_ref[...]).astype(LOW))
    put(2, mul_left(source, grad_value_ref[...]).astype(LOW))
    grad_norm = mul_right(grad_query_ref[...], matrix(0))
    grad_source = mul_right(grad_key_ref[...], matrix(1))
    grad_source = grad_source + mul_right(grad_value_ref[...], matrix(2))
    if crossed:
        extra_ref[...] = grad_source.astype(LOW)
    else:
        grad_norm = grad_norm + grad_source
    grad_rows, grad_gain = rms_back(rows_ref[...], gain_ref[...], grad_norm)
    result_ref[...] = (grad + grad_rows).astype(result_ref.dtype)
    gain_grad_ref[...] = grad_gain


def attention_backward(grad, rows, gain_row, weights, kept, source, bias):
    crossed, biased = source is not None, bias is not None
    operands = [section_bit(0)[None], grad, rows, gain_row[None], weights[1], *kept]
    places = None if weights[0] is None else slot_places()
    half = jax.ShapeDtypeStruct((MATRICES // 2 * D, D), LOW)
    operands += [source] * crossed + [bias] * biased
    low = pltpu.VMEM(rows.shape, LOW)
    extra = jax.ShapeDtypeStruct(bias.shape, FULL) if biased else jax.ShapeDtypeStruct(rows.shape, LOW)
    return pl.pallas_call(
        functools.partial(attention_backward_kernel, biased, crossed, places),
        grid=(1,),
        in_specs=[pl.BlockSpec(memory_space=pltpu.SMEM)]
        + [whole()] * 3
        + [weight_spec(weights)]
        + [whole()] * (len(operands) - 5),
        out_specs=[whole()] * 5,
        out_shape=[
            jax.ShapeDtypeStruct(rows.shape, FULL if crossed else LOW),
            half,
            half,
            jax.ShapeDtypeStruct((1, D), FULL),
            extra,
        ],
        scratch_shapes=[low] * 4,
        compiler_params=params(),
        name="attention_backward",
    )(*operands)


def adamw(weight, first, second, gradient, rate):
    first = BETA_ONE * first + (1 - BETA_ONE) * gradient
    second = BETA_TWO * second + (1 - BETA_TWO) * gradient * gradient
    stepped = first / (1 - BETA_ONE**STEP) / (jnp.sqrt(second / (1 - BETA_TWO**STEP)) + ADAM_EPS)
    return (first, second, weight - rate * (stepped + DECAY * weight))


def ordered(own, other, mine, axis):
    return jnp.where(
        mine == 0, jnp.stack([own, other], axis), jnp.stack([other, own], axis)
    )


def slot_places():
    order = low_bit_order()
    return [order.index(section) for section in range(len(order))]


def low_bit_order():
    sections = lax.axis_size("section")
    return sorted(range(sections), key=lambda p: (p & 1, (p >> 1) & 1, p >> 2))


def slot_layout():
    return [1] + list(range(bit_count() - 1, 1, -1))


def shampoo_terms(low, full, left_block, right_full):
    rows = low.shape[0]
    start = (lax.axis_index("section") // MATRICES) * rows
    columns = lax.dynamic_slice_in_dim(full, start, rows, 1)
    blended = to_low(forward_mul(left_block, full))
    direction = forward_mul(blended, right_full)
    left_term = jnp.einsum("rd,ed->re", low, full, preferred_element_type=jnp.float32)
    right_term = jnp.einsum("dr,de->re", columns, full, preferred_element_type=jnp.float32)
    terms = jnp.stack([low, to_low(direction), to_low(left_term), to_low(right_term)])
    return terms.reshape(4, 2, 2, rows // 4, D)


def gather_small(values):
    values = ordered(values, swap_half(values), lax.axis_index("dp"), 0)[None]
    for bit in range(bit_count()):
        both = ordered(values, swap_bit(values, bit), section_bit(bit), 0)
        values = both.reshape((-1,) + values.shape[1:])
    return values


def lookup_rows(ids, shard_low):
    bits = bit_count()
    start = lax.axis_index("section") * shard_low.shape[0]
    mine = section_bit(0)

    def owned(some_ids):
        hit = some_ids.reshape(-1, 1) == jnp.arange(shard_low.shape[0])[None, :]
        return to_low(forward_mul(hit.astype(jnp.bfloat16), shard_low))

    split = (ids - start).reshape((2,) * bits + (MICRO, -1))
    split = jnp.moveaxis(split, bits, 0)
    sent, kept = pick(split, 1 - mine, bits), pick(split, mine, bits)
    arrived = swap_bit(owned(sent), 0)
    rows = (owned(kept) + arrived).reshape(MICRO, -1, D)
    layout = range(bits - 1, 0, -1)
    orders = [list(range(1, bits)), list(range(2, bits)) + [1]]
    chains = [halved(rows[micro], layout, orders[micro]) for micro in range(MICRO)]
    return jnp.concatenate(interleave(chains, arrived))


def local(
    token_ids,
    targets,
    objective,
    buckets,
    table,
    table_first,
    table_second,
    inner_weight,
    inner_first,
    inner_second,
    outer_weight,
    outer_first,
    outer_second,
    gain_rows,
    gain_first,
    gain_second,
    position_bias,
    bias_first,
    bias_second,
    attention,
    left_stats,
    right_stats,
    left_roots,
    right_inverse_roots,
):
    sections = lax.axis_size("section")
    section_index = lax.axis_index("section")
    half = lax.axis_index("dp")
    is_encoder = half == 0
    is_decoder = half == 1
    length = token_ids.shape[-1]
    vocab_rows = table.shape[0]
    bits = sections.bit_length() - 1

    packed = jnp.concatenate(
        [token_ids.reshape(-1), targets.reshape(-1), jnp.broadcast_to(objective.reshape(-1), (length,))]
    )
    every = gather_small(packed.reshape(-1, length)).reshape(sections, 2, -1).swapaxes(0, 1)
    every_tokens = every[:, :, : MICRO * length]
    every_targets = every[:, :, MICRO * length : (MICRO + 1) * length]
    every_objective = every[:, :, (MICRO + 1) * length]
    halves = sections // 2
    encoder_ids = every_tokens[:, :halves].reshape(sections, MICRO * length)
    decoder_ids = every_tokens[:, halves:].reshape(sections, MICRO * length)
    own_ids = jnp.where(is_encoder, encoder_ids, decoder_ids)

    def of_micro(values):
        return jnp.where(is_encoder, values[:, halves:], values[:, :halves])

    goal_ids = of_micro(every_targets).reshape(-1)
    goal_objective = of_micro(every_objective).reshape(sections)
    live_all = (
        jnp.arange(length)[None, :] < jnp.where(goal_objective == 1, length, SPAN)[:, None]
    ).astype(jnp.float32)
    live_rows = pick(live_all, section_index, 0)

    shard_low = to_low(table)
    attention_low = to_low(attention)
    shard_rows = attention.shape[1] * MATRICES
    self_shard = lax.dynamic_slice_in_dim(attention_low, half * MATRICES, MATRICES, 0)
    weight_shard = jnp.stack(
        [
            self_shard.reshape(shard_rows, D),
            to_low(pick(inner_weight, half, 0).T),
            to_low(pick(outer_weight, half, 0)),
            attention_low[8:12].reshape(shard_rows, D),
        ]
    )
    weights = lax.all_gather(
        weight_shard, "section", axis=1, tiled=True, axis_index_groups=[low_bit_order()]
    )
    def natural(slot):
        split = slot.reshape(2, 2, sections // 4, MATRICES, -1, D)
        return jnp.transpose(split, (3, 2, 1, 0, 4, 5)).reshape(MATRICES, D, D)

    if attention.shape[1] % 16 == 0:
        self_weights, cross_weights = (0, weights), (3, weights)
    else:
        self_weights, cross_weights = (None, natural(weights[0])), (None, natural(weights[3]))

    bucket_square = offset_square(pick(buckets, half, 0), length)
    bucket_range = jnp.arange(position_bias.shape[1])
    onehot = (bucket_square[:, :, None] == bucket_range).astype(jnp.bfloat16)
    bias_term = position_table(onehot, pick(position_bias, half, 0))
    allowed = is_encoder | (jnp.arange(length)[:, None] >= jnp.arange(length)[None, :])

    rows_in = to_full(lookup_rows(own_ids, shard_low))
    gain_self = gain_rows[jnp.where(is_encoder, 0, 3)]
    gain_feed = gain_rows[jnp.where(is_encoder, 1, 5)]
    bias_term = jnp.where(allowed, bias_term, NEGATIVE)
    resid, kept_self = attention_forward(rows_in, gain_self, self_weights, None, bias_term)

    def encoder_rest():
        return feed_forward(resid, gain_feed, gain_rows[2], weights, 1.0)

    first, second = section_bit(0), section_bit(1)
    root_rows = jnp.stack([left_roots, right_inverse_roots])
    own_roots = lax.dynamic_slice_in_dim(root_rows, half * MATRICES, MATRICES, 1)
    root_rows = jnp.stack([own_roots, root_rows[:, 8:12]]).reshape(4, 2, 2, -1, D)
    root_rows, unused = lax.optimization_barrier((root_rows, resid))
    root_part = swap_bit(pick(root_rows, 1 - first, 1), 0)

    after_enc, encoded, before_enc = lax.cond(
        is_encoder, encoder_rest, lambda: jax.tree.map(jnp.zeros_like, encoder_rest())
    )
    encoded, root_part = lax.optimization_barrier((encoded, root_part))
    arrived = to_decoder(encoded)
    root_rows = ordered(pick(root_rows, first, 1), root_part, first, 2)
    root_part = swap_bit(pick(root_rows, 1 - second, 1), 1)

    def decoder_rest(after, before):
        rows_feed, kept_cross = attention_forward(
            resid, gain_rows[4], cross_weights, arrived, None
        )
        after, final, before = feed_forward(
            rows_feed, gain_feed, gain_rows[6], weights, D ** (-0.5)
        )
        return (final, after, before, rows_feed, kept_cross)

    def decoder_skip(after, before):
        empty = jnp.zeros(resid.shape, jnp.bfloat16)
        return (empty, after, before, resid, [empty] * 5)

    final_low, after_feed, before_feed, rows_feed, kept_cross = lax.cond(
        is_decoder, decoder_rest, decoder_skip, after_enc, before_enc
    )

    final_low, root_part = lax.optimization_barrier((final_low, root_part))
    root_rows = ordered(pick(root_rows, second, 1), root_part, second, 1)
    root_rows = root_rows.reshape(2, 2, -1, D)
    root_lefts, root_rights = root_rows[:, 0], root_rows[:, 1]

    final_split = final_low.reshape(MICRO, length, D)
    handed = to_encoder(final_split[0])
    own_rows = jnp.where(is_encoder, handed, final_split[1])
    head_low = own_rows * live_rows[:, None].astype(jnp.bfloat16)
    all_rows = lax.all_gather(head_low, "section", axis=0, tiled=True)
    logits = jnp.einsum("nd,vd->nv", all_rows, shard_low, preferred_element_type=jnp.float32)
    goal_hit = (goal_ids - section_index * vocab_rows)[:, None] == jnp.arange(vocab_rows)[None, :]
    row_peak = jnp.max(logits, -1)
    row_total = jnp.sum(jnp.exp(logits - row_peak[:, None]), -1)
    goal_logit = jnp.sum(jnp.where(goal_hit, logits, 0.0), -1)
    every_stat = lax.all_gather(jnp.stack([row_peak, row_total]), "section")
    top_peak = jnp.max(every_stat[:, 0], 0)
    log_total = top_peak + jnp.log(
        jnp.sum(every_stat[:, 1] * jnp.exp(every_stat[:, 0] - top_peak), 0)
    )
    grad_logits = to_low(jnp.exp(logits - log_total[:, None]) - goal_hit.astype(jnp.float32))
    grad_all = forward_mul(grad_logits, shard_low)
    def head_table_task():
        yield (None, 14, None, None)
        product = lambda grads: mul_left(grads, all_rows)
        return (yield ("core", 10, product, grad_logits))

    chain = halved(grad_all, range(bits - 1, -1, -1), range(bits))
    grad_head, head_table = interleave([chain, head_table_task()], log_total)
    grad_head = to_full(grad_head)
    grad_head = to_low(grad_head * live_rows[:, None])
    own_live = lax.dynamic_slice_in_dim(log_total, section_index * length, length, 0)
    loss_part = jnp.sum(live_rows * own_live) - jnp.sum(live_all.reshape(-1) * goal_logit)
    count_part = jnp.sum(live_rows)
    grad_final = jnp.stack([to_decoder(grad_head), grad_head]).reshape(MICRO * length, D)

    def decoder_back():
        grad_rows, *feed_grads, gains = feed_backward(
            grad_final,
            after_feed,
            gain_rows[6],
            rows_feed,
            gain_feed,
            before_feed,
            weights,
            D ** (-0.5),
        )
        grad_rows, *cross_grads, gain_cross, grad_source = attention_backward(
            grad_rows, resid, gain_rows[4], cross_weights, kept_cross, arrived, None
        )
        gains = jnp.concatenate([gain_cross, gains])
        return (grad_source, grad_rows, feed_grads, cross_grads, gains)

    root_steps = list(range(bits - 1, 1, -1))

    def root_step(stage):
        return swap_bit(root_rights, root_steps[stage])

    def grown(stage, part):
        mine = section_bit(root_steps[stage])
        return ordered(root_rights, part, mine, 1 + stage)

    for stage in range(len(root_steps) - 2):
        root_rights = grown(stage, root_step(stage))
    root_part = root_step(len(root_steps) - 2)
    grad_source, grad_dec, feed_dec, cross_grads, gains_dec = lax.cond(
        is_decoder, decoder_back, lambda: jax.tree.map(jnp.zeros_like, decoder_back())
    )
    back_source = to_encoder(grad_source)

    back_source, feed_dec, cross_grads, root_part = lax.optimization_barrier(
        (back_source, feed_dec, cross_grads, root_part)
    )
    root_rights = grown(len(root_steps) - 2, root_part)
    root_part = root_step(len(root_steps) - 1)

    late = to_low(to_full(feed_dec[1]) + to_full(swap_bit(feed_dec[0], 0, (1,))))
    late_split = late.reshape(2, -1, D)
    late_arrived = swap_bit(pick(late_split, 1 - second, 0), 1, (1,))

    def self_back(grad_rows):
        return attention_backward(
            grad_rows, rows_in, gain_self, self_weights, kept_self, None, bias_term
        )

    def encoder_feed():
        grad_rows, *feed_grads, gains = feed_backward(
            back_source,
            after_feed,
            gain_rows[2],
            resid,
            gain_feed,
            before_feed,
            weights,
            1.0,
        )
        return (grad_rows, gains, jnp.zeros(bias_term.shape, jnp.float32), feed_grads)

    def decoder_self():
        embed_low, *self_grads, gain_grad, score_grad = self_back(grad_dec)
        gains = jnp.concatenate([gain_grad, gain_grad])
        return (to_full(embed_low), gains, score_grad, self_grads + cross_grads)

    grad_rows, gains_middle, score_middle, grads_middle = lax.cond(
        is_encoder, encoder_feed, decoder_self
    )
    grad_rows, grads_middle = lax.optimization_barrier((grad_rows, grads_middle))
    sent_first = swap_bit(grads_middle[0], 0)
    sent_second = swap_bit(grads_middle[2], 0)

    def encoder_self():
        embed_low, *self_grads, gain_grad, score_grad = self_back(grad_rows)
        gains = jnp.concatenate([gain_grad, gains_middle, jnp.zeros((4, D), jnp.float32)])
        return (embed_low, gains, score_grad, self_grads)

    def decoder_skip_self():
        gains = jnp.concatenate([jnp.zeros((3, D), jnp.float32), gains_middle[:1], gains_dec])
        return (to_low(grad_rows), gains, score_middle, feed_dec[2:])

    embed_low, gain_part, score_grad, third_grads = lax.cond(
        is_encoder, encoder_self, decoder_skip_self
    )
    embed_low, third_grads, sent_first, sent_second, late_arrived, root_part = (
        lax.optimization_barrier(
            (embed_low, third_grads, sent_first, sent_second, late_arrived, root_part)
        )
    )
    late = to_low(to_full(pick(late_split, second, 0)) + to_full(late_arrived))
    root_rights = grown(len(root_steps) - 1, root_part).reshape(2, D, D)
    bias_grad = jnp.einsum("hqk,qkb->bh", score_grad, onehot.astype(jnp.float32), precision=HIGH)

    found = {}
    own_local = (own_ids.reshape(-1) - section_index * vocab_rows)[None, :]

    def squares(values):
        return jnp.sum(to_full(values) * to_full(values))

    def rows_task():
        every_rows = yield ("gather", 80, lambda rows: lax.all_gather(rows, "section"), embed_low)
        found["rows"] = every_rows.reshape(-1, D)

    cuts = [vocab_rows * part // 64 * 16 for part in range(4)] + [vocab_rows]

    def table_task(part):
        start, stop = cuts[part], cuts[part + 1]
        yield from until(found, ["rows"])

        def product(rows):
            hit = own_local == jnp.arange(start, stop)[:, None]
            return to_low(mul(hit.astype(jnp.bfloat16), rows) + head_table[start:stop])

        own = yield ("core", 6, product, found["rows"])
        other = yield ("dp", 19, swap_half, own)
        both = to_full(own) + to_full(other)
        found["table", part] = squares(both)
        return both

    def first_task():
        rows = to_low(to_full(grads_middle[1]) + to_full(sent_first))
        found["first"] = yield from halved(rows, slot_layout(), range(1, bits))

    def second_task():
        yield (None, 4, None, None)
        rows = to_low(to_full(grads_middle[3]) + to_full(sent_second))
        block = yield from halved(rows, slot_layout(), range(1, bits))
        found["second"] = block
        found["cross_square"] = squares(block)
        full = yield from doubled(block, (1,))
        terms = shampoo_terms(block, full, root_lefts[1], root_rights[1])
        found["cross_direction"] = squares(terms[1])
        terms = yield from to_rows(terms, (1,))
        other = yield ("dp", 30, to_encoder, terms)
        return jnp.where(is_encoder, other, terms)

    def third_task():
        found["third"] = yield from halved(tuple(third_grads), slot_layout(), range(1, bits))

    def late_task():
        found["late"] = yield from halved(late, slot_layout()[1:], range(2, bits), (1,))

    def self_task():
        yield from until(found, ["first", "third"])
        block = jnp.where(is_encoder, found["third"], found["first"])
        found["self_square"] = squares(block)
        full = yield from doubled(block)
        terms = shampoo_terms(block, full, root_lefts[0], root_rights[0])
        found["self_direction"] = squares(terms[1])
        terms = yield from to_rows(terms)
        other = yield ("dp", 30, swap_half, terms)
        return ordered(terms, other, half, 1).reshape(4, 2 * MATRICES, -1, D)

    def feed_task():
        yield from until(found, ["first", "second", "third", "late"])
        own = jnp.where(
            is_encoder,
            jnp.stack([found["first"], found["second"]]),
            jnp.stack([found["late"], found["third"]]),
        )
        found["feed_square"] = squares(own)
        other = yield ("dp", 15, swap_half, own)
        return to_full(ordered(own, other, half, 1))

    def small_task():
        small = jnp.concatenate(
            [gain_part.reshape(-1), jnp.where(half == 0, bias_grad, 0.0).reshape(-1)]
            + [jnp.where(half == 1, bias_grad, 0.0).reshape(-1)]
        )
        small = yield from summed(small.reshape(-1, 128))
        return small.reshape(-1)

    def norm_task():
        tables = [("table", part) for part in range(4)]
        yield from until(
            found,
            tables + ["self_square", "cross_square", "feed_square"]
            + ["self_direction", "cross_direction"],
        )
        cross_live = is_decoder.astype(jnp.float32)
        square_sum = (
            0.5 * sum(found[name] for name in tables)
            + found["self_square"]
            + found["feed_square"]
            + cross_live * found["cross_square"]
        )
        matrix = 2 * section_bit(0) + section_bit(1)
        names = jnp.arange(3 * MATRICES)
        own_matrix, cross_matrix = half * MATRICES + matrix, 2 * MATRICES + matrix
        directions = jnp.where(names == own_matrix, found["self_direction"], 0.0)
        directions = directions + jnp.where(
            names == cross_matrix, cross_live * found["cross_direction"], 0.0
        )
        sums = jnp.concatenate([jnp.stack([loss_part, count_part, square_sum]), directions])
        sums = yield from summed(jnp.pad(sums, (0, 128 - sums.shape[0])).reshape(1, 128))
        return sums[0, : 3 + 3 * MATRICES]

    tasks = [rows_task(), first_task(), third_task(), second_task(), late_task(), self_task()]
    tasks += [feed_task(), small_task(), norm_task()] + [table_task(part) for part in range(4)]
    results = interleave(tasks, embed_low)
    cross_terms, self_terms = results[3], results[5]
    feed_both, small, sums = results[6:9]
    table_grad = jnp.concatenate(results[9:])
    attention_grad, direction, left_term, right_term = to_full(
        jnp.concatenate([self_terms, cross_terms], 1)
    )
    inner_part = jnp.swapaxes(feed_both[0], 1, 2)
    outer_part = feed_both[1]
    gain_full = small[: gain_rows.size].reshape(gain_rows.shape)
    bias_full = small[gain_rows.size :].reshape(position_bias.shape)
    small_square = squares(gain_full) + squares(bias_full)

    grad_norm = jnp.sqrt(sums[2] + small_square)
    clip_factor = CLIP / jnp.maximum(grad_norm, CLIP)
    table_out = adamw(table, table_first, table_second, table_grad * clip_factor, RATE_TABLE)
    inner_out = adamw(inner_weight, inner_first, inner_second, inner_part * clip_factor, RATE_INNER)
    outer_out = adamw(outer_weight, outer_first, outer_second, outer_part * clip_factor, RATE_INNER)
    gain_out = adamw(gain_rows, gain_first, gain_second, gain_full * clip_factor, RATE_GAIN)
    bias_out = adamw(position_bias, bias_first, bias_second, bias_full * clip_factor, RATE_BIAS)
    clip_square = clip_factor * clip_factor
    left_new = BETA_STATS * left_stats + (1 - BETA_STATS) * clip_square * left_term
    right_new = BETA_STATS * right_stats + (1 - BETA_STATS) * clip_square * right_term
    spread = jnp.sqrt(sums[3:] / (D * D) + EPS)[:, None, None]
    attention_new = attention - RATE_ATTENTION * (direction / spread + DECAY * attention)
    return (
        sums[0],
        sums[1],
        grad_norm,
        *table_out,
        *inner_out,
        *outer_out,
        *gain_out,
        *bias_out,
        attention_grad * clip_factor,
        left_new,
        right_new,
        attention_new,
    )


def solution(mesh):
    in_specs = (
        P("dp", "section", None, None),
        P("dp", "section", None),
        P("dp", "section"),
        P(),
        P("section", None),
        P("section", None),
        P("section", None),
        P(None, None, "section"),
        P(None, None, "section"),
        P(None, None, "section"),
        P(None, "section", None),
        P(None, "section", None),
        P(None, "section", None),
        P(),
        P(),
        P(),
        P(),
        P(),
        P(),
        P(None, "section", None),
        P(None, "section", None),
        P(None, "section", None),
        P(None, "section", None),
        P(None, "section", None),
    )
    out_specs = (
        P(),
        P(),
        P(),
        P("section", None),
        P("section", None),
        P("section", None),
        P(None, None, "section"),
        P(None, None, "section"),
        P(None, None, "section"),
        P(None, "section", None),
        P(None, "section", None),
        P(None, "section", None),
        P(),
        P(),
        P(),
        P(),
        P(),
        P(),
        P(None, "section", None),
        P(None, "section", None),
        P(None, "section", None),
        P(None, "section", None),
    )
    return jax.shard_map(local, mesh=mesh, in_specs=in_specs, out_specs=out_specs, check_vma=False)
```

```python
import functools
import heapq
import math

import jax
import jax.numpy as jnp
from jax import lax
from jax.experimental import pallas as pl
from jax.experimental.pallas import tpu as pltpu
from jax.sharding import PartitionSpec as P

D = 768
HEADS = 12
DK = 64
MICRO = 2
STEP = 5
SPAN = 28
MATRICES = 4


EPS = 1e-06
CLIP = 1.0
BETA_ONE = 0.9
BETA_TWO = 0.95
BETA_STATS = 0.95
ADAM_EPS = 1e-08
DECAY = 0.01
RATE_TABLE = 0.5
RATE_INNER = 0.01
RATE_GAIN = 0.2
RATE_BIAS = 0.3
RATE_ATTENTION = 0.01
NEGATIVE = -1000000000.0
HIGH = lax.Precision.HIGHEST
VMEM_BYTES = 52 * 1024 * 1024
LOW = jnp.bfloat16
FULL = jnp.float32


def to_low(values):
    return values.astype(jnp.bfloat16)


def to_full(values):
    return values.astype(jnp.float32)


def pick(values, index, axis):
    return lax.dynamic_index_in_dim(values, index, axis, False)


def bit_count():
    return lax.axis_size("section").bit_length() - 1


def section_bit(bit):
    return (lax.axis_index("section") >> bit) & 1


def swap_bit(value, bit, planes=(0, 1)):
    pairs = [
        (2 * source + plane, 2 * (source ^ (1 << bit)) + plane)
        for source in range(lax.axis_size("section"))
        for plane in planes
    ]
    return lax.ppermute(value, ("section", "dp"), pairs)


def swap_half(value):
    return lax.ppermute(value, "dp", [(0, 1), (1, 0)])


def to_decoder(value):
    return lax.ppermute(value, "dp", [(0, 1)])


def to_encoder(value):
    return lax.ppermute(value, "dp", [(1, 0)])


def over(bit, planes=(0, 1)):
    return lambda value: swap_bit(value, bit, planes)


def link_cost(bit, value):
    return 4 + value.size * (6e-6 if bit == 0 else 6.5e-5 if bit < 3 else 1.1e-4)


def zero_after(value):
    mark = value[(0,) * value.ndim]
    return jnp.where(mark != mark, 1.0, 0.0)


def tied(value, *others):
    for other in others:
        value = value + zero_after(other).astype(value.dtype)
    return value


def interleave(tasks, after):
    results, free, pending, now, count = [None] * len(tasks), {}, [], 0.0, 0
    last = after

    def advance(index, arrived):
        nonlocal last, now, count
        posted = True
        while posted:
            try:
                link, cost, move, value = tasks[index].send(arrived)
            except StopIteration as stop:
                results[index] = stop.value
                return
            posted = cost < 0
            if posted:
                value, last = lax.optimization_barrier((value, last))
                free[link] = max(now, free.get(link, 0.0)) - cost
                arrived = move(value)
        count += 1
        if move is None:
            heapq.heappush(pending, (now + cost, count, index, None))
            return
        value, last = lax.optimization_barrier((value, last))
        if link == "core":
            now += cost
            free[link] = now
        else:
            now += 1.0
            free[link] = max(now, free.get(link, 0.0)) + cost
        heapq.heappush(pending, (free[link], count, index, move(value)))

    for index in range(len(tasks)):
        advance(index, None)
    while pending:
        ended, unused, index, arrived = heapq.heappop(pending)
        now = max(now, ended)
        if arrived is not None:
            now += 2.0 + 6e-6 * min(arrived.size, D * D)
            arrived, last = lax.optimization_barrier((arrived, last))
            last = arrived
        advance(index, arrived)
    return results


def halved(rows, layout, order, planes=(0, 1)):
    layout = list(layout)
    if isinstance(rows, tuple):
        part, kept = rows
        arrived = yield (0, link_cost(0, part), over(0, planes), part)
        rows = to_low(to_full(kept) + to_full(arrived))
    for bit in order:
        place = layout.index(bit)
        layout.remove(bit)
        split = rows.reshape(2**place, 2, -1, D)
        mine = section_bit(bit)
        part = to_low(pick(split, 1 - mine, 1)).reshape(-1, D)
        arrived = yield (bit, link_cost(bit, part), over(bit, planes), part)
        rows = to_low(to_full(pick(split, mine, 1).reshape(-1, D)) + to_full(arrived))
    return rows


def doubled(block, planes=(0, 1)):
    for stage, bit in enumerate(range(bit_count() - 1, 1, -1)):
        arrived = yield (bit, link_cost(bit, block), over(bit, planes), block)
        block = ordered(block, arrived, section_bit(bit), stage)
    return block.reshape(-1, D)


def to_rows(terms, planes=(0, 1)):
    first, second = section_bit(0), section_bit(1)
    part = pick(terms, 1 - first, 2)
    arrived = yield (0, link_cost(0, part), over(0, planes), part)
    terms = ordered(pick(terms, first, 2), arrived, first, 1)
    part = pick(terms, 1 - second, 2)
    arrived = yield (1, link_cost(1, part), over(1, planes), part)
    terms = ordered(pick(terms, second, 2), arrived, second, 2)
    return terms.reshape(terms.shape[0], MATRICES, -1, D)


def summed(values):
    for bit in range(bit_count()):
        arrived = yield (bit, 5, over(bit), values)
        values = values + arrived
    return values


def until(found, names):
    while not all(name in found for name in names):
        yield (None, 2, None, None)


def forward_mul(left, right):
    return jnp.dot(left, right, preferred_element_type=jnp.float32)


def offset_square(row, length):
    width = 2 * length
    padded = jnp.pad(row, (0, width - row.shape[0]))
    flat = jnp.tile(padded, length)[length - 1 : length - 1 + length * (width - 1)]
    return flat.reshape(length, width - 1)[:, :length]


def position_table(onehot, bias_layer):
    return jnp.einsum("qkb,bh->hqk", onehot.astype(jnp.float32), bias_layer, precision=HIGH)


def mul(left, right):
    return lax.dot_general(left, right, (((1,), (0,)), ((), ())), preferred_element_type=FULL)


def mul_right(left, right):
    return lax.dot_general(left, right, (((1,), (1,)), ((), ())), preferred_element_type=FULL)


def mul_left(left, right):
    return lax.dot_general(left, right, (((0,), (0,)), ((), ())), preferred_element_type=FULL)


def rms_scale(values):
    return lax.rsqrt(jnp.mean(values * values, -1, keepdims=True) + EPS)


def rms_back(values, gain_row, upstream):
    scale = rms_scale(values)
    normal = values * scale
    grad_gain = jnp.sum(upstream * normal, 0, keepdims=True)
    weighted = upstream * gain_row
    inner = jnp.mean(weighted * normal, -1, keepdims=True)
    return scale * (weighted - normal * inner), grad_gain


def gelu_parts(values):
    inner = math.sqrt(2.0 / math.pi) * (values + 0.044715 * values * values * values)
    bent = jnp.tanh(inner)
    slope = math.sqrt(2.0 / math.pi) * (1.0 + 3 * 0.044715 * values * values)
    value = 0.5 * values * (1.0 + bent)
    grad = 0.5 * (1.0 + bent) + 0.5 * values * (1.0 - bent * bent) * slope
    return value, grad


def params():
    return pltpu.CompilerParams(vmem_limit_bytes=VMEM_BYTES)


def whole():
    return pl.BlockSpec(memory_space=pltpu.VMEM)


def feed_forward_kernel(
    last_scale, rows_ref, gain_ref, last_ref, in_ref, out_ref, after_ref, head_ref, before_ref, norm_ref, total_ref
):
    step = pl.program_id(0)

    @pl.when(step == 0)
    def start():
        rows = rows_ref[...]
        norm_ref[...] = (rows * rms_scale(rows) * gain_ref[...]).astype(LOW)
        total_ref[...] = rows

    before = mul_right(norm_ref[...], in_ref[0])
    before_ref[...] = before
    active, unused = gelu_parts(before)
    total_ref[...] += mul(active.astype(LOW), out_ref[0])

    @pl.when(step == pl.num_programs(0) - 1)
    def finish():
        after = total_ref[...]
        after_ref[...] = after
        head_ref[...] = (after * rms_scale(after) * last_ref[...] * last_scale).astype(LOW)


def feed_forward(rows, gain_row, last_gain, weights, last_scale):
    count, hidden = rows.shape[0], weights.shape[1]
    chunk = D
    fixed = pl.BlockSpec((count, D), lambda j: (0, 0))
    row = pl.BlockSpec((1, D), lambda j: (0, 0))
    return pl.pallas_call(
        functools.partial(feed_forward_kernel, last_scale),
        grid=(hidden // chunk,),
        in_specs=[
            fixed,
            row,
            row,
            pl.BlockSpec((1, chunk, D), lambda j: (1, j, 0)),
            pl.BlockSpec((1, chunk, D), lambda j: (2, j, 0)),
        ],
        out_specs=[fixed, fixed, pl.BlockSpec((count, chunk), lambda j: (0, j))],
        out_shape=[
            jax.ShapeDtypeStruct((count, D), FULL),
            jax.ShapeDtypeStruct((count, D), LOW),
            jax.ShapeDtypeStruct((count, hidden), FULL),
        ],
        scratch_shapes=[pltpu.VMEM((count, D), LOW), pltpu.VMEM((count, D), FULL)],
        compiler_params=params(),
        name="feed_forward",
    )(rows, gain_row[None], last_gain[None], weights, weights)


def feed_backward_kernel(
    last_scale,
    mine_ref,
    upstream_ref,
    after_ref,
    last_ref,
    rows_ref,
    gain_ref,
    before_ref,
    in_ref,
    out_ref,
    grad_ref,
    sent_ref,
    kept_ref,
    gains_ref,
    resid_ref,
    low_ref,
    norm_ref,
    total_ref,
):
    step = pl.program_id(0)

    @pl.when(step == 0)
    def start():
        upstream = upstream_ref[...].astype(FULL) * last_scale
        resid, grad_last = rms_back(after_ref[...], last_ref[...], upstream)
        resid_ref[...] = resid
        low_ref[...] = resid.astype(LOW)
        rows = rows_ref[...]
        norm_ref[...] = (rows * rms_scale(rows) * gain_ref[...]).astype(LOW)
        total_ref[...] = jnp.zeros_like(total_ref)
        gains_ref[1:2] = grad_last

    grad_out = low_ref[...]
    active, slope = gelu_parts(before_ref[...])
    grad_before = (mul_right(grad_out, out_ref[0]) * slope).astype(LOW)
    total_ref[...] += mul(grad_before, in_ref[0])
    in_grad = mul_left(grad_before, norm_ref[...]).astype(LOW)
    out_grad = mul_left(active.astype(LOW), grad_out).astype(LOW)

    @pl.when(step < 2)
    def send():
        sent_ref[0] = in_grad
        sent_ref[1] = out_grad

    @pl.when(step >= 2)
    def keep():
        kept_ref[0] = in_grad
        kept_ref[1] = out_grad

    @pl.when(step == pl.num_programs(0) - 1)
    def finish():
        grad_rows, grad_gain = rms_back(rows_ref[...], gain_ref[...], total_ref[...])
        grad_ref[...] = resid_ref[...] + grad_rows
        gains_ref[0:1] = grad_gain


def feed_backward(upstream, after, last_gain, rows, gain_row, before, weights, last_scale):
    count, hidden = before.shape
    chunk = hidden // 4

    def place(step, mine):
        return 2 * ((step >= 2) == (mine[0] == 1)) + step % 2

    fixed = pl.BlockSpec((count, D), lambda j, mine: (0, 0))
    row = pl.BlockSpec((1, D), lambda j, mine: (0, 0))
    half = jax.ShapeDtypeStruct((2, hidden // 2, D), LOW)
    return pl.pallas_call(
        functools.partial(feed_backward_kernel, last_scale),
        grid_spec=pltpu.PrefetchScalarGridSpec(
            num_scalar_prefetch=1,
            grid=(4,),
            in_specs=[
                fixed,
                fixed,
                row,
                fixed,
                row,
                pl.BlockSpec((count, chunk), lambda j, mine: (0, place(j, mine))),
                pl.BlockSpec((1, chunk, D), lambda j, mine: (1, place(j, mine), 0)),
                pl.BlockSpec((1, chunk, D), lambda j, mine: (2, place(j, mine), 0)),
            ],
            out_specs=[
                fixed,
                pl.BlockSpec((2, chunk, D), lambda j, mine: (0, jnp.minimum(j, 1), 0)),
                pl.BlockSpec((2, chunk, D), lambda j, mine: (0, jnp.maximum(j - 2, 0), 0)),
                pl.BlockSpec((2, D), lambda j, mine: (0, 0)),
            ],
            scratch_shapes=[
                pltpu.VMEM((count, D), FULL),
                pltpu.VMEM((count, D), LOW),
                pltpu.VMEM((count, D), LOW),
                pltpu.VMEM((count, D), FULL),
            ],
        ),
        out_shape=[
            jax.ShapeDtypeStruct((count, D), FULL),
            half,
            half,
            jax.ShapeDtypeStruct((2, D), FULL),
        ],
        compiler_params=params(),
        name="feed_backward",
    )(section_bit(0)[None], upstream, after, last_gain[None], rows, gain_row[None], before, weights, weights)


def weight_spec(weights):
    slot, values = weights
    if slot is None:
        return pl.BlockSpec(memory_space=pltpu.VMEM)
    return pl.BlockSpec((1,) + values.shape[1:], lambda i: (slot, 0, 0))


def matrix_reader(ref, places):
    if places is None:
        return lambda m: ref[m]
    rows = D // len(places)
    return lambda m: jnp.concatenate(
        [ref[0, pl.ds((place * MATRICES + m) * rows, rows)] for place in places]
    )


def head_pairs(length):
    for sequence in range(MICRO):
        for pair in range(HEADS // 2):
            yield slice(sequence * length, (sequence + 1) * length), slice(
                pair * 2 * DK, (pair + 1) * 2 * DK
            ), pair


def both_heads(rows):
    left = lax.broadcasted_iota(jnp.int32, rows.shape, 1) < DK
    none = jnp.zeros_like(rows)
    return jnp.concatenate([jnp.where(left, rows, none), jnp.where(left, none, rows)])


def one_pair(rows):
    length = rows.shape[0] // 2
    left = lax.broadcasted_iota(jnp.int32, (length, rows.shape[1]), 1) < DK
    return jnp.where(left, rows[:length], rows[length:])


def probabilities(queries, keys_in, bias):
    scores = mul_right(queries, keys_in) * DK ** (-0.5)
    if bias is not None:
        scores = scores + bias
    raised = jnp.exp(scores - jnp.max(scores, -1, keepdims=True))
    return raised * (1.0 / jnp.sum(raised, -1, keepdims=True))


def attention_forward_kernel(biased, crossed, places, *refs):
    refs = list(refs)
    rows_ref, gain_ref, weight_ref = refs[:3]
    matrix = matrix_reader(weight_ref, places)
    source_ref = refs[3] if crossed else None
    bias_ref = refs[3 + crossed] if biased else None
    after_ref, norm_ref, query_ref, key_ref, value_ref, mixed_ref = refs[3 + crossed + biased :]
    rows = rows_ref[...]
    normed = (rows * rms_scale(rows) * gain_ref[...]).astype(LOW)
    norm_ref[...] = normed
    source = source_ref[...] if crossed else normed
    query_ref[...] = mul(normed, matrix(0)).astype(LOW)
    key_ref[...] = mul(source, matrix(1)).astype(LOW)
    value_ref[...] = mul(source, matrix(2)).astype(LOW)
    length = rows.shape[0] // MICRO
    for rows_at, columns, pair in head_pairs(length):
        queries = both_heads(query_ref[rows_at, columns])
        bias = bias_ref[2 * pair : 2 * pair + 2].reshape(2 * length, length) if biased else None
        probs = probabilities(queries, key_ref[rows_at, columns], bias)
        mixed = mul(probs.astype(LOW), value_ref[rows_at, columns])
        mixed_ref[rows_at, columns] = one_pair(mixed).astype(LOW)
    after_ref[...] = rows + mul(mixed_ref[...], matrix(3))


def attention_forward(rows, gain_row, weights, source, bias):
    crossed, biased = source is not None, bias is not None
    operands = [rows, gain_row[None], weights[1]]
    operands += [source] * crossed + [bias] * biased
    places = None if weights[0] is None else slot_places()
    low = jax.ShapeDtypeStruct(rows.shape, LOW)
    after, *kept = pl.pallas_call(
        functools.partial(attention_forward_kernel, biased, crossed, places),
        grid=(1,),
        in_specs=[whole()] * 2 + [weight_spec(weights)] + [whole()] * (len(operands) - 3),
        out_specs=[whole()] * 6,
        out_shape=[jax.ShapeDtypeStruct(rows.shape, FULL)] + [low] * 5,
        compiler_params=params(),
        name="attention_forward",
    )(*operands)
    return after, kept


def attention_backward_kernel(biased, crossed, places, mine_ref, *refs):
    refs = list(refs)
    grad_ref, rows_ref, gain_ref, weight_ref = refs[:4]
    matrix = matrix_reader(weight_ref, places)
    norm_ref, query_ref, key_ref, value_ref, mixed_ref = refs[4:9]
    source_ref = refs[9] if crossed else None
    bias_ref = refs[9 + crossed] if biased else None
    refs = refs[9 + crossed + biased :]
    result_ref, sent_ref, kept_ref, gain_grad_ref, extra_ref = refs[:5]
    grad_query_ref, grad_key_ref, grad_value_ref, grad_mixed_ref = refs[5:]
    mine = mine_ref[0]

    def put(m, value):
        @pl.when(mine == m // 2)
        def keep():
            kept_ref[pl.ds(m % 2 * D, D)] = value

        @pl.when(mine != m // 2)
        def send():
            sent_ref[pl.ds(m % 2 * D, D)] = value

    grad = grad_ref[...]
    grad_out = grad.astype(LOW)
    grad_mixed_ref[...] = mul_right(grad_out, matrix(3)).astype(LOW)
    put(3, mul_left(mixed_ref[...], grad_out).astype(LOW))
    length = grad.shape[0] // MICRO
    scale = DK ** (-0.5)
    for rows_at, columns, pair in head_pairs(length):
        queries, keys_in = both_heads(query_ref[rows_at, columns]), key_ref[rows_at, columns]
        grad_mixed = both_heads(grad_mixed_ref[rows_at, columns])
        bias = bias_ref[2 * pair : 2 * pair + 2].reshape(2 * length, length) if biased else None
        probs = probabilities(queries, keys_in, bias)
        grad_probs = mul_right(grad_mixed, value_ref[rows_at, columns])
        grad_scores = probs * (grad_probs - jnp.sum(probs * grad_probs, -1, keepdims=True))
        grad_scores = grad_scores.astype(LOW)
        if biased:
            score_rows = grad_scores.astype(FULL).reshape(2, length, length)
            if rows_at.start == 0:
                extra_ref[2 * pair : 2 * pair + 2] = score_rows
            else:
                extra_ref[2 * pair : 2 * pair + 2] += score_rows
        grad_query_ref[rows_at, columns] = (one_pair(mul(grad_scores, keys_in)) * scale).astype(LOW)
        grad_key_ref[rows_at, columns] = (mul_left(grad_scores, queries) * scale).astype(LOW)
        grad_value_ref[rows_at, columns] = mul_left(probs.astype(LOW), grad_mixed).astype(LOW)
    normed = norm_ref[...]
    source = source_ref[...] if crossed else normed
    put(0, mul_left(normed, grad_query_ref[...]).astype(LOW))
    put(1, mul_left(source, grad_key_ref[...]).astype(LOW))
    put(2, mul_left(source, grad_value_ref[...]).astype(LOW))
    grad_norm = mul_right(grad_query_ref[...], matrix(0))
    grad_source = mul_right(grad_key_ref[...], matrix(1))
    grad_source = grad_source + mul_right(grad_value_ref[...], matrix(2))
    if crossed:
        extra_ref[...] = grad_source.astype(LOW)
    else:
        grad_norm = grad_norm + grad_source
    grad_rows, grad_gain = rms_back(rows_ref[...], gain_ref[...], grad_norm)
    result_ref[...] = (grad + grad_rows).astype(result_ref.dtype)
    gain_grad_ref[...] = grad_gain


def attention_backward(grad, rows, gain_row, weights, kept, source, bias):
    crossed, biased = source is not None, bias is not None
    operands = [section_bit(0)[None], grad, rows, gain_row[None], weights[1], *kept]
    places = None if weights[0] is None else slot_places()
    half = jax.ShapeDtypeStruct((MATRICES // 2 * D, D), LOW)
    operands += [source] * crossed + [bias] * biased
    low = pltpu.VMEM(rows.shape, LOW)
    extra = jax.ShapeDtypeStruct(bias.shape, FULL) if biased else jax.ShapeDtypeStruct(rows.shape, LOW)
    return pl.pallas_call(
        functools.partial(attention_backward_kernel, biased, crossed, places),
        grid=(1,),
        in_specs=[pl.BlockSpec(memory_space=pltpu.SMEM)]
        + [whole()] * 3
        + [weight_spec(weights)]
        + [whole()] * (len(operands) - 5),
        out_specs=[whole()] * 5,
        out_shape=[
            jax.ShapeDtypeStruct(rows.shape, FULL if crossed else LOW),
            half,
            half,
            jax.ShapeDtypeStruct((1, D), FULL),
            extra,
        ],
        scratch_shapes=[low] * 4,
        compiler_params=params(),
        name="attention_backward",
    )(*operands)


def adamw(weight, first, second, gradient, rate):
    first = BETA_ONE * first + (1 - BETA_ONE) * gradient
    second = BETA_TWO * second + (1 - BETA_TWO) * gradient * gradient
    stepped = first / (1 - BETA_ONE**STEP) / (jnp.sqrt(second / (1 - BETA_TWO**STEP)) + ADAM_EPS)
    return (first, second, weight - rate * (stepped + DECAY * weight))


def ordered(own, other, mine, axis):
    return jnp.where(
        mine == 0, jnp.stack([own, other], axis), jnp.stack([other, own], axis)
    )


def low_bit_order():
    return sorted(range(lax.axis_size("section")), key=lambda section: (section & 1, section))


def slot_places():
    order = low_bit_order()
    return [order.index(section) for section in range(len(order))]


def slot_layout():
    return [1] + list(range(bit_count() - 1, 1, -1))


def shampoo_terms(low, full, left_block, right_full):
    rows = low.shape[0]
    start = (lax.axis_index("section") // MATRICES) * rows
    columns = lax.dynamic_slice_in_dim(full, start, rows, 1)
    blended = to_low(forward_mul(left_block, full))
    direction = forward_mul(blended, right_full)
    left_term = jnp.einsum("rd,ed->re", low, full, preferred_element_type=jnp.float32)
    right_term = jnp.einsum("dr,de->re", columns, full, preferred_element_type=jnp.float32)
    terms = jnp.stack([low, to_low(direction), to_low(left_term), to_low(right_term)])
    return terms.reshape(4, 2, 2, rows // 4, D)


def gather_small(values):
    values = ordered(values, swap_half(values), lax.axis_index("dp"), 0)[None]
    for bit in range(bit_count()):
        both = ordered(values, swap_bit(values, bit), section_bit(bit), 0)
        values = both.reshape((-1,) + values.shape[1:])
    return values


def lookup_rows(ids, shard_low):
    bits = bit_count()
    start = lax.axis_index("section") * shard_low.shape[0]
    mine = section_bit(0)

    def owned(some_ids):
        hit = some_ids.reshape(-1, 1) == jnp.arange(shard_low.shape[0])[None, :]
        return to_low(forward_mul(hit.astype(jnp.bfloat16), shard_low))

    split = (ids - start).reshape((2,) * bits + (MICRO, -1))
    split = jnp.moveaxis(split, bits, 0)
    sent, kept = pick(split, 1 - mine, bits), pick(split, mine, bits)
    arrived = swap_bit(owned(sent), 0)
    rows = (owned(kept) + arrived).reshape(MICRO, -1, D)
    layout = range(bits - 1, 0, -1)
    orders = [list(range(1, bits)), list(range(2, bits)) + [1]]
    chains = [halved(rows[micro], layout, orders[micro]) for micro in range(MICRO)]
    return jnp.concatenate(interleave(chains, arrived))


def local(
    token_ids,
    targets,
    objective,
    buckets,
    table,
    table_first,
    table_second,
    inner_weight,
    inner_first,
    inner_second,
    outer_weight,
    outer_first,
    outer_second,
    gain_rows,
    gain_first,
    gain_second,
    position_bias,
    bias_first,
    bias_second,
    attention,
    left_stats,
    right_stats,
    left_roots,
    right_inverse_roots,
):
    sections = lax.axis_size("section")
    section_index = lax.axis_index("section")
    half = lax.axis_index("dp")
    is_encoder = half == 0
    is_decoder = half == 1
    length = token_ids.shape[-1]
    vocab_rows = table.shape[0]
    bits = sections.bit_length() - 1

    packed = jnp.concatenate(
        [token_ids.reshape(-1), targets.reshape(-1), jnp.broadcast_to(objective.reshape(-1), (length,))]
    )
    every = gather_small(packed.reshape(-1, length)).reshape(sections, 2, -1).swapaxes(0, 1)
    every_tokens = every[:, :, : MICRO * length]
    every_targets = every[:, :, MICRO * length : (MICRO + 1) * length]
    every_objective = every[:, :, (MICRO + 1) * length]
    halves = sections // 2
    encoder_ids = every_tokens[:, :halves].reshape(sections, MICRO * length)
    decoder_ids = every_tokens[:, halves:].reshape(sections, MICRO * length)
    own_ids = jnp.where(is_encoder, encoder_ids, decoder_ids)

    def of_micro(values):
        return jnp.where(is_encoder, values[:, halves:], values[:, :halves])

    goal_ids = of_micro(every_targets).reshape(-1)
    goal_objective = of_micro(every_objective).reshape(sections)
    live_all = (
        jnp.arange(length)[None, :] < jnp.where(goal_objective == 1, length, SPAN)[:, None]
    ).astype(jnp.float32)
    live_rows = pick(live_all, section_index, 0)

    shard_low = to_low(table)
    attention_low = to_low(attention)
    shard_rows = attention.shape[1] * MATRICES
    self_shard = lax.dynamic_slice_in_dim(attention_low, half * MATRICES, MATRICES, 0)
    weight_shard = jnp.stack(
        [
            self_shard.reshape(shard_rows, D),
            to_low(pick(inner_weight, half, 0).T),
            to_low(pick(outer_weight, half, 0)),
            attention_low[8:12].reshape(shard_rows, D),
        ]
    )
    weights = lax.all_gather(
        weight_shard, "section", axis=1, tiled=True, axis_index_groups=[low_bit_order()]
    )
    def natural(slot):
        split = slot.reshape(2, sections // 2, MATRICES, -1, D)
        return jnp.transpose(split, (2, 1, 0, 3, 4)).reshape(MATRICES, D, D)

    if attention.shape[1] % 16 == 0:
        self_weights, cross_weights = (0, weights), (3, weights)
    else:
        self_weights, cross_weights = (None, natural(weights[0])), (None, natural(weights[3]))

    bucket_square = offset_square(pick(buckets, half, 0), length)
    bucket_range = jnp.arange(position_bias.shape[1])
    onehot = (bucket_square[:, :, None] == bucket_range).astype(jnp.bfloat16)
    bias_term = position_table(onehot, pick(position_bias, half, 0))
    allowed = is_encoder | (jnp.arange(length)[:, None] >= jnp.arange(length)[None, :])

    rows_in = to_full(lookup_rows(own_ids, shard_low))
    gain_self = gain_rows[jnp.where(is_encoder, 0, 3)]
    gain_feed = gain_rows[jnp.where(is_encoder, 1, 5)]
    bias_term = jnp.where(allowed, bias_term, NEGATIVE)
    resid, kept_self = attention_forward(rows_in, gain_self, self_weights, None, bias_term)

    def encoder_rest():
        return feed_forward(resid, gain_feed, gain_rows[2], weights, 1.0)

    first, second = section_bit(0), section_bit(1)
    root_rows = jnp.stack([left_roots, right_inverse_roots])
    own_roots = lax.dynamic_slice_in_dim(root_rows, half * MATRICES, MATRICES, 1)
    root_rows = jnp.stack([own_roots, root_rows[:, 8:12]]).reshape(4, 2, 2, -1, D)
    root_part = swap_bit(pick(root_rows, 1 - first, 1), 0)
    root_rows, resid, root_part = lax.optimization_barrier((root_rows, resid, root_part))
    root_rows = ordered(pick(root_rows, first, 1), root_part, first, 2)
    root_part = swap_bit(pick(root_rows, 1 - second, 1), 1)

    after_enc, encoded, before_enc = lax.cond(
        is_encoder, encoder_rest, lambda: jax.tree.map(jnp.zeros_like, encoder_rest())
    )
    encoded, root_part = lax.optimization_barrier((encoded, root_part))
    arrived = to_decoder(encoded)
    root_rows = ordered(pick(root_rows, second, 1), root_part, second, 1)
    root_rows = root_rows.reshape(2, 2, -1, D)
    root_lefts, root_rights = root_rows[:, 0], root_rows[:, 1]
    root_steps = list(range(bits - 1, 1, -1))

    def root_step(stage):
        return swap_bit(root_rights, root_steps[stage])

    def grown(stage, part):
        mine = section_bit(root_steps[stage])
        return ordered(root_rights, part, mine, 1 + stage)

    for stage in range(len(root_steps) - 2):
        root_rights = grown(stage, root_step(stage))
    root_part = root_step(len(root_steps) - 2)

    def decoder_rest(after, before):
        rows_feed, kept_cross = attention_forward(
            resid, gain_rows[4], cross_weights, arrived, None
        )
        after, final, before = feed_forward(
            rows_feed, gain_feed, gain_rows[6], weights, D ** (-0.5)
        )
        return (final, after, before, rows_feed, kept_cross)

    def decoder_skip(after, before):
        empty = jnp.zeros(resid.shape, jnp.bfloat16)
        return (empty, after, before, resid, [empty] * 5)

    final_low, after_feed, before_feed, rows_feed, kept_cross = lax.cond(
        is_decoder, decoder_rest, decoder_skip, after_enc, before_enc
    )

    final_low, root_part = lax.optimization_barrier((final_low, root_part))
    root_rights = grown(len(root_steps) - 2, root_part)

    final_split = final_low.reshape(MICRO, length, D)
    handed = to_encoder(final_split[0])
    own_rows = jnp.where(is_encoder, handed, final_split[1])
    head_low = own_rows * live_rows[:, None].astype(jnp.bfloat16)
    all_rows = lax.all_gather(head_low, "section", axis=0, tiled=True)
    logits = jnp.einsum("nd,vd->nv", all_rows, shard_low, preferred_element_type=jnp.float32)
    goal_hit = (goal_ids - section_index * vocab_rows)[:, None] == jnp.arange(vocab_rows)[None, :]
    row_peak = jnp.max(logits, -1)
    row_total = jnp.sum(jnp.exp(logits - row_peak[:, None]), -1)
    goal_logit = jnp.sum(jnp.where(goal_hit, logits, 0.0), -1)
    every_stat = lax.all_gather(jnp.stack([row_peak, row_total]), "section")
    top_peak = jnp.max(every_stat[:, 0], 0)
    log_total = top_peak + jnp.log(
        jnp.sum(every_stat[:, 1] * jnp.exp(every_stat[:, 0] - top_peak), 0)
    )
    grad_logits = to_low(jnp.exp(logits - log_total[:, None]) - goal_hit.astype(jnp.float32))
    grad_all = forward_mul(grad_logits, shard_low)
    def head_table_task():
        yield (None, 14, None, None)
        product = lambda grads: mul_left(grads, all_rows)
        return (yield ("core", 10, product, grad_logits))

    chain = halved(grad_all, range(bits - 1, -1, -1), range(bits))
    grad_head, head_table = interleave([chain, head_table_task()], log_total)
    grad_head = to_full(grad_head)
    grad_head = to_low(grad_head * live_rows[:, None])
    own_live = lax.dynamic_slice_in_dim(log_total, section_index * length, length, 0)
    loss_part = jnp.sum(live_rows * own_live) - jnp.sum(live_all.reshape(-1) * goal_logit)
    count_part = jnp.sum(live_rows)
    grad_final = jnp.stack([to_decoder(grad_head), grad_head]).reshape(MICRO * length, D)

    def decoder_back():
        grad_rows, *feed_grads, gains = feed_backward(
            grad_final,
            after_feed,
            gain_rows[6],
            rows_feed,
            gain_feed,
            before_feed,
            weights,
            D ** (-0.5),
        )
        grad_rows, *cross_grads, gain_cross, grad_source = attention_backward(
            grad_rows, resid, gain_rows[4], cross_weights, kept_cross, arrived, None
        )
        gains = jnp.concatenate([gain_cross, gains])
        return (grad_source, grad_rows, feed_grads, cross_grads, gains)

    root_rights, grad_final = lax.optimization_barrier((root_rights, grad_final))
    root_part = root_step(len(root_steps) - 1)
    grad_source, grad_dec, feed_dec, cross_grads, gains_dec = lax.cond(
        is_decoder, decoder_back, lambda: jax.tree.map(jnp.zeros_like, decoder_back())
    )
    back_source = to_encoder(grad_source)

    back_source, feed_dec, cross_grads, root_part = lax.optimization_barrier(
        (back_source, feed_dec, cross_grads, root_part)
    )
    root_rights = grown(len(root_steps) - 1, root_part).reshape(2, D, D)

    late = to_low(to_full(cross_grads[1]) + to_full(swap_bit(cross_grads[0], 0, (1,))))
    late_split = late.reshape(2, -1, D)
    late_part, back_source, grad_dec = lax.optimization_barrier(
        (pick(late_split, 1 - second, 0), back_source, grad_dec)
    )
    late_arrived = swap_bit(late_part, 1, (1,))

    def self_back(grad_rows):
        return attention_backward(
            grad_rows, rows_in, gain_self, self_weights, kept_self, None, bias_term
        )

    def encoder_feed():
        grad_rows, *feed_grads, gains = feed_backward(
            back_source,
            after_feed,
            gain_rows[2],
            resid,
            gain_feed,
            before_feed,
            weights,
            1.0,
        )
        empty = jnp.zeros((MATRICES // 2 * D, D), jnp.bfloat16)
        score = jnp.zeros(bias_term.shape, jnp.float32)
        return (grad_rows, gains, score, [empty, empty], feed_grads)

    def decoder_self():
        embed_low, *self_grads, gain_grad, score_grad = self_back(grad_dec)
        gains = jnp.concatenate([gain_grad, gain_grad])
        return (to_full(embed_low), gains, score_grad, self_grads, feed_dec)

    grad_rows, gains_middle, score_middle, self_middle, feed_grads = lax.cond(
        is_encoder, encoder_feed, decoder_self
    )
    grad_rows, self_middle, feed_grads, late_arrived = lax.optimization_barrier(
        (grad_rows, self_middle, feed_grads, late_arrived)
    )
    late = to_low(to_full(pick(late_split, second, 0)) + to_full(late_arrived))
    third = section_bit(2)
    late_split = late.reshape(2 ** (bits - 3), 2, -1, D)
    late_part, grad_rows = lax.optimization_barrier(
        (pick(late_split, 1 - third, 1).reshape(-1, D), grad_rows)
    )
    late_arrived = swap_bit(late_part, 2, (1,))

    feed_arrived = swap_bit(feed_grads[0], 0)

    def encoder_self():
        embed_low, *self_grads, gain_grad, score_grad = self_back(grad_rows)
        gains = jnp.concatenate([gain_grad, gains_middle, jnp.zeros((4, D), jnp.float32)])
        return (embed_low, gains, score_grad, self_grads)

    def decoder_skip_self():
        gains = jnp.concatenate([jnp.zeros((3, D), jnp.float32), gains_middle[:1], gains_dec])
        return (to_low(grad_rows), gains, score_middle, self_middle)

    embed_low, gain_part, score_grad, self_grads = lax.cond(
        is_encoder, encoder_self, decoder_skip_self
    )
    embed_low, self_grads, late_arrived, feed_arrived = lax.optimization_barrier(
        (embed_low, self_grads, late_arrived, feed_arrived)
    )
    feed_half = to_low(to_full(feed_grads[1]) + to_full(feed_arrived))
    late = pick(late_split, third, 1).reshape(-1, D)
    late = to_low(to_full(late) + to_full(late_arrived))

    found = {}
    own_local = (own_ids.reshape(-1) - section_index * vocab_rows)[None, :]

    def squares(values):
        return jnp.sum(to_full(values) * to_full(values))

    def rows_task():
        every_rows = yield ("gather", 80, lambda rows: lax.all_gather(rows, "section"), embed_low)
        found["rows"] = every_rows.reshape(-1, D)

    def feed_task():
        yield (None, 10, None, None)
        layout = ["matrix"] + list(range(bits - 1, 0, -1))
        own = yield from halved(feed_half.reshape(-1, D), layout, range(1, bits))
        own = own.reshape(2, -1, D)
        found["feed_square"] = squares(own)
        found["feed"] = own
        return own, (yield ("dp", -15, swap_half, own))

    block_rows = -(-vocab_rows // 16) * 8
    shared = 2 * block_rows - vocab_rows
    starts = [0, vocab_rows - block_rows]

    def table_task():
        yield from until(found, ["rows"])
        own_start, other_start = jnp.where(is_encoder, jnp.array(starts), jnp.array(starts[::-1]))

        def product(start):
            def rows_of(rows):
                hit = own_local == start + jnp.arange(block_rows)[:, None]
                head = lax.dynamic_slice_in_dim(head_table, start, block_rows, 0)
                return to_low(mul(hit.astype(jnp.bfloat16), rows) + head)

            return rows_of

        sent = yield ("core", 10, product(other_start), found["rows"])
        found["table_sent"] = sent
        arrived = yield ("dp", -36, swap_half, sent)
        own = yield ("core", 10, product(own_start), found["rows"])
        yield (None, 30, None, None)
        own = to_low(to_full(own) + to_full(arrived))
        counted = is_encoder | (jnp.arange(block_rows) >= shared)
        found["table_square"] = squares(jnp.where(counted[:, None], own, jnp.zeros_like(own)))
        other = yield ("dp", -36, swap_half, own)
        return jnp.concatenate(
            [jnp.where(is_encoder, own, other), jnp.where(is_encoder, other, own)[shared:]]
        )

    def cross_task():
        layout = [bit for bit in slot_layout()[1:] if bit > 2]
        block = yield from halved(late, layout, range(3, bits), (1,))
        found["cross_square"] = squares(block)
        full = yield from doubled(block, (1,))
        terms = shampoo_terms(block, full, root_lefts[1], root_rights[1])
        found["cross_direction"] = squares(terms[1])
        terms = yield from to_rows(terms, (1,))
        yield from until(found, ["feed"])
        other = yield ("dp", -30, to_encoder, tied(terms, found["feed"]))
        return terms, other

    def self_task():
        block = yield from halved(tuple(self_grads), slot_layout(), range(1, bits))
        found["self_square"] = squares(block)
        yield from until(found, ["table_sent"])
        full = yield from doubled(tied(block, found["table_sent"]))
        terms = shampoo_terms(block, full, root_lefts[0], root_rights[0])
        found["self_direction"] = squares(terms[1])
        terms = yield from to_rows(terms)
        yield from until(found, ["feed"])
        other = yield ("dp", -30, swap_half, tied(terms, found["feed"]))
        return terms, other

    def small_task():
        yield (None, 25, None, None)

        def of_buckets(values):
            return jnp.einsum(
                "hqk,qkb->bh", values, onehot.astype(jnp.float32), precision=HIGH
            ).reshape(1, -1)

        bias_grad = yield ("core", 6, of_buckets, score_grad)
        rows = [jnp.where(half == layer, bias_grad, 0.0) for layer in range(2)]
        rows = jnp.concatenate(rows, 1).reshape(-1, D)
        found["small"] = yield from summed(jnp.concatenate([gain_part, rows]))

    def norm_task():
        yield from until(
            found, ["self_square", "cross_square", "small", "feed_square", "table_square"]
        )
        square_sum = found["self_square"] + is_decoder.astype(jnp.float32) * found["cross_square"]
        square_sum = square_sum + found["feed_square"] + found["table_square"]
        sums = jnp.stack([loss_part, count_part, square_sum])
        sums = yield from summed(jnp.pad(sums, (0, D - sums.shape[0])).reshape(1, D))
        sums = jnp.concatenate([found["small"], sums])
        return sums, (yield ("dp", -5, swap_half, sums))

    def direction_task():
        yield from until(found, ["self_direction", "cross_direction"])
        matrix = 2 * section_bit(0) + section_bit(1)
        names = jnp.arange(3 * MATRICES)
        own_matrix, cross_matrix = half * MATRICES + matrix, 2 * MATRICES + matrix
        sums = jnp.where(names == own_matrix, found["self_direction"], 0.0)
        sums = sums + jnp.where(
            names == cross_matrix, is_decoder * found["cross_direction"], 0.0
        )
        sums = yield from summed(jnp.pad(sums, (0, 128 - sums.shape[0])).reshape(1, 128))
        return sums, (yield ("dp", -5, swap_half, sums))

    tasks = [rows_task(), self_task(), cross_task(), table_task(), feed_task()]
    tasks += [small_task(), norm_task(), direction_task()]
    results = interleave(tasks, embed_low)
    self_terms, cross_terms, table_grad, feed_both = results[1:5]
    norm_sums, directions = results[6:]
    norm_sums = norm_sums[0] + norm_sums[1]
    small, sums = norm_sums[:-1], norm_sums[-1]
    directions = (directions[0] + directions[1])[0, : 3 * MATRICES]
    table_grad = to_full(table_grad)
    gain_full = small[: gain_rows.shape[0]]
    bias_full = small[gain_rows.shape[0] :].reshape(position_bias.shape)
    small_square = squares(gain_full) + squares(bias_full)

    grad_norm = jnp.sqrt(sums[2] + small_square)
    clip_factor = CLIP / jnp.maximum(grad_norm, CLIP)
    table_out = adamw(table, table_first, table_second, table_grad * clip_factor, RATE_TABLE)
    feed_both = to_full(ordered(*feed_both, half, 1))
    inner_part = jnp.swapaxes(feed_both[0], 1, 2)
    outer_part = feed_both[1]
    inner_out = adamw(inner_weight, inner_first, inner_second, inner_part * clip_factor, RATE_INNER)
    outer_out = adamw(outer_weight, outer_first, outer_second, outer_part * clip_factor, RATE_INNER)
    table_out, self_terms, cross_terms = lax.optimization_barrier(
        (table_out, self_terms, cross_terms)
    )
    terms = jnp.concatenate(
        [
            ordered(*self_terms, half, 1).reshape(4, 2 * MATRICES, -1, D),
            jnp.where(is_encoder, cross_terms[1], cross_terms[0]),
        ],
        1,
    )
    attention_grad, direction, left_term, right_term = to_full(terms)
    gain_out = adamw(gain_rows, gain_first, gain_second, gain_full * clip_factor, RATE_GAIN)
    bias_out = adamw(position_bias, bias_first, bias_second, bias_full * clip_factor, RATE_BIAS)
    clip_square = clip_factor * clip_factor
    left_new = BETA_STATS * left_stats + (1 - BETA_STATS) * clip_square * left_term
    right_new = BETA_STATS * right_stats + (1 - BETA_STATS) * clip_square * right_term
    spread = jnp.sqrt(directions / (D * D) + EPS)[:, None, None]
    attention_new = attention - RATE_ATTENTION * (direction / spread + DECAY * attention)
    return (
        sums[0],
        sums[1],
        grad_norm,
        *table_out,
        *inner_out,
        *outer_out,
        *gain_out,
        *bias_out,
        attention_grad * clip_factor,
        left_new,
        right_new,
        attention_new,
    )


def solution(mesh):
    in_specs = (
        P("dp", "section", None, None),
        P("dp", "section", None),
        P("dp", "section"),
        P(),
        P("section", None),
        P("section", None),
        P("section", None),
        P(None, None, "section"),
        P(None, None, "section"),
        P(None, None, "section"),
        P(None, "section", None),
        P(None, "section", None),
        P(None, "section", None),
        P(),
        P(),
        P(),
        P(),
        P(),
        P(),
        P(None, "section", None),
        P(None, "section", None),
        P(None, "section", None),
        P(None, "section", None),
        P(None, "section", None),
    )
    out_specs = (
        P(),
        P(),
        P(),
        P("section", None),
        P("section", None),
        P("section", None),
        P(None, None, "section"),
        P(None, None, "section"),
        P(None, None, "section"),
        P(None, "section", None),
        P(None, "section", None),
        P(None, "section", None),
        P(),
        P(),
        P(),
        P(),
        P(),
        P(),
        P(None, "section", None),
        P(None, "section", None),
        P(None, "section", None),
        P(None, "section", None),
    )
    return jax.shard_map(local, mesh=mesh, in_specs=in_specs, out_specs=out_specs, check_vma=False)
```

```python
import functools
import heapq
import math

import jax
import jax.numpy as jnp
from jax import lax
from jax.experimental import pallas as pl
from jax.experimental.pallas import tpu as pltpu
from jax.sharding import PartitionSpec as P

D = 768
HEADS = 12
DK = 64
MICRO = 2
STEP = 5
SPAN = 28
MATRICES = 4


EPS = 1e-06
CLIP = 1.0
BETA_ONE = 0.9
BETA_TWO = 0.95
BETA_STATS = 0.95
ADAM_EPS = 1e-08
DECAY = 0.01
RATE_TABLE = 0.5
RATE_INNER = 0.01
RATE_GAIN = 0.2
RATE_BIAS = 0.3
RATE_ATTENTION = 0.01
NEGATIVE = -1000000000.0
HIGH = lax.Precision.HIGHEST
VMEM_BYTES = 52 * 1024 * 1024
LOW = jnp.bfloat16
FULL = jnp.float32


def to_low(values):
    return values.astype(jnp.bfloat16)


def to_full(values):
    return values.astype(jnp.float32)


def pick(values, index, axis):
    return lax.dynamic_index_in_dim(values, index, axis, False)


def bit_count():
    return lax.axis_size("section").bit_length() - 1


def section_bit(bit):
    return (lax.axis_index("section") >> bit) & 1


def swap_bit(value, bit, planes=(0, 1)):
    pairs = [
        (2 * source + plane, 2 * (source ^ (1 << bit)) + plane)
        for source in range(lax.axis_size("section"))
        for plane in planes
    ]
    return lax.ppermute(value, ("section", "dp"), pairs)


def swap_half(value):
    return lax.ppermute(value, "dp", [(0, 1), (1, 0)])


def to_decoder(value):
    return lax.ppermute(value, "dp", [(0, 1)])


def to_encoder(value):
    return lax.ppermute(value, "dp", [(1, 0)])


def over(bit, planes=(0, 1)):
    return lambda value: swap_bit(value, bit, planes)


def link_cost(bit, value):
    return 4 + value.size * (6e-6 if bit == 0 else 6.5e-5 if bit < 3 else 1.1e-4)


def zero_after(value):
    mark = value[(0,) * value.ndim]
    return jnp.where(mark != mark, 1.0, 0.0)


def tied(value, *others):
    for other in others:
        value = value + zero_after(other).astype(value.dtype)
    return value


def interleave(tasks, after):
    results, free, pending, now, count = [None] * len(tasks), {}, [], 0.0, 0
    last = after

    def advance(index, arrived):
        nonlocal last, now, count
        posted = True
        while posted:
            try:
                link, cost, move, value = tasks[index].send(arrived)
            except StopIteration as stop:
                results[index] = stop.value
                return
            posted = cost < 0
            if posted:
                value, last = lax.optimization_barrier((value, last))
                free[link] = max(now, free.get(link, 0.0)) - cost
                arrived = move(value)
        count += 1
        if move is None:
            heapq.heappush(pending, (now + cost, count, index, None))
            return
        value, last = lax.optimization_barrier((value, last))
        if link == "core":
            now += cost
            free[link] = now
        else:
            now += 1.0
            free[link] = max(now, free.get(link, 0.0)) + cost
        heapq.heappush(pending, (free[link], count, index, move(value)))

    for index in range(len(tasks)):
        advance(index, None)
    while pending:
        ended, unused, index, arrived = heapq.heappop(pending)
        now = max(now, ended)
        if arrived is not None:
            now += 2.0 + 6e-6 * min(arrived.size, D * D)
            arrived, last = lax.optimization_barrier((arrived, last))
            last = arrived
        advance(index, arrived)
    return results


def halved(rows, layout, order, planes=(0, 1)):
    layout = list(layout)
    if isinstance(rows, tuple):
        part, kept = rows
        arrived = yield (0, link_cost(0, part), over(0, planes), part)
        rows = to_low(to_full(kept) + to_full(arrived))
    for bit in order:
        place = layout.index(bit)
        layout.remove(bit)
        split = rows.reshape(2**place, 2, -1, D)
        mine = section_bit(bit)
        part = to_low(pick(split, 1 - mine, 1)).reshape(-1, D)
        arrived = yield (bit, link_cost(bit, part), over(bit, planes), part)
        rows = to_low(to_full(pick(split, mine, 1).reshape(-1, D)) + to_full(arrived))
    return rows


def doubled(block, planes=(0, 1)):
    for stage, bit in enumerate(range(bit_count() - 1, 1, -1)):
        arrived = yield (bit, link_cost(bit, block), over(bit, planes), block)
        block = ordered(block, arrived, section_bit(bit), stage)
    return block.reshape(-1, D)


def to_rows(terms, planes=(0, 1)):
    first, second = section_bit(0), section_bit(1)
    part = pick(terms, 1 - first, 2)
    arrived = yield (0, link_cost(0, part), over(0, planes), part)
    terms = ordered(pick(terms, first, 2), arrived, first, 1)
    part = pick(terms, 1 - second, 2)
    arrived = yield (1, link_cost(1, part), over(1, planes), part)
    terms = ordered(pick(terms, second, 2), arrived, second, 2)
    return terms.reshape(terms.shape[0], MATRICES, -1, D)


def summed(values):
    for bit in range(bit_count()):
        arrived = yield (bit, 5, over(bit), values)
        values = values + arrived
    return values


def until(found, names):
    while not all(name in found for name in names):
        yield (None, 2, None, None)


def forward_mul(left, right):
    return jnp.dot(left, right, preferred_element_type=jnp.float32)


def offset_square(row, length):
    width = 2 * length
    padded = jnp.pad(row, (0, width - row.shape[0]))
    flat = jnp.tile(padded, length)[length - 1 : length - 1 + length * (width - 1)]
    return flat.reshape(length, width - 1)[:, :length]


def position_table(onehot, bias_layer):
    return jnp.einsum("qkb,bh->hqk", onehot.astype(jnp.float32), bias_layer, precision=HIGH)


def mul(left, right):
    return lax.dot_general(left, right, (((1,), (0,)), ((), ())), preferred_element_type=FULL)


def mul_right(left, right):
    return lax.dot_general(left, right, (((1,), (1,)), ((), ())), preferred_element_type=FULL)


def mul_left(left, right):
    return lax.dot_general(left, right, (((0,), (0,)), ((), ())), preferred_element_type=FULL)


def rms_scale(values):
    return lax.rsqrt(jnp.mean(values * values, -1, keepdims=True) + EPS)


def rms_back(values, gain_row, upstream):
    scale = rms_scale(values)
    normal = values * scale
    grad_gain = jnp.sum(upstream * normal, 0, keepdims=True)
    weighted = upstream * gain_row
    inner = jnp.mean(weighted * normal, -1, keepdims=True)
    return scale * (weighted - normal * inner), grad_gain


def gelu_parts(values):
    inner = math.sqrt(2.0 / math.pi) * (values + 0.044715 * values * values * values)
    bent = jnp.tanh(inner)
    slope = math.sqrt(2.0 / math.pi) * (1.0 + 3 * 0.044715 * values * values)
    value = 0.5 * values * (1.0 + bent)
    grad = 0.5 * (1.0 + bent) + 0.5 * values * (1.0 - bent * bent) * slope
    return value, grad


def params():
    return pltpu.CompilerParams(vmem_limit_bytes=VMEM_BYTES)


def whole():
    return pl.BlockSpec(memory_space=pltpu.VMEM)


def feed_forward_kernel(
    last_scale, rows_ref, gain_ref, last_ref, in_ref, out_ref, after_ref, head_ref, before_ref, norm_ref, total_ref
):
    step = pl.program_id(0)

    @pl.when(step == 0)
    def start():
        rows = rows_ref[...]
        norm_ref[...] = (rows * rms_scale(rows) * gain_ref[...]).astype(LOW)
        total_ref[...] = rows

    before = mul_right(norm_ref[...], in_ref[0])
    before_ref[...] = before
    active, unused = gelu_parts(before)
    total_ref[...] += mul(active.astype(LOW), out_ref[0])

    @pl.when(step == pl.num_programs(0) - 1)
    def finish():
        after = total_ref[...]
        after_ref[...] = after
        head_ref[...] = (after * rms_scale(after) * last_ref[...] * last_scale).astype(LOW)


def feed_forward(rows, gain_row, last_gain, weights, last_scale):
    count, hidden = rows.shape[0], weights.shape[1]
    chunk = D
    fixed = pl.BlockSpec((count, D), lambda j: (0, 0))
    row = pl.BlockSpec((1, D), lambda j: (0, 0))
    return pl.pallas_call(
        functools.partial(feed_forward_kernel, last_scale),
        grid=(hidden // chunk,),
        in_specs=[
            fixed,
            row,
            row,
            pl.BlockSpec((1, chunk, D), lambda j: (1, j, 0)),
            pl.BlockSpec((1, chunk, D), lambda j: (2, j, 0)),
        ],
        out_specs=[fixed, fixed, pl.BlockSpec((count, chunk), lambda j: (0, j))],
        out_shape=[
            jax.ShapeDtypeStruct((count, D), FULL),
            jax.ShapeDtypeStruct((count, D), LOW),
            jax.ShapeDtypeStruct((count, hidden), FULL),
        ],
        scratch_shapes=[pltpu.VMEM((count, D), LOW), pltpu.VMEM((count, D), FULL)],
        compiler_params=params(),
        name="feed_forward",
    )(rows, gain_row[None], last_gain[None], weights, weights)


def feed_backward_kernel(
    last_scale,
    mine_ref,
    upstream_ref,
    after_ref,
    last_ref,
    rows_ref,
    gain_ref,
    before_ref,
    in_ref,
    out_ref,
    grad_ref,
    sent_ref,
    kept_ref,
    gains_ref,
    resid_ref,
    low_ref,
    norm_ref,
    total_ref,
):
    step = pl.program_id(0)

    @pl.when(step == 0)
    def start():
        upstream = upstream_ref[...].astype(FULL) * last_scale
        resid, grad_last = rms_back(after_ref[...], last_ref[...], upstream)
        resid_ref[...] = resid
        low_ref[...] = resid.astype(LOW)
        rows = rows_ref[...]
        norm_ref[...] = (rows * rms_scale(rows) * gain_ref[...]).astype(LOW)
        total_ref[...] = jnp.zeros_like(total_ref)
        gains_ref[1:2] = grad_last

    grad_out = low_ref[...]
    active, slope = gelu_parts(before_ref[...])
    grad_before = (mul_right(grad_out, out_ref[0]) * slope).astype(LOW)
    total_ref[...] += mul(grad_before, in_ref[0])
    in_grad = mul_left(grad_before, norm_ref[...]).astype(LOW)
    out_grad = mul_left(active.astype(LOW), grad_out).astype(LOW)

    @pl.when(step < 2)
    def send():
        sent_ref[0] = in_grad
        sent_ref[1] = out_grad

    @pl.when(step >= 2)
    def keep():
        kept_ref[0] = in_grad
        kept_ref[1] = out_grad

    @pl.when(step == pl.num_programs(0) - 1)
    def finish():
        grad_rows, grad_gain = rms_back(rows_ref[...], gain_ref[...], total_ref[...])
        grad_ref[...] = resid_ref[...] + grad_rows
        gains_ref[0:1] = grad_gain


def feed_backward(upstream, after, last_gain, rows, gain_row, before, weights, last_scale):
    count, hidden = before.shape
    chunk = hidden // 4

    def place(step, mine):
        return 2 * ((step >= 2) == (mine[0] == 1)) + step % 2

    fixed = pl.BlockSpec((count, D), lambda j, mine: (0, 0))
    row = pl.BlockSpec((1, D), lambda j, mine: (0, 0))
    half = jax.ShapeDtypeStruct((2, hidden // 2, D), LOW)
    return pl.pallas_call(
        functools.partial(feed_backward_kernel, last_scale),
        grid_spec=pltpu.PrefetchScalarGridSpec(
            num_scalar_prefetch=1,
            grid=(4,),
            in_specs=[
                fixed,
                fixed,
                row,
                fixed,
                row,
                pl.BlockSpec((count, chunk), lambda j, mine: (0, place(j, mine))),
                pl.BlockSpec((1, chunk, D), lambda j, mine: (1, place(j, mine), 0)),
                pl.BlockSpec((1, chunk, D), lambda j, mine: (2, place(j, mine), 0)),
            ],
            out_specs=[
                fixed,
                pl.BlockSpec((2, chunk, D), lambda j, mine: (0, jnp.minimum(j, 1), 0)),
                pl.BlockSpec((2, chunk, D), lambda j, mine: (0, jnp.maximum(j - 2, 0), 0)),
                pl.BlockSpec((2, D), lambda j, mine: (0, 0)),
            ],
            scratch_shapes=[
                pltpu.VMEM((count, D), FULL),
                pltpu.VMEM((count, D), LOW),
                pltpu.VMEM((count, D), LOW),
                pltpu.VMEM((count, D), FULL),
            ],
        ),
        out_shape=[
            jax.ShapeDtypeStruct((count, D), FULL),
            half,
            half,
            jax.ShapeDtypeStruct((2, D), FULL),
        ],
        compiler_params=params(),
        name="feed_backward",
    )(section_bit(0)[None], upstream, after, last_gain[None], rows, gain_row[None], before, weights, weights)


def weight_spec(weights):
    slot, values = weights
    if slot is None:
        return pl.BlockSpec(memory_space=pltpu.VMEM)
    return pl.BlockSpec((1,) + values.shape[1:], lambda i: (slot, 0, 0))


def matrix_reader(ref, places):
    if places is None:
        return lambda m: ref[m]
    rows = D // len(places)
    return lambda m: jnp.concatenate(
        [ref[0, pl.ds((place * MATRICES + m) * rows, rows)] for place in places]
    )


def head_pairs(length):
    for sequence in range(MICRO):
        for pair in range(HEADS // 2):
            yield slice(sequence * length, (sequence + 1) * length), slice(
                pair * 2 * DK, (pair + 1) * 2 * DK
            ), pair


def both_heads(rows):
    left = lax.broadcasted_iota(jnp.int32, rows.shape, 1) < DK
    none = jnp.zeros_like(rows)
    return jnp.concatenate([jnp.where(left, rows, none), jnp.where(left, none, rows)])


def one_pair(rows):
    length = rows.shape[0] // 2
    left = lax.broadcasted_iota(jnp.int32, (length, rows.shape[1]), 1) < DK
    return jnp.where(left, rows[:length], rows[length:])


def probabilities(queries, keys_in, bias):
    scores = mul_right(queries, keys_in) * DK ** (-0.5)
    if bias is not None:
        scores = scores + bias
    raised = jnp.exp(scores - jnp.max(scores, -1, keepdims=True))
    return raised * (1.0 / jnp.sum(raised, -1, keepdims=True))


def attention_forward_kernel(biased, crossed, places, *refs):
    refs = list(refs)
    rows_ref, gain_ref, weight_ref = refs[:3]
    matrix = matrix_reader(weight_ref, places)
    source_ref = refs[3] if crossed else None
    bias_ref = refs[3 + crossed] if biased else None
    after_ref, norm_ref, query_ref, key_ref, value_ref, mixed_ref = refs[3 + crossed + biased :]
    rows = rows_ref[...]
    normed = (rows * rms_scale(rows) * gain_ref[...]).astype(LOW)
    norm_ref[...] = normed
    source = source_ref[...] if crossed else normed
    query_ref[...] = mul(normed, matrix(0)).astype(LOW)
    key_ref[...] = mul(source, matrix(1)).astype(LOW)
    value_ref[...] = mul(source, matrix(2)).astype(LOW)
    length = rows.shape[0] // MICRO
    for rows_at, columns, pair in head_pairs(length):
        queries = both_heads(query_ref[rows_at, columns])
        bias = bias_ref[2 * pair : 2 * pair + 2].reshape(2 * length, length) if biased else None
        probs = probabilities(queries, key_ref[rows_at, columns], bias)
        mixed = mul(probs.astype(LOW), value_ref[rows_at, columns])
        mixed_ref[rows_at, columns] = one_pair(mixed).astype(LOW)
    after_ref[...] = rows + mul(mixed_ref[...], matrix(3))


def attention_forward(rows, gain_row, weights, source, bias):
    crossed, biased = source is not None, bias is not None
    operands = [rows, gain_row[None], weights[1]]
    operands += [source] * crossed + [bias] * biased
    places = None if weights[0] is None else slot_places()
    low = jax.ShapeDtypeStruct(rows.shape, LOW)
    after, *kept = pl.pallas_call(
        functools.partial(attention_forward_kernel, biased, crossed, places),
        grid=(1,),
        in_specs=[whole()] * 2 + [weight_spec(weights)] + [whole()] * (len(operands) - 3),
        out_specs=[whole()] * 6,
        out_shape=[jax.ShapeDtypeStruct(rows.shape, FULL)] + [low] * 5,
        compiler_params=params(),
        name="attention_forward",
    )(*operands)
    return after, kept


def attention_backward_kernel(biased, crossed, places, mine_ref, *refs):
    refs = list(refs)
    grad_ref, rows_ref, gain_ref, weight_ref = refs[:4]
    matrix = matrix_reader(weight_ref, places)
    norm_ref, query_ref, key_ref, value_ref, mixed_ref = refs[4:9]
    source_ref = refs[9] if crossed else None
    bias_ref = refs[9 + crossed] if biased else None
    refs = refs[9 + crossed + biased :]
    result_ref, sent_ref, kept_ref, gain_grad_ref, extra_ref = refs[:5]
    grad_query_ref, grad_key_ref, grad_value_ref, grad_mixed_ref = refs[5:]
    mine = mine_ref[0]

    def put(m, value):
        @pl.when(mine == m // 2)
        def keep():
            kept_ref[pl.ds(m % 2 * D, D)] = value

        @pl.when(mine != m // 2)
        def send():
            sent_ref[pl.ds(m % 2 * D, D)] = value

    grad = grad_ref[...]
    grad_out = grad.astype(LOW)
    grad_mixed_ref[...] = mul_right(grad_out, matrix(3)).astype(LOW)
    put(3, mul_left(mixed_ref[...], grad_out).astype(LOW))
    length = grad.shape[0] // MICRO
    scale = DK ** (-0.5)
    for rows_at, columns, pair in head_pairs(length):
        queries, keys_in = both_heads(query_ref[rows_at, columns]), key_ref[rows_at, columns]
        grad_mixed = both_heads(grad_mixed_ref[rows_at, columns])
        bias = bias_ref[2 * pair : 2 * pair + 2].reshape(2 * length, length) if biased else None
        probs = probabilities(queries, keys_in, bias)
        grad_probs = mul_right(grad_mixed, value_ref[rows_at, columns])
        grad_scores = probs * (grad_probs - jnp.sum(probs * grad_probs, -1, keepdims=True))
        grad_scores = grad_scores.astype(LOW)
        if biased:
            score_rows = grad_scores.astype(FULL).reshape(2, length, length)
            if rows_at.start == 0:
                extra_ref[2 * pair : 2 * pair + 2] = score_rows
            else:
                extra_ref[2 * pair : 2 * pair + 2] += score_rows
        grad_query_ref[rows_at, columns] = (one_pair(mul(grad_scores, keys_in)) * scale).astype(LOW)
        grad_key_ref[rows_at, columns] = (mul_left(grad_scores, queries) * scale).astype(LOW)
        grad_value_ref[rows_at, columns] = mul_left(probs.astype(LOW), grad_mixed).astype(LOW)
    normed = norm_ref[...]
    source = source_ref[...] if crossed else normed
    put(0, mul_left(normed, grad_query_ref[...]).astype(LOW))
    put(1, mul_left(source, grad_key_ref[...]).astype(LOW))
    put(2, mul_left(source, grad_value_ref[...]).astype(LOW))
    grad_norm = mul_right(grad_query_ref[...], matrix(0))
    grad_source = mul_right(grad_key_ref[...], matrix(1))
    grad_source = grad_source + mul_right(grad_value_ref[...], matrix(2))
    if crossed:
        extra_ref[...] = grad_source.astype(LOW)
    else:
        grad_norm = grad_norm + grad_source
    grad_rows, grad_gain = rms_back(rows_ref[...], gain_ref[...], grad_norm)
    result_ref[...] = (grad + grad_rows).astype(result_ref.dtype)
    gain_grad_ref[...] = grad_gain


def attention_backward(grad, rows, gain_row, weights, kept, source, bias):
    crossed, biased = source is not None, bias is not None
    operands = [section_bit(0)[None], grad, rows, gain_row[None], weights[1], *kept]
    places = None if weights[0] is None else slot_places()
    half = jax.ShapeDtypeStruct((MATRICES // 2 * D, D), LOW)
    operands += [source] * crossed + [bias] * biased
    low = pltpu.VMEM(rows.shape, LOW)
    extra = jax.ShapeDtypeStruct(bias.shape, FULL) if biased else jax.ShapeDtypeStruct(rows.shape, LOW)
    return pl.pallas_call(
        functools.partial(attention_backward_kernel, biased, crossed, places),
        grid=(1,),
        in_specs=[pl.BlockSpec(memory_space=pltpu.SMEM)]
        + [whole()] * 3
        + [weight_spec(weights)]
        + [whole()] * (len(operands) - 5),
        out_specs=[whole()] * 5,
        out_shape=[
            jax.ShapeDtypeStruct(rows.shape, FULL if crossed else LOW),
            half,
            half,
            jax.ShapeDtypeStruct((1, D), FULL),
            extra,
        ],
        scratch_shapes=[low] * 4,
        compiler_params=params(),
        name="attention_backward",
    )(*operands)


def adamw(weight, first, second, gradient, rate):
    first = BETA_ONE * first + (1 - BETA_ONE) * gradient
    second = BETA_TWO * second + (1 - BETA_TWO) * gradient * gradient
    stepped = first / (1 - BETA_ONE**STEP) / (jnp.sqrt(second / (1 - BETA_TWO**STEP)) + ADAM_EPS)
    return (first, second, weight - rate * (stepped + DECAY * weight))


def ordered(own, other, mine, axis):
    return jnp.where(
        mine == 0, jnp.stack([own, other], axis), jnp.stack([other, own], axis)
    )


def low_bit_order():
    return sorted(range(lax.axis_size("section")), key=lambda section: (section & 1, section))


def slot_places():
    order = low_bit_order()
    return [order.index(section) for section in range(len(order))]


def slot_layout():
    return [1] + list(range(bit_count() - 1, 1, -1))


def shampoo_terms(low, full, left_block, right_full):
    rows = low.shape[0]
    start = (lax.axis_index("section") // MATRICES) * rows
    columns = lax.dynamic_slice_in_dim(full, start, rows, 1)
    blended = to_low(forward_mul(left_block, full))
    direction = forward_mul(blended, right_full)
    left_term = jnp.einsum("rd,ed->re", low, full, preferred_element_type=jnp.float32)
    right_term = jnp.einsum("dr,de->re", columns, full, preferred_element_type=jnp.float32)
    terms = jnp.stack([low, to_low(direction), to_low(left_term), to_low(right_term)])
    return terms.reshape(4, 2, 2, rows // 4, D)


def gather_small(values):
    values = ordered(values, swap_half(values), lax.axis_index("dp"), 0)[None]
    for bit in range(bit_count()):
        both = ordered(values, swap_bit(values, bit), section_bit(bit), 0)
        values = both.reshape((-1,) + values.shape[1:])
    return values


def lookup_rows(ids, shard_low):
    bits = bit_count()
    start = lax.axis_index("section") * shard_low.shape[0]
    mine = section_bit(0)

    def owned(some_ids):
        hit = some_ids.reshape(-1, 1) == jnp.arange(shard_low.shape[0])[None, :]
        return to_low(forward_mul(hit.astype(jnp.bfloat16), shard_low))

    split = (ids - start).reshape((2,) * bits + (MICRO, -1))
    split = jnp.moveaxis(split, bits, 0)
    sent, kept = pick(split, 1 - mine, bits), pick(split, mine, bits)
    arrived = swap_bit(owned(sent), 0)
    rows = (owned(kept) + arrived).reshape(MICRO, -1, D)
    layout = range(bits - 1, 0, -1)
    orders = [list(range(1, bits)), list(range(2, bits)) + [1]]
    chains = [halved(rows[micro], layout, orders[micro]) for micro in range(MICRO)]
    return jnp.concatenate(interleave(chains, arrived))


def local(
    token_ids,
    targets,
    objective,
    buckets,
    table,
    table_first,
    table_second,
    inner_weight,
    inner_first,
    inner_second,
    outer_weight,
    outer_first,
    outer_second,
    gain_rows,
    gain_first,
    gain_second,
    position_bias,
    bias_first,
    bias_second,
    attention,
    left_stats,
    right_stats,
    left_roots,
    right_inverse_roots,
):
    sections = lax.axis_size("section")
    section_index = lax.axis_index("section")
    half = lax.axis_index("dp")
    is_encoder = half == 0
    is_decoder = half == 1
    length = token_ids.shape[-1]
    vocab_rows = table.shape[0]
    bits = sections.bit_length() - 1

    packed = jnp.concatenate(
        [token_ids.reshape(-1), targets.reshape(-1), jnp.broadcast_to(objective.reshape(-1), (length,))]
    )
    every = gather_small(packed.reshape(-1, length)).reshape(sections, 2, -1).swapaxes(0, 1)
    every_tokens = every[:, :, : MICRO * length]
    every_targets = every[:, :, MICRO * length : (MICRO + 1) * length]
    every_objective = every[:, :, (MICRO + 1) * length]
    halves = sections // 2
    encoder_ids = every_tokens[:, :halves].reshape(sections, MICRO * length)
    decoder_ids = every_tokens[:, halves:].reshape(sections, MICRO * length)
    own_ids = jnp.where(is_encoder, encoder_ids, decoder_ids)

    def of_micro(values):
        return jnp.where(is_encoder, values[:, halves:], values[:, :halves])

    goal_ids = of_micro(every_targets).reshape(-1)
    goal_objective = of_micro(every_objective).reshape(sections)
    live_all = (
        jnp.arange(length)[None, :] < jnp.where(goal_objective == 1, length, SPAN)[:, None]
    ).astype(jnp.float32)
    live_rows = pick(live_all, section_index, 0)

    shard_low = to_low(table)
    attention_low = to_low(attention)
    shard_rows = attention.shape[1] * MATRICES
    self_shard = lax.dynamic_slice_in_dim(attention_low, half * MATRICES, MATRICES, 0)
    weight_shard = jnp.stack(
        [
            self_shard.reshape(shard_rows, D),
            to_low(pick(inner_weight, half, 0).T),
            to_low(pick(outer_weight, half, 0)),
            attention_low[8:12].reshape(shard_rows, D),
        ]
    )
    weights = lax.all_gather(
        weight_shard, "section", axis=1, tiled=True, axis_index_groups=[low_bit_order()]
    )
    def natural(slot):
        split = slot.reshape(2, sections // 2, MATRICES, -1, D)
        return jnp.transpose(split, (2, 1, 0, 3, 4)).reshape(MATRICES, D, D)

    if attention.shape[1] % 16 == 0:
        self_weights, cross_weights = (0, weights), (3, weights)
    else:
        self_weights, cross_weights = (None, natural(weights[0])), (None, natural(weights[3]))

    bucket_square = offset_square(pick(buckets, half, 0), length)
    bucket_range = jnp.arange(position_bias.shape[1])
    onehot = (bucket_square[:, :, None] == bucket_range).astype(jnp.bfloat16)
    bias_term = position_table(onehot, pick(position_bias, half, 0))
    allowed = is_encoder | (jnp.arange(length)[:, None] >= jnp.arange(length)[None, :])

    rows_in = to_full(lookup_rows(own_ids, shard_low))
    gain_self = gain_rows[jnp.where(is_encoder, 0, 3)]
    gain_feed = gain_rows[jnp.where(is_encoder, 1, 5)]
    bias_term = jnp.where(allowed, bias_term, NEGATIVE)
    resid, kept_self = attention_forward(rows_in, gain_self, self_weights, None, bias_term)

    def encoder_rest():
        return feed_forward(resid, gain_feed, gain_rows[2], weights, 1.0)

    first, second = section_bit(0), section_bit(1)
    root_rows = jnp.stack([left_roots, right_inverse_roots])
    own_roots = lax.dynamic_slice_in_dim(root_rows, half * MATRICES, MATRICES, 1)
    root_rows = jnp.stack([own_roots, root_rows[:, 8:12]]).reshape(4, 2, 2, -1, D)
    root_part = swap_bit(pick(root_rows, 1 - first, 1), 0)
    root_rows, resid, root_part = lax.optimization_barrier((root_rows, resid, root_part))
    root_rows = ordered(pick(root_rows, first, 1), root_part, first, 2)
    root_part = swap_bit(pick(root_rows, 1 - second, 1), 1)

    after_enc, encoded, before_enc = lax.cond(
        is_encoder, encoder_rest, lambda: jax.tree.map(jnp.zeros_like, encoder_rest())
    )
    encoded, root_part = lax.optimization_barrier((encoded, root_part))
    arrived = to_decoder(encoded)
    root_rows = ordered(pick(root_rows, second, 1), root_part, second, 1)
    root_rows = root_rows.reshape(2, 2, -1, D)
    root_lefts, root_rights = root_rows[:, 0], root_rows[:, 1]
    root_steps = list(range(bits - 1, 1, -1))

    def root_step(stage):
        return swap_bit(root_rights, root_steps[stage])

    def grown(stage, part):
        mine = section_bit(root_steps[stage])
        return ordered(root_rights, part, mine, 1 + stage)

    for stage in range(len(root_steps) - 2):
        root_rights = grown(stage, root_step(stage))
    root_part = root_step(len(root_steps) - 2)

    def decoder_rest(after, before):
        rows_feed, kept_cross = attention_forward(
            resid, gain_rows[4], cross_weights, arrived, None
        )
        after, final, before = feed_forward(
            rows_feed, gain_feed, gain_rows[6], weights, D ** (-0.5)
        )
        return (final, after, before, rows_feed, kept_cross)

    def decoder_skip(after, before):
        empty = jnp.zeros(resid.shape, jnp.bfloat16)
        return (empty, after, before, resid, [empty] * 5)

    final_low, after_feed, before_feed, rows_feed, kept_cross = lax.cond(
        is_decoder, decoder_rest, decoder_skip, after_enc, before_enc
    )

    final_low, root_part = lax.optimization_barrier((final_low, root_part))
    root_rights = grown(len(root_steps) - 2, root_part)

    final_split = final_low.reshape(MICRO, length, D)
    handed = to_encoder(final_split[0])
    own_rows = jnp.where(is_encoder, handed, final_split[1])
    head_low = own_rows * live_rows[:, None].astype(jnp.bfloat16)
    all_rows = lax.all_gather(head_low, "section", axis=0, tiled=True)
    logits = jnp.einsum("nd,vd->nv", all_rows, shard_low, preferred_element_type=jnp.float32)
    goal_hit = (goal_ids - section_index * vocab_rows)[:, None] == jnp.arange(vocab_rows)[None, :]
    row_peak = jnp.max(logits, -1)
    row_total = jnp.sum(jnp.exp(logits - row_peak[:, None]), -1)
    goal_logit = jnp.sum(jnp.where(goal_hit, logits, 0.0), -1)
    for bit in range(bits):
        other_peak, other_total = swap_bit(jnp.stack([row_peak, row_total]), bit)
        top_peak = jnp.maximum(row_peak, other_peak)
        row_total = row_total * jnp.exp(row_peak - top_peak)
        row_total = row_total + other_total * jnp.exp(other_peak - top_peak)
        row_peak = top_peak
    log_total = row_peak + jnp.log(row_total)
    grad_logits = to_low(jnp.exp(logits - log_total[:, None]) - goal_hit.astype(jnp.float32))
    grad_all = forward_mul(grad_logits, shard_low)
    def head_table_task():
        yield (None, 14, None, None)
        product = lambda grads: mul_left(grads, all_rows)
        return (yield ("core", 10, product, grad_logits))

    chain = halved(grad_all, range(bits - 1, -1, -1), range(bits))
    grad_head, head_table = interleave([chain, head_table_task()], log_total)
    grad_head = to_full(grad_head)
    grad_head = to_low(grad_head * live_rows[:, None])
    own_live = lax.dynamic_slice_in_dim(log_total, section_index * length, length, 0)
    loss_part = jnp.sum(live_rows * own_live) - jnp.sum(live_all.reshape(-1) * goal_logit)
    count_part = jnp.sum(live_rows)
    grad_final = jnp.stack([to_decoder(grad_head), grad_head]).reshape(MICRO * length, D)

    def decoder_back():
        grad_rows, *feed_grads, gains = feed_backward(
            grad_final,
            after_feed,
            gain_rows[6],
            rows_feed,
            gain_feed,
            before_feed,
            weights,
            D ** (-0.5),
        )
        grad_rows, *cross_grads, gain_cross, grad_source = attention_backward(
            grad_rows, resid, gain_rows[4], cross_weights, kept_cross, arrived, None
        )
        gains = jnp.concatenate([gain_cross, gains])
        return (grad_source, grad_rows, feed_grads, cross_grads, gains)

    root_rights, grad_final = lax.optimization_barrier((root_rights, grad_final))
    root_part = root_step(len(root_steps) - 1)
    grad_source, grad_dec, feed_dec, cross_grads, gains_dec = lax.cond(
        is_decoder, decoder_back, lambda: jax.tree.map(jnp.zeros_like, decoder_back())
    )
    back_source = to_encoder(grad_source)

    back_source, feed_dec, cross_grads, root_part = lax.optimization_barrier(
        (back_source, feed_dec, cross_grads, root_part)
    )
    root_rights = grown(len(root_steps) - 1, root_part).reshape(2, D, D)

    late = to_low(to_full(cross_grads[1]) + to_full(swap_bit(cross_grads[0], 0, (1,))))
    late_split = late.reshape(2, -1, D)
    late_part, back_source, grad_dec = lax.optimization_barrier(
        (pick(late_split, 1 - second, 0), back_source, grad_dec)
    )
    late_arrived = swap_bit(late_part, 1, (1,))

    def self_back(grad_rows):
        return attention_backward(
            grad_rows, rows_in, gain_self, self_weights, kept_self, None, bias_term
        )

    def encoder_feed():
        grad_rows, *feed_grads, gains = feed_backward(
            back_source,
            after_feed,
            gain_rows[2],
            resid,
            gain_feed,
            before_feed,
            weights,
            1.0,
        )
        empty = jnp.zeros((MATRICES // 2 * D, D), jnp.bfloat16)
        score = jnp.zeros(bias_term.shape, jnp.float32)
        return (grad_rows, gains, score, [empty, empty], feed_grads)

    def decoder_self():
        embed_low, *self_grads, gain_grad, score_grad = self_back(grad_dec)
        gains = jnp.concatenate([gain_grad, gain_grad])
        return (to_full(embed_low), gains, score_grad, self_grads, feed_dec)

    grad_rows, gains_middle, score_middle, self_middle, feed_grads = lax.cond(
        is_encoder, encoder_feed, decoder_self
    )
    grad_rows, self_middle, feed_grads, late_arrived = lax.optimization_barrier(
        (grad_rows, self_middle, feed_grads, late_arrived)
    )
    late = to_low(to_full(pick(late_split, second, 0)) + to_full(late_arrived))
    third = section_bit(2)
    late_split = late.reshape(2 ** (bits - 3), 2, -1, D)
    late_part, grad_rows = lax.optimization_barrier(
        (pick(late_split, 1 - third, 1).reshape(-1, D), grad_rows)
    )
    late_arrived = swap_bit(late_part, 2, (1,))

    feed_arrived = swap_bit(feed_grads[0], 0)

    def encoder_self():
        embed_low, *self_grads, gain_grad, score_grad = self_back(grad_rows)
        gains = jnp.concatenate([gain_grad, gains_middle, jnp.zeros((4, D), jnp.float32)])
        return (embed_low, gains, score_grad, self_grads)

    def decoder_skip_self():
        gains = jnp.concatenate([jnp.zeros((3, D), jnp.float32), gains_middle[:1], gains_dec])
        return (to_low(grad_rows), gains, score_middle, self_middle)

    embed_low, gain_part, score_grad, self_grads = lax.cond(
        is_encoder, encoder_self, decoder_skip_self
    )
    embed_low, self_grads, late_arrived, feed_arrived = lax.optimization_barrier(
        (embed_low, self_grads, late_arrived, feed_arrived)
    )
    feed_half = to_low(to_full(feed_grads[1]) + to_full(feed_arrived))
    late = pick(late_split, third, 1).reshape(-1, D)
    late = to_low(to_full(late) + to_full(late_arrived))

    found = {}
    own_local = (own_ids.reshape(-1) - section_index * vocab_rows)[None, :]

    def squares(values):
        return jnp.sum(to_full(values) * to_full(values))

    def rows_task():
        every_rows = yield ("gather", 80, lambda rows: lax.all_gather(rows, "section"), embed_low)
        found["rows"] = every_rows.reshape(-1, D)

    def feed_task():
        yield (None, 10, None, None)
        layout = ["matrix"] + list(range(bits - 1, 0, -1))
        own = yield from halved(feed_half.reshape(-1, D), layout, range(1, 3))
        found["feed_two"] = own
        own = yield from halved(own, layout[:-2], range(3, bits))
        own = own.reshape(2, -1, D)
        found["feed_square"] = squares(own)
        found["feed"] = own
        return own, (yield ("dp", -15, swap_half, own))

    block_rows = -(-vocab_rows // 16) * 8
    shared = 2 * block_rows - vocab_rows
    starts = [0, vocab_rows - block_rows]

    def table_task():
        yield from until(found, ["rows", "feed_two"])
        own_start, other_start = jnp.where(is_encoder, jnp.array(starts), jnp.array(starts[::-1]))

        def product(start):
            def rows_of(rows):
                hit = own_local == start + jnp.arange(block_rows)[:, None]
                head = lax.dynamic_slice_in_dim(head_table, start, block_rows, 0)
                return to_low(mul(hit.astype(jnp.bfloat16), rows) + head)

            return rows_of

        sent = yield ("core", 10, product(other_start), found["rows"])
        found["table_sent"] = sent
        arrived = yield ("dp", -36, swap_half, sent)
        own = yield ("core", 10, product(own_start), found["rows"])
        yield (None, 30, None, None)
        own = to_low(to_full(own) + to_full(arrived))
        counted = is_encoder | (jnp.arange(block_rows) >= shared)
        found["table_square"] = squares(jnp.where(counted[:, None], own, jnp.zeros_like(own)))
        other = yield ("dp", -36, swap_half, own)
        return jnp.concatenate(
            [jnp.where(is_encoder, own, other), jnp.where(is_encoder, other, own)[shared:]]
        )

    def cross_task():
        layout = [bit for bit in slot_layout()[1:] if bit > 2]
        block = yield from halved(late, layout, range(3, bits), (1,))
        found["cross_square"] = squares(block)
        full = yield from doubled(block, (1,))
        terms = shampoo_terms(block, full, root_lefts[1], root_rights[1])
        found["cross_direction"] = squares(terms[1])
        terms = yield from to_rows(terms, (1,))
        yield from until(found, ["feed"])
        other = yield ("dp", -30, to_encoder, tied(terms, found["feed"]))
        return terms, other

    def self_task():
        block = yield from halved(tuple(self_grads), slot_layout(), range(1, bits))
        found["self_square"] = squares(block)
        yield from until(found, ["table_sent"])
        full = yield from doubled(tied(block, found["table_sent"]))
        terms = shampoo_terms(block, full, root_lefts[0], root_rights[0])
        found["self_direction"] = squares(terms[1])
        terms = yield from to_rows(terms)
        yield from until(found, ["feed"])
        other = yield ("dp", -30, swap_half, tied(terms, found["feed"]))
        return terms, other

    def norm_task():
        yield from until(found, ["self_square", "cross_square", "feed_square", "table_square"])
        bias_grad = jnp.einsum(
            "hqk,qkb->bh", score_grad, onehot.astype(jnp.float32), precision=HIGH
        ).reshape(1, -1)
        bias_rows = [jnp.where(half == layer, bias_grad, 0.0) for layer in range(2)]
        square_sum = found["self_square"] + is_decoder.astype(jnp.float32) * found["cross_square"]
        square_sum = square_sum + found["feed_square"] + found["table_square"]
        sums = jnp.stack([loss_part, count_part, square_sum])
        sums = jnp.pad(sums, (0, D - sums.shape[0])).reshape(1, D)
        bias_rows = jnp.concatenate(bias_rows, 1).reshape(-1, D)
        sums = yield from summed(jnp.concatenate([gain_part, bias_rows, sums]))
        return sums, (yield ("dp", -5, swap_half, sums))

    def direction_task():
        yield from until(found, ["self_direction", "cross_direction"])
        matrix = 2 * section_bit(0) + section_bit(1)
        names = jnp.arange(3 * MATRICES)
        own_matrix, cross_matrix = half * MATRICES + matrix, 2 * MATRICES + matrix
        sums = jnp.where(names == own_matrix, found["self_direction"], 0.0)
        sums = sums + jnp.where(
            names == cross_matrix, is_decoder * found["cross_direction"], 0.0
        )
        sums = yield from summed(jnp.pad(sums, (0, 128 - sums.shape[0])).reshape(1, 128))
        return sums, (yield ("dp", -5, swap_half, sums))

    tasks = [rows_task(), self_task(), cross_task(), table_task(), feed_task()]
    tasks += [norm_task(), direction_task()]
    results = interleave(tasks, embed_low)
    self_terms, cross_terms, table_grad, feed_both = results[1:5]
    norm_sums, directions = results[5:]
    norm_sums = norm_sums[0] + norm_sums[1]
    small, sums = norm_sums[:-1], norm_sums[-1]
    directions = (directions[0] + directions[1])[0, : 3 * MATRICES]
    gain_full = small[: gain_rows.shape[0]]
    bias_full = small[gain_rows.shape[0] :].reshape(position_bias.shape)
    small_square = squares(gain_full) + squares(bias_full)

    grad_norm = jnp.sqrt(sums[2] + small_square)
    clip_factor = CLIP / jnp.maximum(grad_norm, CLIP)
    table_out = adamw(table, table_first, table_second, table_grad * clip_factor, RATE_TABLE)
    feed_both = to_full(ordered(*feed_both, half, 1))
    inner_part = jnp.swapaxes(feed_both[0], 1, 2)
    outer_part = feed_both[1]
    inner_out = adamw(inner_weight, inner_first, inner_second, inner_part * clip_factor, RATE_INNER)
    outer_out = adamw(outer_weight, outer_first, outer_second, outer_part * clip_factor, RATE_INNER)
    table_out, self_terms, cross_terms = lax.optimization_barrier(
        (table_out, self_terms, cross_terms)
    )
    terms = jnp.concatenate(
        [
            ordered(*self_terms, half, 1).reshape(4, 2 * MATRICES, -1, D),
            jnp.where(is_encoder, cross_terms[1], cross_terms[0]),
        ],
        1,
    )
    attention_grad, direction, left_term, right_term = to_full(terms)
    gain_out = adamw(gain_rows, gain_first, gain_second, gain_full * clip_factor, RATE_GAIN)
    bias_out = adamw(position_bias, bias_first, bias_second, bias_full * clip_factor, RATE_BIAS)
    clip_square = clip_factor * clip_factor
    left_new = BETA_STATS * left_stats + (1 - BETA_STATS) * clip_square * left_term
    right_new = BETA_STATS * right_stats + (1 - BETA_STATS) * clip_square * right_term
    spread = jnp.sqrt(directions / (D * D) + EPS)[:, None, None]
    attention_new = attention - RATE_ATTENTION * (direction / spread + DECAY * attention)
    return (
        sums[0],
        sums[1],
        grad_norm,
        *table_out,
        *inner_out,
        *outer_out,
        *gain_out,
        *bias_out,
        attention_grad * clip_factor,
        left_new,
        right_new,
        attention_new,
    )


def solution(mesh):
    in_specs = (
        P("dp", "section", None, None),
        P("dp", "section", None),
        P("dp", "section"),
        P(),
        P("section", None),
        P("section", None),
        P("section", None),
        P(None, None, "section"),
        P(None, None, "section"),
        P(None, None, "section"),
        P(None, "section", None),
        P(None, "section", None),
        P(None, "section", None),
        P(),
        P(),
        P(),
        P(),
        P(),
        P(),
        P(None, "section", None),
        P(None, "section", None),
        P(None, "section", None),
        P(None, "section", None),
        P(None, "section", None),
    )
    out_specs = (
        P(),
        P(),
        P(),
        P("section", None),
        P("section", None),
        P("section", None),
        P(None, None, "section"),
        P(None, None, "section"),
        P(None, None, "section"),
        P(None, "section", None),
        P(None, "section", None),
        P(None, "section", None),
        P(),
        P(),
        P(),
        P(),
        P(),
        P(),
        P(None, "section", None),
        P(None, "section", None),
        P(None, "section", None),
        P(None, "section", None),
    )
    return jax.shard_map(local, mesh=mesh, in_specs=in_specs, out_specs=out_specs, check_vma=False)
```

```python
import functools
import heapq
import math

import jax
import jax.numpy as jnp
from jax import lax
from jax.experimental import pallas as pl
from jax.experimental.pallas import tpu as pltpu
from jax.sharding import PartitionSpec as P

D = 768
HEADS = 12
DK = 64
MICRO = 2
STEP = 5
SPAN = 28
MATRICES = 4


EPS = 1e-06
CLIP = 1.0
BETA_ONE = 0.9
BETA_TWO = 0.95
BETA_STATS = 0.95
ADAM_EPS = 1e-08
DECAY = 0.01
RATE_TABLE = 0.5
RATE_INNER = 0.01
RATE_GAIN = 0.2
RATE_BIAS = 0.3
RATE_ATTENTION = 0.01
NEGATIVE = -1000000000.0
HIGH = lax.Precision.HIGHEST
VMEM_BYTES = 52 * 1024 * 1024
LOW = jnp.bfloat16
FULL = jnp.float32


def to_low(values):
    return values.astype(jnp.bfloat16)


def to_full(values):
    return values.astype(jnp.float32)


def pick(values, index, axis):
    return lax.dynamic_index_in_dim(values, index, axis, False)


def bit_count():
    return lax.axis_size("section").bit_length() - 1


def section_bit(bit):
    return (lax.axis_index("section") >> bit) & 1


def swap_bit(value, bit, planes=(0, 1)):
    pairs = [
        (2 * source + plane, 2 * (source ^ (1 << bit)) + plane)
        for source in range(lax.axis_size("section"))
        for plane in planes
    ]
    return lax.ppermute(value, ("section", "dp"), pairs)


def swap_half(value):
    return lax.ppermute(value, "dp", [(0, 1), (1, 0)])


def to_decoder(value):
    return lax.ppermute(value, "dp", [(0, 1)])


def to_encoder(value):
    return lax.ppermute(value, "dp", [(1, 0)])


def over(bit, planes=(0, 1)):
    return lambda value: swap_bit(value, bit, planes)


def link_cost(bit, value):
    return 4 + value.size * (6e-6 if bit == 0 else 6.5e-5 if bit < 3 else 1.1e-4)


def zero_after(value):
    mark = value[(0,) * value.ndim]
    return jnp.where(mark != mark, 1.0, 0.0)


def tied(value, *others):
    for other in others:
        value = value + zero_after(other).astype(value.dtype)
    return value


def interleave(tasks, after):
    results, free, pending, now, count = [None] * len(tasks), {}, [], 0.0, 0
    last = after

    def advance(index, arrived):
        nonlocal last, now, count
        posted = True
        while posted:
            try:
                link, cost, move, value = tasks[index].send(arrived)
            except StopIteration as stop:
                results[index] = stop.value
                return
            posted = cost < 0
            if posted:
                value, last = lax.optimization_barrier((value, last))
                free[link] = max(now, free.get(link, 0.0)) - cost
                arrived = move(value)
        count += 1
        if move is None:
            heapq.heappush(pending, (now + cost, count, index, None))
            return
        value, last = lax.optimization_barrier((value, last))
        if link == "core":
            now += cost
            free[link] = now
        else:
            now += 1.0
            free[link] = max(now, free.get(link, 0.0)) + cost
        heapq.heappush(pending, (free[link], count, index, move(value)))

    for index in range(len(tasks)):
        advance(index, None)
    while pending:
        ended, unused, index, arrived = heapq.heappop(pending)
        now = max(now, ended)
        if arrived is not None:
            now += 2.0 + 6e-6 * min(arrived.size, D * D)
            arrived, last = lax.optimization_barrier((arrived, last))
            last = arrived
        advance(index, arrived)
    return results


def halved(rows, layout, order, planes=(0, 1)):
    layout = list(layout)
    if isinstance(rows, tuple):
        part, kept = rows
        arrived = yield (0, link_cost(0, part), over(0, planes), part)
        rows = to_low(to_full(kept) + to_full(arrived))
    for bit in order:
        place = layout.index(bit)
        layout.remove(bit)
        split = rows.reshape(2**place, 2, -1, D)
        mine = section_bit(bit)
        part = to_low(pick(split, 1 - mine, 1)).reshape(-1, D)
        arrived = yield (bit, link_cost(bit, part), over(bit, planes), part)
        rows = to_low(to_full(pick(split, mine, 1).reshape(-1, D)) + to_full(arrived))
    return rows


def doubled(block, planes=(0, 1)):
    for stage, bit in enumerate(range(bit_count() - 1, 1, -1)):
        arrived = yield (bit, link_cost(bit, block), over(bit, planes), block)
        block = ordered(block, arrived, section_bit(bit), stage)
    return block.reshape(-1, D)


def to_rows(terms, planes=(0, 1)):
    first, second = section_bit(0), section_bit(1)
    part = pick(terms, 1 - first, 2)
    arrived = yield (0, link_cost(0, part), over(0, planes), part)
    terms = ordered(pick(terms, first, 2), arrived, first, 1)
    part = pick(terms, 1 - second, 2)
    arrived = yield (1, link_cost(1, part), over(1, planes), part)
    terms = ordered(pick(terms, second, 2), arrived, second, 2)
    return terms.reshape(terms.shape[0], MATRICES, -1, D)


def summed(values):
    for bit in range(bit_count()):
        arrived = yield (bit, 5, over(bit), values)
        values = values + arrived
    return values


def until(found, names):
    while not all(name in found for name in names):
        yield (None, 2, None, None)


def forward_mul(left, right):
    return jnp.dot(left, right, preferred_element_type=jnp.float32)


def offset_square(row, length):
    width = 2 * length
    padded = jnp.pad(row, (0, width - row.shape[0]))
    flat = jnp.tile(padded, length)[length - 1 : length - 1 + length * (width - 1)]
    return flat.reshape(length, width - 1)[:, :length]


def position_table(onehot, bias_layer):
    return jnp.einsum("qkb,bh->hqk", onehot.astype(jnp.float32), bias_layer, precision=HIGH)


def mul(left, right):
    return lax.dot_general(left, right, (((1,), (0,)), ((), ())), preferred_element_type=FULL)


def mul_right(left, right):
    return lax.dot_general(left, right, (((1,), (1,)), ((), ())), preferred_element_type=FULL)


def mul_left(left, right):
    return lax.dot_general(left, right, (((0,), (0,)), ((), ())), preferred_element_type=FULL)


def rms_scale(values):
    return lax.rsqrt(jnp.mean(values * values, -1, keepdims=True) + EPS)


def rms_back(values, gain_row, upstream):
    scale = rms_scale(values)
    normal = values * scale
    grad_gain = jnp.sum(upstream * normal, 0, keepdims=True)
    weighted = upstream * gain_row
    inner = jnp.mean(weighted * normal, -1, keepdims=True)
    return scale * (weighted - normal * inner), grad_gain


def gelu_parts(values):
    inner = math.sqrt(2.0 / math.pi) * (values + 0.044715 * values * values * values)
    bent = jnp.tanh(inner)
    slope = math.sqrt(2.0 / math.pi) * (1.0 + 3 * 0.044715 * values * values)
    value = 0.5 * values * (1.0 + bent)
    grad = 0.5 * (1.0 + bent) + 0.5 * values * (1.0 - bent * bent) * slope
    return value, grad


def params():
    return pltpu.CompilerParams(vmem_limit_bytes=VMEM_BYTES)


def whole():
    return pl.BlockSpec(memory_space=pltpu.VMEM)


def feed_forward_kernel(
    last_scale, rows_ref, gain_ref, last_ref, in_ref, out_ref, after_ref, head_ref, before_ref, norm_ref, total_ref
):
    step = pl.program_id(0)

    @pl.when(step == 0)
    def start():
        rows = rows_ref[...]
        norm_ref[...] = (rows * rms_scale(rows) * gain_ref[...]).astype(LOW)
        total_ref[...] = rows

    before = mul_right(norm_ref[...], in_ref[0])
    before_ref[...] = before
    active, unused = gelu_parts(before)
    total_ref[...] += mul(active.astype(LOW), out_ref[0])

    @pl.when(step == pl.num_programs(0) - 1)
    def finish():
        after = total_ref[...]
        after_ref[...] = after
        head_ref[...] = (after * rms_scale(after) * last_ref[...] * last_scale).astype(LOW)


def feed_forward(rows, gain_row, last_gain, weights, last_scale):
    count, hidden = rows.shape[0], weights.shape[1]
    chunk = D
    fixed = pl.BlockSpec((count, D), lambda j: (0, 0))
    row = pl.BlockSpec((1, D), lambda j: (0, 0))
    return pl.pallas_call(
        functools.partial(feed_forward_kernel, last_scale),
        grid=(hidden // chunk,),
        in_specs=[
            fixed,
            row,
            row,
            pl.BlockSpec((1, chunk, D), lambda j: (1, j, 0)),
            pl.BlockSpec((1, chunk, D), lambda j: (2, j, 0)),
        ],
        out_specs=[fixed, fixed, pl.BlockSpec((count, chunk), lambda j: (0, j))],
        out_shape=[
            jax.ShapeDtypeStruct((count, D), FULL),
            jax.ShapeDtypeStruct((count, D), LOW),
            jax.ShapeDtypeStruct((count, hidden), FULL),
        ],
        scratch_shapes=[pltpu.VMEM((count, D), LOW), pltpu.VMEM((count, D), FULL)],
        compiler_params=params(),
        name="feed_forward",
    )(rows, gain_row[None], last_gain[None], weights, weights)


def feed_backward_kernel(
    last_scale,
    mine_ref,
    upstream_ref,
    after_ref,
    last_ref,
    rows_ref,
    gain_ref,
    before_ref,
    in_ref,
    out_ref,
    grad_ref,
    sent_ref,
    kept_ref,
    gains_ref,
    resid_ref,
    low_ref,
    norm_ref,
    total_ref,
):
    step = pl.program_id(0)

    @pl.when(step == 0)
    def start():
        upstream = upstream_ref[...].astype(FULL) * last_scale
        resid, grad_last = rms_back(after_ref[...], last_ref[...], upstream)
        resid_ref[...] = resid
        low_ref[...] = resid.astype(LOW)
        rows = rows_ref[...]
        norm_ref[...] = (rows * rms_scale(rows) * gain_ref[...]).astype(LOW)
        total_ref[...] = jnp.zeros_like(total_ref)
        gains_ref[1:2] = grad_last

    grad_out = low_ref[...]
    active, slope = gelu_parts(before_ref[...])
    grad_before = (mul_right(grad_out, out_ref[0]) * slope).astype(LOW)
    total_ref[...] += mul(grad_before, in_ref[0])
    in_grad = mul_left(grad_before, norm_ref[...]).astype(LOW)
    out_grad = mul_left(active.astype(LOW), grad_out).astype(LOW)

    @pl.when(step < 2)
    def send():
        sent_ref[0] = in_grad
        sent_ref[1] = out_grad

    @pl.when(step >= 2)
    def keep():
        kept_ref[0] = in_grad
        kept_ref[1] = out_grad

    @pl.when(step == pl.num_programs(0) - 1)
    def finish():
        grad_rows, grad_gain = rms_back(rows_ref[...], gain_ref[...], total_ref[...])
        grad_ref[...] = resid_ref[...] + grad_rows
        gains_ref[0:1] = grad_gain


def feed_backward(upstream, after, last_gain, rows, gain_row, before, weights, last_scale):
    count, hidden = before.shape
    chunk = hidden // 4

    def place(step, mine):
        return 2 * ((step >= 2) == (mine[0] == 1)) + step % 2

    fixed = pl.BlockSpec((count, D), lambda j, mine: (0, 0))
    row = pl.BlockSpec((1, D), lambda j, mine: (0, 0))
    half = jax.ShapeDtypeStruct((2, hidden // 2, D), LOW)
    return pl.pallas_call(
        functools.partial(feed_backward_kernel, last_scale),
        grid_spec=pltpu.PrefetchScalarGridSpec(
            num_scalar_prefetch=1,
            grid=(4,),
            in_specs=[
                fixed,
                fixed,
                row,
                fixed,
                row,
                pl.BlockSpec((count, chunk), lambda j, mine: (0, place(j, mine))),
                pl.BlockSpec((1, chunk, D), lambda j, mine: (1, place(j, mine), 0)),
                pl.BlockSpec((1, chunk, D), lambda j, mine: (2, place(j, mine), 0)),
            ],
            out_specs=[
                fixed,
                pl.BlockSpec((2, chunk, D), lambda j, mine: (0, jnp.minimum(j, 1), 0)),
                pl.BlockSpec((2, chunk, D), lambda j, mine: (0, jnp.maximum(j - 2, 0), 0)),
                pl.BlockSpec((2, D), lambda j, mine: (0, 0)),
            ],
            scratch_shapes=[
                pltpu.VMEM((count, D), FULL),
                pltpu.VMEM((count, D), LOW),
                pltpu.VMEM((count, D), LOW),
                pltpu.VMEM((count, D), FULL),
            ],
        ),
        out_shape=[
            jax.ShapeDtypeStruct((count, D), FULL),
            half,
            half,
            jax.ShapeDtypeStruct((2, D), FULL),
        ],
        compiler_params=params(),
        name="feed_backward",
    )(section_bit(0)[None], upstream, after, last_gain[None], rows, gain_row[None], before, weights, weights)


def weight_spec(weights):
    slot, values = weights
    if slot is None:
        return pl.BlockSpec(memory_space=pltpu.VMEM)
    return pl.BlockSpec((1,) + values.shape[1:], lambda i: (slot, 0, 0))


def matrix_reader(ref, places):
    if places is None:
        return lambda m: ref[m]
    rows = D // len(places)
    return lambda m: jnp.concatenate(
        [ref[0, pl.ds((place * MATRICES + m) * rows, rows)] for place in places]
    )


def head_pairs(length):
    for sequence in range(MICRO):
        for pair in range(HEADS // 2):
            yield slice(sequence * length, (sequence + 1) * length), slice(
                pair * 2 * DK, (pair + 1) * 2 * DK
            ), pair


def both_heads(rows):
    left = lax.broadcasted_iota(jnp.int32, rows.shape, 1) < DK
    none = jnp.zeros_like(rows)
    return jnp.concatenate([jnp.where(left, rows, none), jnp.where(left, none, rows)])


def one_pair(rows):
    length = rows.shape[0] // 2
    left = lax.broadcasted_iota(jnp.int32, (length, rows.shape[1]), 1) < DK
    return jnp.where(left, rows[:length], rows[length:])


def probabilities(queries, keys_in, bias):
    scores = mul_right(queries, keys_in) * DK ** (-0.5)
    if bias is not None:
        scores = scores + bias
    raised = jnp.exp(scores - jnp.max(scores, -1, keepdims=True))
    return raised * (1.0 / jnp.sum(raised, -1, keepdims=True))


def attention_forward_kernel(biased, crossed, places, *refs):
    refs = list(refs)
    rows_ref, gain_ref, weight_ref = refs[:3]
    matrix = matrix_reader(weight_ref, places)
    source_ref = refs[3] if crossed else None
    bias_ref = refs[3 + crossed] if biased else None
    after_ref, norm_ref, query_ref, key_ref, value_ref, mixed_ref = refs[3 + crossed + biased :]
    rows = rows_ref[...]
    normed = (rows * rms_scale(rows) * gain_ref[...]).astype(LOW)
    norm_ref[...] = normed
    source = source_ref[...] if crossed else normed
    query_ref[...] = mul(normed, matrix(0)).astype(LOW)
    key_ref[...] = mul(source, matrix(1)).astype(LOW)
    value_ref[...] = mul(source, matrix(2)).astype(LOW)
    length = rows.shape[0] // MICRO
    for rows_at, columns, pair in head_pairs(length):
        queries = both_heads(query_ref[rows_at, columns])
        bias = bias_ref[2 * pair : 2 * pair + 2].reshape(2 * length, length) if biased else None
        probs = probabilities(queries, key_ref[rows_at, columns], bias)
        mixed = mul(probs.astype(LOW), value_ref[rows_at, columns])
        mixed_ref[rows_at, columns] = one_pair(mixed).astype(LOW)
    after_ref[...] = rows + mul(mixed_ref[...], matrix(3))


def attention_forward(rows, gain_row, weights, source, bias):
    crossed, biased = source is not None, bias is not None
    operands = [rows, gain_row[None], weights[1]]
    operands += [source] * crossed + [bias] * biased
    places = None if weights[0] is None else slot_places()
    low = jax.ShapeDtypeStruct(rows.shape, LOW)
    after, *kept = pl.pallas_call(
        functools.partial(attention_forward_kernel, biased, crossed, places),
        grid=(1,),
        in_specs=[whole()] * 2 + [weight_spec(weights)] + [whole()] * (len(operands) - 3),
        out_specs=[whole()] * 6,
        out_shape=[jax.ShapeDtypeStruct(rows.shape, FULL)] + [low] * 5,
        compiler_params=params(),
        name="attention_forward",
    )(*operands)
    return after, kept


def attention_backward_kernel(biased, crossed, places, mine_ref, *refs):
    refs = list(refs)
    grad_ref, rows_ref, gain_ref, weight_ref = refs[:4]
    matrix = matrix_reader(weight_ref, places)
    norm_ref, query_ref, key_ref, value_ref, mixed_ref = refs[4:9]
    source_ref = refs[9] if crossed else None
    bias_ref = refs[9 + crossed] if biased else None
    refs = refs[9 + crossed + biased :]
    result_ref, sent_ref, kept_ref, gain_grad_ref, extra_ref = refs[:5]
    grad_query_ref, grad_key_ref, grad_value_ref, grad_mixed_ref = refs[5:]
    mine = mine_ref[0]

    def put(m, value):
        @pl.when(mine == m // 2)
        def keep():
            kept_ref[pl.ds(m % 2 * D, D)] = value

        @pl.when(mine != m // 2)
        def send():
            sent_ref[pl.ds(m % 2 * D, D)] = value

    grad = grad_ref[...]
    grad_out = grad.astype(LOW)
    grad_mixed_ref[...] = mul_right(grad_out, matrix(3)).astype(LOW)
    put(3, mul_left(mixed_ref[...], grad_out).astype(LOW))
    length = grad.shape[0] // MICRO
    scale = DK ** (-0.5)
    for rows_at, columns, pair in head_pairs(length):
        queries, keys_in = both_heads(query_ref[rows_at, columns]), key_ref[rows_at, columns]
        grad_mixed = both_heads(grad_mixed_ref[rows_at, columns])
        bias = bias_ref[2 * pair : 2 * pair + 2].reshape(2 * length, length) if biased else None
        probs = probabilities(queries, keys_in, bias)
        grad_probs = mul_right(grad_mixed, value_ref[rows_at, columns])
        grad_scores = probs * (grad_probs - jnp.sum(probs * grad_probs, -1, keepdims=True))
        grad_scores = grad_scores.astype(LOW)
        if biased:
            score_rows = grad_scores.astype(FULL).reshape(2, length, length)
            if rows_at.start == 0:
                extra_ref[2 * pair : 2 * pair + 2] = score_rows
            else:
                extra_ref[2 * pair : 2 * pair + 2] += score_rows
        grad_query_ref[rows_at, columns] = (one_pair(mul(grad_scores, keys_in)) * scale).astype(LOW)
        grad_key_ref[rows_at, columns] = (mul_left(grad_scores, queries) * scale).astype(LOW)
        grad_value_ref[rows_at, columns] = mul_left(probs.astype(LOW), grad_mixed).astype(LOW)
    normed = norm_ref[...]
    source = source_ref[...] if crossed else normed
    put(0, mul_left(normed, grad_query_ref[...]).astype(LOW))
    put(1, mul_left(source, grad_key_ref[...]).astype(LOW))
    put(2, mul_left(source, grad_value_ref[...]).astype(LOW))
    grad_norm = mul_right(grad_query_ref[...], matrix(0))
    grad_source = mul_right(grad_key_ref[...], matrix(1))
    grad_source = grad_source + mul_right(grad_value_ref[...], matrix(2))
    if crossed:
        extra_ref[...] = grad_source.astype(LOW)
    else:
        grad_norm = grad_norm + grad_source
    grad_rows, grad_gain = rms_back(rows_ref[...], gain_ref[...], grad_norm)
    result_ref[...] = (grad + grad_rows).astype(result_ref.dtype)
    gain_grad_ref[...] = grad_gain


def attention_backward(grad, rows, gain_row, weights, kept, source, bias):
    crossed, biased = source is not None, bias is not None
    operands = [section_bit(0)[None], grad, rows, gain_row[None], weights[1], *kept]
    places = None if weights[0] is None else slot_places()
    half = jax.ShapeDtypeStruct((MATRICES // 2 * D, D), LOW)
    operands += [source] * crossed + [bias] * biased
    low = pltpu.VMEM(rows.shape, LOW)
    extra = jax.ShapeDtypeStruct(bias.shape, FULL) if biased else jax.ShapeDtypeStruct(rows.shape, LOW)
    return pl.pallas_call(
        functools.partial(attention_backward_kernel, biased, crossed, places),
        grid=(1,),
        in_specs=[pl.BlockSpec(memory_space=pltpu.SMEM)]
        + [whole()] * 3
        + [weight_spec(weights)]
        + [whole()] * (len(operands) - 5),
        out_specs=[whole()] * 5,
        out_shape=[
            jax.ShapeDtypeStruct(rows.shape, FULL if crossed else LOW),
            half,
            half,
            jax.ShapeDtypeStruct((1, D), FULL),
            extra,
        ],
        scratch_shapes=[low] * 4,
        compiler_params=params(),
        name="attention_backward",
    )(*operands)


def adamw(weight, first, second, gradient, rate):
    first = BETA_ONE * first + (1 - BETA_ONE) * gradient
    second = BETA_TWO * second + (1 - BETA_TWO) * gradient * gradient
    stepped = first / (1 - BETA_ONE**STEP) / (jnp.sqrt(second / (1 - BETA_TWO**STEP)) + ADAM_EPS)
    return (first, second, weight - rate * (stepped + DECAY * weight))


def ordered(own, other, mine, axis):
    return jnp.where(
        mine == 0, jnp.stack([own, other], axis), jnp.stack([other, own], axis)
    )


def low_bit_order():
    return sorted(range(lax.axis_size("section")), key=lambda section: (section & 1, section))


def slot_places():
    order = low_bit_order()
    return [order.index(section) for section in range(len(order))]


def slot_layout():
    return [1] + list(range(bit_count() - 1, 1, -1))


def shampoo_terms(low, full, left_block, right_full):
    rows = low.shape[0]
    start = (lax.axis_index("section") // MATRICES) * rows
    columns = lax.dynamic_slice_in_dim(full, start, rows, 1)
    blended = to_low(forward_mul(left_block, full))
    direction = forward_mul(blended, right_full)
    left_term = jnp.einsum("rd,ed->re", low, full, preferred_element_type=jnp.float32)
    right_term = jnp.einsum("dr,de->re", columns, full, preferred_element_type=jnp.float32)
    terms = jnp.stack([low, to_low(direction), to_low(left_term), to_low(right_term)])
    return terms.reshape(4, 2, 2, rows // 4, D)


def gather_small(values):
    values = ordered(values, swap_half(values), lax.axis_index("dp"), 0)[None]
    for bit in range(bit_count()):
        both = ordered(values, swap_bit(values, bit), section_bit(bit), 0)
        values = both.reshape((-1,) + values.shape[1:])
    return values


def lookup_rows(ids, shard_low):
    bits = bit_count()
    start = lax.axis_index("section") * shard_low.shape[0]
    mine = section_bit(0)

    def owned(some_ids):
        hit = some_ids.reshape(-1, 1) == jnp.arange(shard_low.shape[0])[None, :]
        return to_low(forward_mul(hit.astype(jnp.bfloat16), shard_low))

    split = (ids - start).reshape((2,) * bits + (MICRO, -1))
    split = jnp.moveaxis(split, bits, 0)
    sent, kept = pick(split, 1 - mine, bits), pick(split, mine, bits)
    arrived = swap_bit(owned(sent), 0)
    rows = (owned(kept) + arrived).reshape(MICRO, -1, D)
    layout = range(bits - 1, 0, -1)
    orders = [list(range(1, bits)), list(range(2, bits)) + [1]]
    chains = [halved(rows[micro], layout, orders[micro]) for micro in range(MICRO)]
    return jnp.concatenate(interleave(chains, arrived))


def local(
    token_ids,
    targets,
    objective,
    buckets,
    table,
    table_first,
    table_second,
    inner_weight,
    inner_first,
    inner_second,
    outer_weight,
    outer_first,
    outer_second,
    gain_rows,
    gain_first,
    gain_second,
    position_bias,
    bias_first,
    bias_second,
    attention,
    left_stats,
    right_stats,
    left_roots,
    right_inverse_roots,
):
    sections = lax.axis_size("section")
    section_index = lax.axis_index("section")
    half = lax.axis_index("dp")
    is_encoder = half == 0
    is_decoder = half == 1
    length = token_ids.shape[-1]
    vocab_rows = table.shape[0]
    bits = sections.bit_length() - 1

    packed = jnp.concatenate(
        [token_ids.reshape(-1), targets.reshape(-1), jnp.broadcast_to(objective.reshape(-1), (length,))]
    )
    every = gather_small(packed.reshape(-1, length)).reshape(sections, 2, -1).swapaxes(0, 1)
    every_tokens = every[:, :, : MICRO * length]
    every_targets = every[:, :, MICRO * length : (MICRO + 1) * length]
    every_objective = every[:, :, (MICRO + 1) * length]
    halves = sections // 2
    encoder_ids = every_tokens[:, :halves].reshape(sections, MICRO * length)
    decoder_ids = every_tokens[:, halves:].reshape(sections, MICRO * length)
    own_ids = jnp.where(is_encoder, encoder_ids, decoder_ids)

    def of_micro(values):
        return jnp.where(is_encoder, values[:, halves:], values[:, :halves])

    goal_ids = of_micro(every_targets).reshape(-1)
    goal_objective = of_micro(every_objective).reshape(sections)
    live_all = (
        jnp.arange(length)[None, :] < jnp.where(goal_objective == 1, length, SPAN)[:, None]
    ).astype(jnp.float32)
    live_rows = pick(live_all, section_index, 0)

    shard_low = to_low(table)
    attention_low = to_low(attention)
    shard_rows = attention.shape[1] * MATRICES
    self_shard = lax.dynamic_slice_in_dim(attention_low, half * MATRICES, MATRICES, 0)
    weight_shard = jnp.stack(
        [
            self_shard.reshape(shard_rows, D),
            to_low(pick(inner_weight, half, 0).T),
            to_low(pick(outer_weight, half, 0)),
            attention_low[8:12].reshape(shard_rows, D),
        ]
    )
    weights = lax.all_gather(
        weight_shard, "section", axis=1, tiled=True, axis_index_groups=[low_bit_order()]
    )
    def natural(slot):
        split = slot.reshape(2, sections // 2, MATRICES, -1, D)
        return jnp.transpose(split, (2, 1, 0, 3, 4)).reshape(MATRICES, D, D)

    if attention.shape[1] % 16 == 0:
        self_weights, cross_weights = (0, weights), (3, weights)
    else:
        self_weights, cross_weights = (None, natural(weights[0])), (None, natural(weights[3]))

    bucket_square = offset_square(pick(buckets, half, 0), length)
    bucket_range = jnp.arange(position_bias.shape[1])
    onehot = (bucket_square[:, :, None] == bucket_range).astype(jnp.bfloat16)
    bias_term = position_table(onehot, pick(position_bias, half, 0))
    allowed = is_encoder | (jnp.arange(length)[:, None] >= jnp.arange(length)[None, :])

    rows_in = to_full(lookup_rows(own_ids, shard_low))
    gain_self = gain_rows[jnp.where(is_encoder, 0, 3)]
    gain_feed = gain_rows[jnp.where(is_encoder, 1, 5)]
    bias_term = jnp.where(allowed, bias_term, NEGATIVE)
    resid, kept_self = attention_forward(rows_in, gain_self, self_weights, None, bias_term)

    def encoder_rest():
        return feed_forward(resid, gain_feed, gain_rows[2], weights, 1.0)

    first, second = section_bit(0), section_bit(1)
    root_rows = jnp.stack([left_roots, right_inverse_roots])
    own_roots = lax.dynamic_slice_in_dim(root_rows, half * MATRICES, MATRICES, 1)
    root_rows = jnp.stack([own_roots, root_rows[:, 8:12]]).reshape(4, 2, 2, -1, D)
    root_part = swap_bit(pick(root_rows, 1 - first, 1), 0)
    root_rows, resid, root_part = lax.optimization_barrier((root_rows, resid, root_part))
    root_rows = ordered(pick(root_rows, first, 1), root_part, first, 2)
    root_part = swap_bit(pick(root_rows, 1 - second, 1), 1)

    after_enc, encoded, before_enc = lax.cond(
        is_encoder, encoder_rest, lambda: jax.tree.map(jnp.zeros_like, encoder_rest())
    )
    encoded, root_part = lax.optimization_barrier((encoded, root_part))
    arrived = to_decoder(encoded)
    root_rows = ordered(pick(root_rows, second, 1), root_part, second, 1)
    root_rows = root_rows.reshape(2, 2, -1, D)
    root_lefts, root_rights = root_rows[:, 0], root_rows[:, 1]
    root_steps = list(range(bits - 1, 1, -1))

    def root_step(stage):
        return swap_bit(root_rights, root_steps[stage])

    def grown(stage, part):
        mine = section_bit(root_steps[stage])
        return ordered(root_rights, part, mine, 1 + stage)

    for stage in range(len(root_steps) - 2):
        root_rights = grown(stage, root_step(stage))
    root_part = root_step(len(root_steps) - 2)

    def decoder_rest(after, before):
        rows_feed, kept_cross = attention_forward(
            resid, gain_rows[4], cross_weights, arrived, None
        )
        after, final, before = feed_forward(
            rows_feed, gain_feed, gain_rows[6], weights, D ** (-0.5)
        )
        return (final, after, before, rows_feed, kept_cross)

    def decoder_skip(after, before):
        empty = jnp.zeros(resid.shape, jnp.bfloat16)
        return (empty, after, before, resid, [empty] * 5)

    final_low, after_feed, before_feed, rows_feed, kept_cross = lax.cond(
        is_decoder, decoder_rest, decoder_skip, after_enc, before_enc
    )

    final_low, root_part = lax.optimization_barrier((final_low, root_part))
    root_rights = grown(len(root_steps) - 2, root_part)

    final_split = final_low.reshape(MICRO, length, D)
    handed = to_encoder(final_split[0])
    own_rows = jnp.where(is_encoder, handed, final_split[1])
    head_low = own_rows * live_rows[:, None].astype(jnp.bfloat16)
    all_rows = lax.all_gather(head_low, "section", axis=0, tiled=True)
    logits = jnp.einsum("nd,vd->nv", all_rows, shard_low, preferred_element_type=jnp.float32)
    goal_hit = (goal_ids - section_index * vocab_rows)[:, None] == jnp.arange(vocab_rows)[None, :]
    row_peak = jnp.max(logits, -1)
    row_total = jnp.sum(jnp.exp(logits - row_peak[:, None]), -1)
    goal_logit = jnp.sum(jnp.where(goal_hit, logits, 0.0), -1)
    for bit in range(bits):
        other_peak, other_total = swap_bit(jnp.stack([row_peak, row_total]), bit)
        top_peak = jnp.maximum(row_peak, other_peak)
        row_total = row_total * jnp.exp(row_peak - top_peak)
        row_total = row_total + other_total * jnp.exp(other_peak - top_peak)
        row_peak = top_peak
    log_total = row_peak + jnp.log(row_total)
    grad_logits = to_low(jnp.exp(logits - log_total[:, None]) - goal_hit.astype(jnp.float32))
    grad_all = forward_mul(grad_logits, shard_low)
    def head_table_task():
        yield (None, 14, None, None)
        product = lambda grads: mul_left(grads, all_rows)
        return (yield ("core", 10, product, grad_logits))

    chain = halved(grad_all, range(bits - 1, -1, -1), range(bits))
    grad_head, head_table = interleave([chain, head_table_task()], log_total)
    grad_head = to_full(grad_head)
    grad_head = to_low(grad_head * live_rows[:, None])
    own_live = lax.dynamic_slice_in_dim(log_total, section_index * length, length, 0)
    loss_part = jnp.sum(live_rows * own_live) - jnp.sum(live_all.reshape(-1) * goal_logit)
    count_part = jnp.sum(live_rows)
    grad_final = jnp.stack([to_decoder(grad_head), grad_head]).reshape(MICRO * length, D)

    def decoder_back():
        grad_rows, *feed_grads, gains = feed_backward(
            grad_final,
            after_feed,
            gain_rows[6],
            rows_feed,
            gain_feed,
            before_feed,
            weights,
            D ** (-0.5),
        )
        grad_rows, *cross_grads, gain_cross, grad_source = attention_backward(
            grad_rows, resid, gain_rows[4], cross_weights, kept_cross, arrived, None
        )
        gains = jnp.concatenate([gain_cross, gains])
        return (grad_source, grad_rows, feed_grads, cross_grads, gains)

    root_rights, grad_final = lax.optimization_barrier((root_rights, grad_final))
    root_part = root_step(len(root_steps) - 1)
    grad_source, grad_dec, feed_dec, cross_grads, gains_dec = lax.cond(
        is_decoder, decoder_back, lambda: jax.tree.map(jnp.zeros_like, decoder_back())
    )
    back_source = to_encoder(grad_source)

    back_source, feed_dec, cross_grads, root_part = lax.optimization_barrier(
        (back_source, feed_dec, cross_grads, root_part)
    )
    root_rights = grown(len(root_steps) - 1, root_part).reshape(2, D, D)

    late = to_low(to_full(cross_grads[1]) + to_full(swap_bit(cross_grads[0], 0, (1,))))
    late_split = late.reshape(2, -1, D)
    late_part, back_source, grad_dec = lax.optimization_barrier(
        (pick(late_split, 1 - second, 0), back_source, grad_dec)
    )
    late_arrived = swap_bit(late_part, 1, (1,))

    def self_back(grad_rows):
        return attention_backward(
            grad_rows, rows_in, gain_self, self_weights, kept_self, None, bias_term
        )

    def encoder_feed():
        grad_rows, *feed_grads, gains = feed_backward(
            back_source,
            after_feed,
            gain_rows[2],
            resid,
            gain_feed,
            before_feed,
            weights,
            1.0,
        )
        empty = jnp.zeros((MATRICES // 2 * D, D), jnp.bfloat16)
        score = jnp.zeros(bias_term.shape, jnp.float32)
        return (grad_rows, gains, score, [empty, empty], feed_grads)

    def decoder_self():
        embed_low, *self_grads, gain_grad, score_grad = self_back(grad_dec)
        gains = jnp.concatenate([gain_grad, gain_grad])
        return (to_full(embed_low), gains, score_grad, self_grads, feed_dec)

    grad_rows, gains_middle, score_middle, self_middle, feed_grads = lax.cond(
        is_encoder, encoder_feed, decoder_self
    )
    grad_rows, self_middle, feed_grads, late_arrived = lax.optimization_barrier(
        (grad_rows, self_middle, feed_grads, late_arrived)
    )
    late = to_low(to_full(pick(late_split, second, 0)) + to_full(late_arrived))
    third = section_bit(2)
    late_split = late.reshape(2 ** (bits - 3), 2, -1, D)
    late_part, grad_rows = lax.optimization_barrier(
        (pick(late_split, 1 - third, 1).reshape(-1, D), grad_rows)
    )
    late_arrived = swap_bit(late_part, 2, (1,))

    feed_arrived = swap_bit(feed_grads[0], 0)

    def encoder_self():
        embed_low, *self_grads, gain_grad, score_grad = self_back(grad_rows)
        gains = jnp.concatenate([gain_grad, gains_middle, jnp.zeros((4, D), jnp.float32)])
        return (embed_low, gains, score_grad, self_grads)

    def decoder_skip_self():
        gains = jnp.concatenate([jnp.zeros((3, D), jnp.float32), gains_middle[:1], gains_dec])
        return (to_low(grad_rows), gains, score_middle, self_middle)

    embed_low, gain_part, score_grad, self_grads = lax.cond(
        is_encoder, encoder_self, decoder_skip_self
    )
    embed_low, self_grads, late_arrived, feed_arrived = lax.optimization_barrier(
        (embed_low, self_grads, late_arrived, feed_arrived)
    )
    feed_half = to_low(to_full(feed_grads[1]) + to_full(feed_arrived))
    late = pick(late_split, third, 1).reshape(-1, D)
    late = to_low(to_full(late) + to_full(late_arrived))

    found = {}
    own_local = (own_ids.reshape(-1) - section_index * vocab_rows)[None, :]

    def squares(values):
        return jnp.sum(to_full(values) * to_full(values))

    def rows_task():
        every_rows = yield ("gather", 80, lambda rows: lax.all_gather(rows, "section"), embed_low)
        found["rows"] = every_rows.reshape(-1, D)

    def feed_task():
        yield (None, 10, None, None)
        layout = ["matrix"] + list(range(bits - 1, 0, -1))
        own = yield from halved(feed_half.reshape(-1, D), layout, range(1, 3))
        found["feed_two"] = own
        own = yield from halved(own, layout[:-2], range(3, bits))
        own = own.reshape(2, -1, D)
        found["feed_square"] = squares(own)
        found["feed"] = own
        return own, (yield ("dp", -15, swap_half, own))

    block_rows = -(-vocab_rows // 16) * 8
    shared = 2 * block_rows - vocab_rows
    starts = [0, vocab_rows - block_rows]

    def table_task():
        yield from until(found, ["rows", "feed_two"])
        own_start, other_start = jnp.where(is_encoder, jnp.array(starts), jnp.array(starts[::-1]))

        def product(start):
            def rows_of(rows):
                hit = own_local == start + jnp.arange(block_rows)[:, None]
                head = lax.dynamic_slice_in_dim(head_table, start, block_rows, 0)
                return to_low(mul(hit.astype(jnp.bfloat16), rows) + head)

            return rows_of

        sent = yield ("core", 10, product(other_start), found["rows"])
        found["table_sent"] = sent
        arrived = yield ("dp", -36, swap_half, sent)
        own = yield ("core", 10, product(own_start), found["rows"])
        yield (None, 30, None, None)
        own = to_low(to_full(own) + to_full(arrived))
        counted = is_encoder | (jnp.arange(block_rows) >= shared)
        found["table_square"] = squares(jnp.where(counted[:, None], own, jnp.zeros_like(own)))
        other = yield ("dp", -36, swap_half, own)
        return jnp.concatenate(
            [jnp.where(is_encoder, own, other), jnp.where(is_encoder, other, own)[shared:]]
        )

    def cross_task():
        layout = [bit for bit in slot_layout()[1:] if bit > 2]
        block = yield from halved(late, layout, range(3, bits), (1,))
        found["cross_square"] = squares(block)
        full = yield from doubled(block, (1,))
        terms = shampoo_terms(block, full, root_lefts[1], root_rights[1])
        found["cross_direction"] = squares(terms[1])
        terms = yield from to_rows(terms, (1,))
        other = yield ("dp", -30, to_encoder, terms)
        return terms, other

    def self_task():
        block = yield from halved(tuple(self_grads), slot_layout(), range(1, bits))
        found["self_square"] = squares(block)
        yield from until(found, ["table_sent"])
        full = yield from doubled(tied(block, found["table_sent"]))
        terms = shampoo_terms(block, full, root_lefts[0], root_rights[0])
        found["self_direction"] = squares(terms[1])
        terms = yield from to_rows(terms)
        other = yield ("dp", -30, swap_half, terms)
        return terms, other

    def norm_task():
        yield from until(found, ["self_square", "cross_square", "feed_square", "table_square"])
        bias_grad = jnp.einsum(
            "hqk,qkb->bh", score_grad, onehot.astype(jnp.float32), precision=HIGH
        ).reshape(1, -1)
        bias_rows = [jnp.where(half == layer, bias_grad, 0.0) for layer in range(2)]
        square_sum = found["self_square"] + is_decoder.astype(jnp.float32) * found["cross_square"]
        square_sum = square_sum + found["feed_square"] + found["table_square"]
        sums = jnp.stack([loss_part, count_part, square_sum])
        sums = jnp.pad(sums, (0, D - sums.shape[0])).reshape(1, D)
        bias_rows = jnp.concatenate(bias_rows, 1).reshape(-1, D)
        sums = yield from summed(jnp.concatenate([gain_part, bias_rows, sums]))
        return sums, (yield ("dp", -5, swap_half, sums))

    def direction_task():
        yield from until(found, ["self_direction", "cross_direction"])
        matrix = 2 * section_bit(0) + section_bit(1)
        names = jnp.arange(3 * MATRICES)
        own_matrix, cross_matrix = half * MATRICES + matrix, 2 * MATRICES + matrix
        sums = jnp.where(names == own_matrix, found["self_direction"], 0.0)
        sums = sums + jnp.where(
            names == cross_matrix, is_decoder * found["cross_direction"], 0.0
        )
        sums = yield from summed(jnp.pad(sums, (0, 128 - sums.shape[0])).reshape(1, 128))
        return sums, (yield ("dp", -5, swap_half, sums))

    tasks = [rows_task(), self_task(), cross_task(), table_task(), feed_task()]
    tasks += [norm_task(), direction_task()]
    results = interleave(tasks, embed_low)
    self_terms, cross_terms, table_grad, feed_both = results[1:5]
    norm_sums, directions = results[5:]
    norm_sums = norm_sums[0] + norm_sums[1]
    small, sums = norm_sums[:-1], norm_sums[-1]
    directions = (directions[0] + directions[1])[0, : 3 * MATRICES]
    gain_full = small[: gain_rows.shape[0]]
    bias_full = small[gain_rows.shape[0] :].reshape(position_bias.shape)
    small_square = squares(gain_full) + squares(bias_full)

    grad_norm = jnp.sqrt(sums[2] + small_square)
    clip_factor = CLIP / jnp.maximum(grad_norm, CLIP)
    table_out = adamw(table, table_first, table_second, table_grad * clip_factor, RATE_TABLE)
    feed_both = to_full(ordered(*feed_both, half, 1))
    inner_part = jnp.swapaxes(feed_both[0], 1, 2)
    outer_part = feed_both[1]
    inner_out = adamw(inner_weight, inner_first, inner_second, inner_part * clip_factor, RATE_INNER)
    outer_out = adamw(outer_weight, outer_first, outer_second, outer_part * clip_factor, RATE_INNER)
    table_out, self_terms, cross_terms = lax.optimization_barrier(
        (table_out, self_terms, cross_terms)
    )
    terms = jnp.concatenate(
        [
            ordered(*self_terms, half, 1).reshape(4, 2 * MATRICES, -1, D),
            jnp.where(is_encoder, cross_terms[1], cross_terms[0]),
        ],
        1,
    )
    attention_grad, direction, left_term, right_term = to_full(terms)
    gain_out = adamw(gain_rows, gain_first, gain_second, gain_full * clip_factor, RATE_GAIN)
    bias_out = adamw(position_bias, bias_first, bias_second, bias_full * clip_factor, RATE_BIAS)
    clip_square = clip_factor * clip_factor
    left_new = BETA_STATS * left_stats + (1 - BETA_STATS) * clip_square * left_term
    right_new = BETA_STATS * right_stats + (1 - BETA_STATS) * clip_square * right_term
    spread = jnp.sqrt(directions / (D * D) + EPS)[:, None, None]
    attention_new = attention - RATE_ATTENTION * (direction / spread + DECAY * attention)
    return (
        sums[0],
        sums[1],
        grad_norm,
        *table_out,
        *inner_out,
        *outer_out,
        *gain_out,
        *bias_out,
        attention_grad * clip_factor,
        left_new,
        right_new,
        attention_new,
    )


def solution(mesh):
    in_specs = (
        P("dp", "section", None, None),
        P("dp", "section", None),
        P("dp", "section"),
        P(),
        P("section", None),
        P("section", None),
        P("section", None),
        P(None, None, "section"),
        P(None, None, "section"),
        P(None, None, "section"),
        P(None, "section", None),
        P(None, "section", None),
        P(None, "section", None),
        P(),
        P(),
        P(),
        P(),
        P(),
        P(),
        P(None, "section", None),
        P(None, "section", None),
        P(None, "section", None),
        P(None, "section", None),
        P(None, "section", None),
    )
    out_specs = (
        P(),
        P(),
        P(),
        P("section", None),
        P("section", None),
        P("section", None),
        P(None, None, "section"),
        P(None, None, "section"),
        P(None, None, "section"),
        P(None, "section", None),
        P(None, "section", None),
        P(None, "section", None),
        P(),
        P(),
        P(),
        P(),
        P(),
        P(),
        P(None, "section", None),
        P(None, "section", None),
        P(None, "section", None),
        P(None, "section", None),
    )
    return jax.shard_map(local, mesh=mesh, in_specs=in_specs, out_specs=out_specs, check_vma=False)
```
